512 devices in a mesh: lam: 32 (over y, x), dom: 16 (over z, core).
Axes of the slice: x: 4, y: 8, z: 8, core: 2. Of those that a mesh axis runs over, the one named last changes fastest.
Arguments:
- cells: int32 [32, 3, 16384], P('lam', None, 'dom'), may hold values from 0 to 127, as said below
- offsets: float32 [32, 3, 16384], P('lam', None, 'dom'), may hold values from 0 to 1
- velocities: float32 [32, 3, 16384], P('lam', None, 'dom'), may hold values from -6 to 6
- charges: float32 [16384], P('dom'), may hold values from -2.5 to 2.5, as said below
- coupling: float32 [16384], P('dom'), may hold values from 0 to 1
- inverse_mass: float32 [16384], P('dom'), may hold values from 0.1 to 1
- lambdas: float32 [32], P('lam'), may hold values from 0 to 0.9
- tile_lists: int32 [32, 128, 6], P('lam', 'dom'), may hold values from 0 to 15, as said below
- halo_lists: int32 [32, 32, 512], P('lam', 'dom'), may hold values from 0 to 1023, as said below
- accept_flags: int32 [2, 32], P(None, 'lam'), may hold values 0 or 1
Outputs:
- new_cells: int32 [32, 3, 16384], P('lam', None, 'dom')
- new_offsets: float32 [32, 3, 16384], P('lam', None, 'dom')
- new_velocities: float32 [32, 3, 16384], P('lam', None, 'dom')
The draws below stay inside these ranges and needn't reach their ends.
Inputs may be any that keep to these rules, and one draw needn't show every extreme that they name: `cells`: for atom a of a window, with d = a // 1024 and c = (a % 1024) // 128: its first cell index lies in [d * 8, (d + 1) * 8) and its second in [c * 16, (c + 1) * 16). The third cell indices of all atoms of one window lie among 8 consecutive values, counted modulo 128 (a membrane slab). `charges`: every charge has a magnitude between 1.5 and 2.5, of either sign. `tile_lists`: row d * 8 + c of a window lists, in order: c; three different clusters among c - 2, c - 1, c + 1, c + 2 modulo 8; 8 + c // 2; 12 + c // 2. `halo_lists`: rows 2d and 2d + 1 hold indices within domain d. Entries c * 64 to (c + 1) * 64 - 1 of row 2d are the atoms of cluster c with the lowest first cell index, those of row 2d + 1 the others (ties by atom number); each of the domain's atoms stands once in the two rows.
All inputs are finite; a program needn't handle non-finite values. No bound on the sum of `accept_flags` on one device may be relied on, other than what follows from the above.
Results may differ from the reference program's by a relative error of at most 0.0003.
Values sent between devices are 32-bit elements; how exact they have to be, the bound alone decides.
No kernel may reach another device: no remote copies, remote signals or barrier semaphores. Data moves between devices by JAX's collectives and lax.ppermute only.
A program may use at most 64 MiB of HBM per device.

```python
import math
import jax
import jax.numpy as jnp
from jax import lax

K = 128
A_DEV = 1024
CLUSTER = 128
NJ = 6
STEPS = 2
ROUNDS = 2
WINDOWS = 32
ATOMS = 16384
CLUSTERS = 8
PLANES = 8
HALO = 512
N_DOM = 16


def cell_layout(key):
    atom_index = jnp.arange(ATOMS, dtype=jnp.int32)
    domain = atom_index // A_DEV
    column = atom_index % A_DEV // CLUSTER
    band_width = K // CLUSTERS
    first = domain[None, :] * PLANES + jax.random.randint(jax.random.fold_in(key, 11), (WINDOWS, ATOMS), 0, PLANES)
    second = column[None, :] * band_width + jax.random.randint(jax.random.fold_in(key, 12), (WINDOWS, ATOMS), 0, band_width)
    slab_start = jax.random.randint(jax.random.fold_in(key, 14), (WINDOWS, 1), 0, K)
    third = (slab_start + jax.random.randint(jax.random.fold_in(key, 13), (WINDOWS, ATOMS), 0, 8)) % K
    return jnp.stack([first, second, third], axis=1).astype(jnp.int32)


def draw_cells(key, part):
    layout = cell_layout(key)
    return layout


def draw_halo_lists(key, part):
    layout = cell_layout(key)
    first = layout[:, 0, :].reshape(WINDOWS, N_DOM, CLUSTERS, CLUSTER)
    lane = jnp.arange(CLUSTER, dtype=jnp.int32)
    score = first * CLUSTER + lane
    sorted_lanes = jnp.argsort(score, axis=-1, stable=True).astype(jnp.int32)
    local_index = jnp.arange(CLUSTERS, dtype=jnp.int32)[:, None] * CLUSTER + sorted_lanes
    half_size = CLUSTER // 2
    lower_rows = local_index[..., :half_size].reshape(WINDOWS, N_DOM, HALO)
    upper_rows = local_index[..., half_size:].reshape(WINDOWS, N_DOM, HALO)
    return jnp.stack([lower_rows, upper_rows], axis=2).reshape(WINDOWS, 2 * N_DOM, HALO).astype(jnp.int32)


def draw_tile_lists(key, part):
    key = jax.random.fold_in(key, 3)
    row_count = WINDOWS * N_DOM * CLUSTERS
    score = jax.random.randint(key, (row_count, 4), 0, 1 << 20) * 4 + jnp.arange(4, dtype=jnp.int32)[None, :]
    ranked = jnp.argsort(score, axis=-1, stable=True).astype(jnp.int32)
    steps_table = jnp.array([1, 2, CLUSTERS - 1, CLUSTERS - 2], dtype=jnp.int32)
    cluster = jnp.arange(row_count, dtype=jnp.int32) % CLUSTERS
    picked = (cluster[:, None] + steps_table[ranked[:, :3]]) % CLUSTERS
    lower_halo = CLUSTERS + cluster // 2
    upper_halo = CLUSTERS + CLUSTERS // 2 + cluster // 2
    table_rows = jnp.concatenate([cluster[:, None], picked, lower_halo[:, None], upper_halo[:, None]], axis=1)
    return table_rows.reshape(WINDOWS, N_DOM * CLUSTERS, NJ).astype(jnp.int32)


def draw_charges(key, part):
    key = jax.random.fold_in(key, 4)
    magnitude = jax.random.uniform(jax.random.fold_in(key, 21), (ATOMS,), jnp.float32, 1.5, 2.5)
    coin = jax.random.bernoulli(jax.random.fold_in(key, 22), 0.5, (ATOMS,)).astype(jnp.float32)
    return (magnitude * (2.0 * coin - 1.0)).astype(jnp.float32)


def with_ends(values, key, least, top_value):
    longest = values.shape.index(max(values.shape))
    spots = []
    for shift in (0, 1):
        where = [jax.random.randint(jax.random.fold_in(key, axis), (), 0, length) for axis, length in enumerate(values.shape)]
        where[longest] = (where[longest] + shift) % values.shape[longest]
        spots.append(tuple(where))
    return values.at[spots[0]].set(least).at[spots[1]].set(top_value)


def block_levels(own_key, dims, cuts, least, top_value):
    level, own = 1.0, jax.random.fold_in(own_key, 6)
    for dim, parts in cuts:
        heights = jnp.exp(jax.random.uniform(jax.random.fold_in(own, dim), (parts,), jnp.float32, least / len(cuts), top_value / len(cuts)))
        level = level * jnp.repeat(heights, dims[dim] // parts).reshape([-1 if axis == dim else 1 for axis in range(len(dims))])
    return level


def centred(stream_key, extent, spread, limit, split=(), kind=jnp.bfloat16):
    level = block_levels(stream_key, extent, split, -0.22, 0.18) if split else 1.0
    values = jax.random.normal(stream_key, extent, jnp.float32) * spread * level
    return jnp.minimum(jnp.maximum(values, -limit), limit).astype(kind)


def setup_inputs(seed: int = 0) -> dict:
    key_of = jax.random.split(jax.random.key(seed), 11)
    return {
        "cells": draw_cells(jax.random.fold_in(key_of[10], 71), 0),
        "offsets": jnp.clip(1.0 * jax.random.uniform(key_of[1], (WINDOWS, 3, ATOMS), jnp.float32) ** block_levels(key_of[1], (WINDOWS, 3, ATOMS), ((0, 32), (2, 16)), -0.2, 0.2), 0.0, 1.0),
        "velocities": centred(key_of[2], (WINDOWS, 3, ATOMS), 1.0, 6.0, ((0, 32), (2, 16)), jnp.float32),
        "charges": draw_charges(jax.random.fold_in(key_of[10], 71), 0),
        "coupling": jnp.clip(1.0 * jax.random.uniform(key_of[4], (ATOMS,), jnp.float32) ** block_levels(key_of[4], (ATOMS,), ((0, 16),), -0.2, 0.2), 0.0, 1.0),
        "inverse_mass": jnp.clip(jnp.exp(math.log(1.0) - 2.3025851 * jax.random.uniform(key_of[5], (ATOMS,), jnp.float32) ** block_levels(key_of[5], (ATOMS,), ((0, 16),), -0.2, 0.2)), 0.1, 1.0),
        "lambdas": jnp.clip(0.9 * jax.random.uniform(key_of[6], (WINDOWS,), jnp.float32) ** block_levels(key_of[6], (WINDOWS,), ((0, 32),), -0.2, 0.2), 0.0, 0.9),
        "tile_lists": draw_tile_lists(jax.random.fold_in(key_of[10], 71), 0),
        "halo_lists": draw_halo_lists(jax.random.fold_in(key_of[10], 71), 0),
        "accept_flags": with_ends((jax.random.randint(key_of[9], (ROUNDS, WINDOWS), 0, 2) < 1).astype(jnp.int32), jax.random.fold_in(key_of[9], 1), 0, 1),
    }


EWALD_BETA = 0.5
COULOMB = 20.0
LJ_DEPTH = 1.0
LJ_SIGMA_SQ = 0.49
SOFT_SCALE = 0.5
SOFT_FLOOR = 0.5
STEP_DT = 0.25
group_size = 4

def spline_set(fraction):
    remainder = 1.0 - fraction
    square = fraction * fraction
    cube_value = square * fraction
    weights = jnp.stack([remainder * remainder * remainder / 6.0, (3.0 * cube_value - 6.0 * square + 4.0) / 6.0, (-3.0 * cube_value + 3.0 * square + 3.0 * fraction + 1.0) / 6.0, cube_value / 6.0])
    slopes = jnp.stack([-0.5 * remainder * remainder, 1.5 * square - 2.0 * fraction, -1.5 * square + fraction + 0.5, 0.5 * square])
    return (weights, slopes)

def influence(frequency_x, frequency_y, frequency_z):
    total_sq = 0.0
    modulus = 1.0
    for frequency in (frequency_x, frequency_y, frequency_z):
        signed = jnp.where(frequency * 2 < K, frequency, frequency - K).astype(jnp.float32) / K
        total_sq = total_sq + signed * signed
        angle_value = 2.0 * math.pi / K * frequency.astype(jnp.float32)
        modulus = modulus * (3.0 / (2.0 + jnp.cos(angle_value))) ** 2
    safe_sq = jnp.where(total_sq > 0, total_sq, 1.0)
    kernel_value = COULOMB * jnp.exp(-math.pi ** 2 * safe_sq / EWALD_BETA ** 2) / (math.pi * float(K) ** 3 * safe_sq) * modulus
    return jnp.where(total_sq > 0, kernel_value, 0.0)

def pair_energy(left_position, left_extra, right_block, lam_value):
    offset_vec = left_position[:, :, :, None] - right_block[:, :3, None, :]
    offset_vec = offset_vec - K * jnp.floor(offset_vec / K + 0.5)
    dist_sq = lax.optimization_barrier(jnp.sum(offset_vec * offset_vec, axis=1))
    softened = dist_sq + SOFT_FLOOR + SOFT_SCALE * lam_value
    radius = jnp.sqrt(softened)
    charge_pair = left_extra[:, 0, :, None] * right_block[:, 3, None, :]
    weight_pair = left_extra[:, 1, :, None] * right_block[:, 4, None, :]
    power_six = (LJ_SIGMA_SQ / softened) ** 3
    energy = COULOMB * charge_pair * jax.scipy.special.erfc(EWALD_BETA * radius) / radius + 4.0 * LJ_DEPTH * weight_pair * (power_six * power_six - power_six)
    return jnp.sum(energy)

def cluster_forces(own_block, pool_block, tile_rows, lam_value):
    cluster_width = own_block.shape[1] // (own_block.shape[1] // CLUSTER)
    clusters = own_block.shape[1] // cluster_width
    slot_count = tile_rows.shape[1]
    own_sets = own_block.reshape(5, clusters, cluster_width).transpose(1, 0, 2).reshape(clusters // group_size, group_size, 5, cluster_width)
    pool_sets = pool_block.reshape(5, -1, cluster_width).transpose(1, 0, 2)
    tile_groups = tile_rows.reshape(clusters // group_size, group_size * slot_count)

    def one_group(unused, group_items):
        own_group, tile_ids = group_items
        left_block = jnp.repeat(own_group, slot_count, axis=0)
        right_block = pool_sets[tile_ids]
        gradient = jax.grad(pair_energy)(left_block[:, :3], left_block[:, 3:], right_block, lam_value)
        return (unused, -lax.optimization_barrier(jnp.sum(gradient.reshape(group_size, slot_count, 3, cluster_width), axis=1)))
    unused, forces = lax.scan(one_group, jnp.float32(0.0), (own_sets, tile_groups))
    return forces.reshape(clusters, 3, cluster_width).transpose(1, 0, 2).reshape(3, clusters * cluster_width)

def short_reference(position, charge_eff, weight, window_tiles, window_halo, lam_value):
    full_block = jnp.concatenate([position, charge_eff[None, :], weight[None, :]], axis=0)

    def per_domain(domain):
        lower_dom = (domain + N_DOM - 1) % N_DOM
        upper_dom = (domain + 1) % N_DOM
        own_block = lax.dynamic_slice_in_dim(full_block, domain * A_DEV, A_DEV, 1)
        below = jnp.take(full_block, lower_dom * A_DEV + window_halo[2 * lower_dom + 1], axis=1)
        above = jnp.take(full_block, upper_dom * A_DEV + window_halo[2 * upper_dom], axis=1)
        pool_block = jnp.concatenate([own_block, below, above], axis=1)
        tile_rows = lax.dynamic_slice_in_dim(window_tiles, domain * CLUSTERS, CLUSTERS, 0)
        return cluster_forces(own_block, pool_block, tile_rows, lam_value)
    forces = lax.map(per_domain, jnp.arange(N_DOM, dtype=jnp.int32))
    return forces.transpose(1, 0, 2).reshape(3, ATOMS)

def mesh_reference(window_cells, window_offsets, charge_eff):
    weight_list = []
    slope_list = []
    point_list = []
    for dim_index in range(3):
        weights, slopes = spline_set(window_offsets[dim_index])
        weight_list.append(weights)
        slope_list.append(slopes)
        point_list.append((window_cells[dim_index][None, :] + jnp.arange(4, dtype=jnp.int32)[:, None]) % K)
    point_x = point_list[0][:, None, None, :]
    point_y = point_list[1][None, :, None, :]
    point_z = point_list[2][None, None, :, :]
    weight_x = weight_list[0][:, None, None, :]
    weight_y = weight_list[1][None, :, None, :]
    weight_z = weight_list[2][None, None, :, :]
    grid = jnp.zeros((K, K, K), jnp.float32).at[point_x, point_y, point_z].add(charge_eff * weight_x * weight_y * weight_z)
    frequency = jnp.arange(K, dtype=jnp.int32)
    kernel_gain = influence(frequency[:, None, None], frequency[None, :, None], frequency[None, None, :])
    potential = jnp.real(jnp.fft.ifftn(kernel_gain * jnp.fft.fftn(grid))) * K ** 3
    values = potential[point_x, point_y, point_z]
    slope_x = slope_list[0][:, None, None, :]
    slope_y = slope_list[1][None, :, None, :]
    slope_z = slope_list[2][None, None, :, :]
    force_x = -charge_eff * lax.optimization_barrier(jnp.sum(slope_x * weight_y * weight_z * values, axis=(0, 1, 2)))
    force_y = -charge_eff * lax.optimization_barrier(jnp.sum(weight_x * slope_y * weight_z * values, axis=(0, 1, 2)))
    force_z = -charge_eff * lax.optimization_barrier(jnp.sum(weight_x * weight_y * slope_z * values, axis=(0, 1, 2)))
    return jnp.stack([force_x, force_y, force_z])

def ladder_order(flag_table, windows):
    window = jnp.arange(windows, dtype=jnp.int32)
    content = window
    for round_index in range(flag_table.shape[0]):
        active = (window % 2 == round_index % 2) & (window + 1 < windows) & (flag_table[round_index] == 1)
        lower_active = jnp.concatenate([jnp.zeros((1,), jnp.bool_), active[:-1]])
        content = jnp.where(active, jnp.roll(content, -1), jnp.where(lower_active, jnp.roll(content, 1), content))
    return content

def reference(cells, offsets, velocities, charges, coupling, inverse_mass, lambdas, tile_lists, halo_lists, accept_flags):

    def one_window(window_items):
        window_cells, window_offsets, window_velocities, lam_value, window_tiles, window_halo = window_items
        weight = 1.0 - lam_value * coupling
        charge_eff = charges * weight
        long_range = mesh_reference(window_cells, window_offsets, charge_eff)

        def total_force(offset_value):
            position = window_cells.astype(jnp.float32) + offset_value
            return short_reference(position, charge_eff, weight, window_tiles, window_halo, lam_value) + long_range
        offset_now = window_offsets
        velocity_now = window_velocities
        force_now = total_force(offset_now)
        for step_index in range(STEPS):
            velocity_now = velocity_now + 0.5 * STEP_DT * force_now * inverse_mass
            offset_now = offset_now + STEP_DT * velocity_now
            force_now = total_force(offset_now)
            velocity_now = velocity_now + 0.5 * STEP_DT * force_now * inverse_mass
        return (offset_now, velocity_now)
    moved_offsets, moved_velocities = lax.map(one_window, (cells, offsets, velocities, lambdas, tile_lists, halo_lists))
    content = ladder_order(accept_flags, WINDOWS)
    return (cells[content], moved_offsets[content], moved_velocities[content])
```

```python
import functools
import math

import jax
import jax.numpy as jnp
import ml_dtypes
import numpy as np
from jax import lax
from jax.experimental import pallas as pl
from jax.experimental.pallas import tpu as pltpu
from jax.sharding import PartitionSpec as P

K = 128
CLUSTER = 128
N_DOM = 16
A_DEV = 1024
CLUSTERS = 8
HALO = 512
MODES = 32
SLAB = 24
ROWS = N_DOM * SLAB

EWALD_BETA = 0.5
COULOMB = 20.0
LJ_DEPTH = 1.0
LJ_SIGMA_SQ = 0.49
SOFT_SCALE = 0.5
SOFT_FLOOR = 0.5
STEP_DT = 0.25

F32 = jnp.float32
BF16 = jnp.bfloat16
HIGHEST = lax.Precision.HIGHEST

TURN = 2.0**32
SPAN_SQ = 2.0**-50
SPAN = 2.0**-25

SCREEN = (
    -0.0818439527,
    0.648023047,
    -2.23331568,
    4.38709699,
    -5.37737017,
    4.16223694,
    -1.81397109,
    0.0540053844,
    0.5630337,
    -5.2346482e-05,
    0.282096019,
)


def real_basis(count):
    half = count // 2
    place = np.arange(count)
    rows = []
    for k in range(half + 1):
        scale = math.sqrt((1.0 if k in (0, half) else 2.0) / count)
        rows.append(scale * np.cos(2.0 * np.pi * (k * place % count) / count))
    for k in range(1, half):
        rows.append(math.sqrt(2.0 / count) * np.sin(2.0 * np.pi * (k * place % count) / count))
    return np.stack(rows)


def halves(table):
    high = table.astype(np.float32).astype(ml_dtypes.bfloat16)
    low = (table - high.astype(np.float64)).astype(np.float32).astype(ml_dtypes.bfloat16)
    return high, low


def basis_table():
    basis = real_basis(K)
    high, low = halves(basis)
    return np.concatenate([high, low, high.T, low.T], axis=0)


def slab_basis():
    basis = real_basis(MODES)
    order = [0, MODES // 2]
    for k in range(1, MODES // 2):
        order += [k, MODES // 2 + k]
    return basis[np.array(order)].astype(np.float32)


def spline_modulus(k):
    return (3.0 / (2.0 + np.cos(2.0 * np.pi * k / K))) ** 2


def slab_weights():
    k = np.arange(K // 2 + 1)
    delta = np.arange(-MODES // 2 + 1, MODES // 2 + 1)
    folded = np.where((k == 0) | (k == K // 2), 1.0, 2.0)
    own = folded * np.exp(-np.pi**2 * (k / K) ** 2 / EWALD_BETA**2) * spline_modulus(k)
    rows = []
    for j in range(MODES // 2 + 1):
        window = np.cos(2 * np.pi * k[:, None] * delta / K) * np.cos(2 * np.pi * j * delta / MODES)
        rows.append(own * window.sum(axis=1))
    return np.stack(rows).astype(np.float32)


def plane_gain():
    k = np.concatenate([np.arange(K // 2 + 1), np.arange(1, K // 2)])
    square = (k / K) ** 2
    factor = np.exp(-np.pi**2 * square / EWALD_BETA**2) * spline_modulus(k)
    return square.astype(np.float32), factor.astype(np.float32)


def split(x):
    high = x.astype(BF16)
    return high, (x - high.astype(F32)).astype(BF16)


def dot3(left, right, dims=(((1,), (0,)), ((), ()))):
    lh, ll = left
    rh, rl = right
    dot = functools.partial(lax.dot_general, dimension_numbers=dims, preferred_element_type=F32)
    return dot(lh, rh) + (dot(lh, rl) + dot(ll, rh))


def spline_set(u):
    v = 1.0 - u
    u2 = u * u
    u3 = u2 * u
    weights = (
        v * v * v / 6.0,
        (3.0 * u3 - 6.0 * u2 + 4.0) / 6.0,
        (-3.0 * u3 + 3.0 * u2 + 3.0 * u + 1.0) / 6.0,
        u3 / 6.0,
    )
    slopes = (-0.5 * v * v, 1.5 * u2 - 2.0 * u, -1.5 * u2 + u + 0.5, 0.5 * u2)
    return weights, slopes


def chosen(distance, rows):
    out = jnp.where(distance == 3, rows[3], 0.0)
    for k in (2, 1, 0):
        out = jnp.where(distance == k, rows[k], out)
    return out


def iota_rows(rows, columns):
    return lax.broadcasted_iota(jnp.int32, (rows, columns), 0)


def fixed_turns(x):
    t = x * (1.0 / K)
    f = t - jnp.floor(t + 0.5)
    return jnp.maximum(f, -0.5) * TURN


def pair_terms(own, other, floor_value):
    ax, ay, az, qa, wa = own
    bx, by, bz, qb, wb = other
    dx = (ax - bx).astype(F32)
    dy = (ay - by).astype(F32)
    dz = (az - bz).astype(F32)
    s = (dx * dx + dy * dy + dz * dz) * SPAN_SQ + floor_value
    w = lax.rsqrt(s)
    u = w * w
    screen = jnp.full_like(w, SCREEN[0])
    for c in SCREEN[1:]:
        screen = screen * w + c
    gauss = jnp.exp2(s * (-(EWALD_BETA**2) * math.log2(math.e)))
    a = LJ_SIGMA_SQ * u
    t = a * a * a
    g = u * ((qa * qb) * (gauss * screen) + (wa * wb) * (t * (t - 0.5)))
    return g * dx, g * dy, g * dz


def own_rows(data_ref, turns, start, rows=8):
    def spread(row):
        return jnp.broadcast_to(row, (rows, CLUSTER))

    columns = pl.ds(start, CLUSTER)
    xyz = [spread(turns[i : i + 1, columns].astype(jnp.int32)) for i in range(3)]
    q = spread(data_ref[3:4, columns] * (2.0 * COULOMB))
    w = spread(data_ref[4:5, columns] * (48.0 * LJ_DEPTH))
    return (*xyz, q, w)


def write_halo(data, lists_ref, low_ref, high_ref):
    lane = lax.broadcasted_iota(jnp.int32, (8, CLUSTER), 1)
    for row, out_ref in ((0, low_ref), (1, high_ref)):
        for k in range(HALO // CLUSTER):
            columns = slice(k * CLUSTER, (k + 1) * CLUSTER)
            index = jnp.broadcast_to(lists_ref[0, row : row + 1, columns] & (CLUSTER - 1), (8, CLUSTER))
            first = data[:, 2 * k * CLUSTER : (2 * k + 1) * CLUSTER]
            second = data[:, (2 * k + 1) * CLUSTER : (2 * k + 2) * CLUSTER]
            out_ref[:, columns] = jnp.where(
                lane < CLUSTER // 2,
                jnp.take_along_axis(first, index, axis=1, mode="promise_in_bounds"),
                jnp.take_along_axis(second, index, axis=1, mode="promise_in_bounds"),
            )


def spread_kernel(
    lam_ref, flag_ref, cells_ref, off_ref, vel_ref, charge_ref, coup_ref, mass_ref, lists_ref, slab_ref,
    out_ref, data_ref, move_ref, low_ref, high_ref, mixed_high, mixed_low,
):
    cells = cells_ref[0]
    off = off_ref[0]
    cells_f = cells.astype(F32)
    weight = 1.0 - lam_ref[0] * coup_ref[...]
    charge = charge_ref[...] * weight

    data_ref[0:3, :] = cells_f + off
    data_ref[3:4, :] = charge
    data_ref[4:5, :] = weight
    data_ref[5:6, :] = mass_ref[...]
    data_ref[6:8, :] = jnp.zeros((2, A_DEV), F32)
    write_halo(data_ref[...], lists_ref, low_ref, high_ref)

    move_ref[0:3, :] = off
    move_ref[3:6, :] = cells_f
    move_ref[6:7, :] = jnp.full((1, A_DEV), flag_ref[0, 0].astype(F32))
    move_ref[7:8, :] = jnp.full((1, A_DEV), flag_ref[1, 0].astype(F32))
    move_ref[8:11, :] = vel_ref[0]
    move_ref[11:16, :] = jnp.zeros((5, A_DEV), F32)

    weights, _ = spline_set(off)
    row = iota_rows(16, A_DEV)
    plane = jnp.where(row < 8, row, 8 + (row & 3))
    x_table = chosen(plane - (cells[0:1] & 7), [m[0:1] for m in weights]) * charge
    z_table = chosen((iota_rows(MODES, A_DEV) - cells[2:3]) & (MODES - 1), [m[2:3] for m in weights])
    z_modes = jnp.dot(slab_ref[...], z_table, precision=HIGHEST, preferred_element_type=F32)
    y_table = chosen((iota_rows(K, A_DEV) - cells[1:2]) & (K - 1), [m[1:2] for m in weights])

    near, far = x_table[0:8], x_table[8:16]
    upper = iota_rows(8, A_DEV) < 4
    for i in range(0, N_DOM, 2):
        pieces = []
        for k in (i, i + 1):
            first = jnp.broadcast_to(z_modes[2 * k : 2 * k + 1], (8, A_DEV))
            second = jnp.broadcast_to(z_modes[2 * k + 1 : 2 * k + 2], (8, A_DEV))
            pieces += [near * first, near * second, far * jnp.where(upper, first, second)]
        high, low = split(jnp.concatenate(pieces, axis=0))
        mixed_high[i * SLAB : (i + 2) * SLAB, :] = high
        mixed_low[i * SLAB : (i + 2) * SLAB, :] = low
    out_ref[...] = dot3((mixed_high[...], mixed_low[...]), split(y_table), (((1,), (1,)), ((), ())))


def mesh_kernel(grid_ref, gain_ref, basis_ref, out_ref, block):
    top = iota_rows(8, K) < 4
    for e in range(N_DOM):
        spill = grid_ref[((e - 1) % N_DOM) * SLAB + 16 : ((e - 1) % N_DOM) * SLAB + 24, :]
        turned = pltpu.roll(spill, 4, 0)
        block[8 * e : 8 * e + 8, :] = grid_ref[e * SLAB : e * SLAB + 8, :] + jnp.where(top, spill, 0.0)
        block[K + 8 * e : K + 8 * e + 8, :] = grid_ref[e * SLAB + 8 : e * SLAB + 16, :] + jnp.where(top, turned, 0.0)
    basis = (basis_ref[0:K, :], basis_ref[K : 2 * K, :])
    turned_basis = (basis_ref[2 * K : 3 * K, :], basis_ref[3 * K : 4 * K, :])
    along_y = dot3(split(block[...]), turned_basis)
    for mode in range(2):
        part = split(along_y[mode * K : (mode + 1) * K])
        scaled = dot3(basis, part) * gain_ref[mode]
        block[mode * K : (mode + 1) * K, :] = dot3(turned_basis, split(scaled))
    block[...] = dot3(split(block[...]), basis)
    for e in range(N_DOM):
        following = 8 * ((e + 1) % N_DOM)
        out_ref[e * SLAB : e * SLAB + 8, :] = block[8 * e : 8 * e + 8, :]
        out_ref[e * SLAB + 8 : e * SLAB + 16, :] = block[K + 8 * e : K + 8 * e + 8, :]
        out_ref[e * SLAB + 16 : e * SLAB + 24, :] = jnp.where(
            top,
            block[following : following + 8, :],
            pltpu.roll(block[K + following : K + following + 8, :], 4, 0),
        )


def write_gain(mode_weights_ref, rows_ref, lanes_ref, gain_ref):
    dom = lax.axis_index("dom")
    square_y, factor_y = lanes_ref[0:1, :], lanes_ref[1:2, :]
    scale = COULOMB / (math.pi * K)
    first = dom
    second = jnp.where(dom == 0, MODES // 2, dom)

    def totals(square):
        one = jnp.zeros_like(square)
        two = jnp.zeros_like(square)
        for k in range(K // 2 + 1):
            whole = square + (k / K) ** 2
            inverse = 1.0 / whole if k else jnp.where(whole > 0.0, 1.0 / jnp.where(whole > 0.0, whole, 1.0), 0.0)
            one = one + inverse * mode_weights_ref[first, k]
            two = two + inverse * mode_weights_ref[second, k]
        return one, two

    def block(start):
        rows = pl.ds(start, 8)
        square = jnp.broadcast_to(rows_ref[rows, 0:1], (8, K)) + square_y
        factor = jnp.broadcast_to(rows_ref[rows, 1:2], (8, K)) * factor_y * scale
        one, two = totals(square)
        return one * factor, two * factor

    def step(b, carry):
        start = pl.multiple_of(b * 8, 8)
        one, two = block(start)
        gain_ref[0, pl.ds(start, 8), :] = one
        gain_ref[1, pl.ds(start, 8), :] = two
        gain_ref[0, pl.ds(start + K // 2, 8), :] = one
        gain_ref[1, pl.ds(start + K // 2, 8), :] = two
        return carry

    lax.fori_loop(0, 8, step, 0)
    one, two = block(K // 2)
    gain_ref[0, K // 2 : K // 2 + 1, :] = one[0:1]
    gain_ref[1, K // 2 : K // 2 + 1, :] = two[0:1]


def own_forces(lam_ref, tiles_ref, data_ref, force_ref, turns, columns):
    turns[...] = fixed_turns(data_ref[0:3, :])
    force_ref[...] = jnp.zeros_like(force_ref)

    def prepare(c, carry):
        start = pl.multiple_of(c * CLUSTER, CLUSTER)
        lanes = pl.ds(start, CLUSTER)
        stack = jnp.concatenate([turns[:, lanes], data_ref[3:8, lanes]], axis=0)
        turned = stack.T
        for i in range(5):
            columns[i, lanes, :] = jnp.broadcast_to(turned[:, i : i + 1], (CLUSTER, CLUSTER))
        return carry

    lax.fori_loop(0, CLUSTERS, prepare, 0)
    floor_value = SOFT_FLOOR + SOFT_SCALE * lam_ref[0]

    def one_cluster(c, carry):
        start = pl.multiple_of(c * CLUSTER, CLUSTER)
        own = own_rows(data_ref, turns, start)
        total = [jnp.zeros((8, CLUSTER), F32) for _ in range(3)]
        for slot in range(4):
            base = c if slot == 0 else tiles_ref[c, slot]
            for chunk in range(CLUSTER // 8):
                rows = pl.ds(pl.multiple_of(base * CLUSTER + chunk * 8, 8), 8)
                other = [columns[i, rows, :] for i in range(5)]
                other[:3] = [x.astype(jnp.int32) for x in other[:3]]
                terms = pair_terms(own, other, floor_value)
                total = [a + b for a, b in zip(total, terms)]
        for i in range(3):
            force_ref[i : i + 1, pl.ds(start, CLUSTER)] = SPAN * jnp.sum(total[i], axis=0, keepdims=True)
        return carry

    lax.fori_loop(0, CLUSTERS, one_cluster, 0)


def own_kernel(lam_ref, tiles_ref, data_ref, force_ref, turns, columns):
    own_forces(lam_ref, tiles_ref, data_ref, force_ref, turns, columns)


def own_gain_kernel(
    lam_ref, tiles_ref, weights_ref, data_ref, rows_ref, lanes_ref, force_ref, gain_ref, turns, columns
):
    write_gain(weights_ref, rows_ref, lanes_ref, gain_ref)
    own_forces(lam_ref, tiles_ref, data_ref, force_ref, turns, columns)


def add_halo_forces(lam_ref, data_ref, below_ref, above_ref, partial_ref, force_ref, turns):
    turns[...] = fixed_turns(data_ref[0:3, :])
    floor_value = SOFT_FLOOR + SOFT_SCALE * lam_ref[0]

    def one_pair(k, carry):
        start = pl.multiple_of(k * CLUSTER, CLUSTER)
        starts = [pl.multiple_of(k * (2 * CLUSTER), CLUSTER), pl.multiple_of(k * (2 * CLUSTER) + CLUSTER, CLUSTER)]
        owns = [own_rows(data_ref, turns, s) for s in starts]
        totals = [[jnp.zeros((8, CLUSTER), F32) for _ in range(3)] for _ in range(2)]
        for source in (below_ref, above_ref):
            block = source[:, pl.ds(start, CLUSTER)]
            stack = jnp.where(iota_rows(8, CLUSTER) < 3, fixed_turns(block), block)
            turned = stack.T
            for chunk in range(CLUSTER // 8):
                part = turned[chunk * 8 : chunk * 8 + 8]
                other = [jnp.broadcast_to(part[:, i : i + 1], (8, CLUSTER)) for i in range(5)]
                other[:3] = [x.astype(jnp.int32) for x in other[:3]]
                for j in range(2):
                    terms = pair_terms(owns[j], other, floor_value)
                    totals[j] = [a + b for a, b in zip(totals[j], terms)]
        for j in range(2):
            lanes = pl.ds(starts[j], CLUSTER)
            for i in range(3):
                force_ref[i : i + 1, lanes] = partial_ref[i : i + 1, lanes] + SPAN * jnp.sum(
                    totals[j][i], axis=0, keepdims=True
                )
        return carry

    lax.fori_loop(0, HALO // CLUSTER, one_pair, 0)


def halo_kernel(lam_ref, data_ref, below_ref, above_ref, partial_ref, force_ref, turns):
    force_ref[...] = jnp.zeros_like(force_ref)
    add_halo_forces(lam_ref, data_ref, below_ref, above_ref, partial_ref, force_ref, turns)


def advance(force, kicks, data_ref, move_ref, lists_ref, data_out, move_out, low_ref, high_ref):
    mass = data_ref[5:6, :]
    velocity = move_ref[8:11, :]
    for _ in range(kicks):
        velocity = velocity + 0.5 * STEP_DT * force * mass
    off = move_ref[0:3, :] + STEP_DT * velocity
    move_out[...] = move_ref[...]
    move_out[0:3, :] = off
    move_out[8:11, :] = velocity
    data_out[...] = data_ref[...]
    data_out[0:3, :] = move_ref[3:6, :] + off
    write_halo(data_out[...], lists_ref, low_ref, high_ref)


def gather_kernel(
    pot_ref, data_ref, move_ref, short_ref, lists_ref, slab_ref,
    long_ref, data_out, move_out, low_ref, high_ref, force,
):
    off = move_ref[0:3, :]
    cells = move_ref[3:6, :].astype(jnp.int32)
    charge = data_ref[3:4, :]
    weights, slopes = spline_set(off)
    row = iota_rows(16, A_DEV)
    reach = jnp.where(row < 8, row, 8 + (row & 3)) - (cells[0:1] & 7)
    x_table = chosen(reach, [m[0:1] for m in weights])
    x_slope = chosen(reach, [m[0:1] for m in slopes])
    reach = (iota_rows(MODES, A_DEV) - cells[2:3]) & (MODES - 1)
    z_table = chosen(reach, [m[2:3] for m in weights])
    z_slope = chosen(reach, [m[2:3] for m in slopes])
    z_modes = jnp.dot(slab_ref[...], z_table, precision=HIGHEST, preferred_element_type=F32)
    z_tilts = jnp.dot(slab_ref[...], z_slope, precision=HIGHEST, preferred_element_type=F32)
    potential = split(pot_ref[...])
    upper = iota_rows(8, CLUSTER) < 4
    for c in range(CLUSTERS):
        lanes = slice(c * CLUSTER, (c + 1) * CLUSTER)
        reach = (iota_rows(K, CLUSTER) - cells[1:2, lanes]) & (K - 1)
        y_both = jnp.concatenate(
            [chosen(reach, [m[1:2, lanes] for m in weights]), chosen(reach, [m[1:2, lanes] for m in slopes])], axis=1
        )
        along = dot3(potential, split(y_both))
        value, tilt = along[:, :CLUSTER], along[:, CLUSTER:]
        sums = [[jnp.zeros((8, CLUSTER), F32) for _ in range(2)] for _ in range(3)]
        for i in range(N_DOM):
            pairs = []
            for table in (z_modes, z_tilts):
                first = jnp.broadcast_to(table[2 * i : 2 * i + 1, lanes], (8, CLUSTER))
                second = jnp.broadcast_to(table[2 * i + 1 : 2 * i + 2, lanes], (8, CLUSTER))
                pairs.append((first, second, jnp.where(upper, first, second)))
            for which, (source, table) in enumerate(((value, 0), (tilt, 0), (value, 1))):
                block = source[i * SLAB : (i + 1) * SLAB]
                first, second, mixed = pairs[table]
                sums[which][0] = sums[which][0] + (first * block[0:8] + second * block[8:16])
                sums[which][1] = sums[which][1] + mixed * block[16:24]
        for i in range(3):
            table = x_slope if i == 0 else x_table
            near = table[0:8, lanes] * sums[i][0] + table[8:16, lanes] * sums[i][1]
            force[i : i + 1, lanes] = -charge[:, lanes] * jnp.sum(near, axis=0, keepdims=True)
    long_ref[...] = jnp.zeros_like(long_ref)
    long_ref[0:3, :] = force[0:3, :]
    advance(
        short_ref[0:3, :] + force[0:3, :], 1, data_ref, move_ref, lists_ref, data_out, move_out, low_ref, high_ref
    )


def halo_step_kernel(
    lam_ref, data_ref, below_ref, above_ref, partial_ref, long_ref, move_ref, lists_ref,
    data_out, move_out, low_ref, high_ref, turns, force,
):
    add_halo_forces(lam_ref, data_ref, below_ref, above_ref, partial_ref, force, turns)
    total = force[0:3, :] + long_ref[0:3, :]
    advance(total, 2, data_ref, move_ref, lists_ref, data_out, move_out, low_ref, high_ref)


def halo_last_kernel(
    lam_ref, data_ref, below_ref, above_ref, partial_ref, long_ref, move_ref, move_out, turns, force
):
    add_halo_forces(lam_ref, data_ref, below_ref, above_ref, partial_ref, force, turns)
    total = force[0:3, :] + long_ref[0:3, :]
    move_out[...] = move_ref[...]
    move_out[8:11, :] = move_ref[8:11, :] + 0.5 * STEP_DT * total * data_ref[5:6, :]


def swap_flag(round_index, here_ref, there_ref):
    window = lax.axis_index("lam")
    windows = lax.axis_size("lam")
    row = 6 + round_index
    lower = jnp.logical_and(window % 2 == round_index % 2, window + 1 < windows)
    upper = jnp.logical_and(window % 2 != round_index % 2, window >= 1)
    here = jnp.where(lower, here_ref[row : row + 1, :], 0.0)
    there = jnp.where(upper, there_ref[row : row + 1, :], 0.0)
    return (here + there) == 1.0


def first_swap_kernel(here_ref, there_ref, out_ref):
    take = swap_flag(0, here_ref, there_ref)
    out_ref[0:6, :] = jnp.where(take, there_ref[0:6, :], here_ref[0:6, :])
    out_ref[6:8, :] = here_ref[6:8, :]
    out_ref[8:16, :] = jnp.where(take, there_ref[8:16, :], here_ref[8:16, :])


def last_swap_kernel(here_ref, there_ref, cells_ref, off_ref, vel_ref):
    take = swap_flag(1, here_ref, there_ref)
    state = jnp.where(take, there_ref[...], here_ref[...])
    off_ref[0] = state[0:3]
    cells_ref[0] = state[3:6].astype(jnp.int32)
    vel_ref[0] = state[8:11]


SMEM = pl.BlockSpec(memory_space=pltpu.SMEM)
VMEM = pl.BlockSpec(memory_space=pltpu.VMEM)


def call(kernel, ins, outs, scratch=(), cost=0):
    return pl.pallas_call(
        kernel,
        out_shape=[jax.ShapeDtypeStruct(shape, dtype) for shape, dtype in outs],
        in_specs=[SMEM if place == "s" else VMEM for place, _ in ins],
        out_specs=[VMEM] * len(outs),
        scratch_shapes=list(scratch),
        compiler_params=pltpu.CompilerParams(vmem_limit_bytes=40 * 2**20),
        cost_estimate=pl.CostEstimate(flops=cost, bytes_accessed=200000, transcendentals=0),
    )(*[value for _, value in ins])


def passed_along(value, axis, by):
    size = lax.axis_size(axis)
    return lax.ppermute(value, axis, [(i, (i + by) % size) for i in range(size)])


def traded(value, round_index):
    windows = lax.axis_size("lam")
    pairs = []
    for w in range(round_index % 2, windows - 1, 2):
        pairs += [(w, w + 1), (w + 1, w)]
    return lax.ppermute(value, "lam", pairs)


def exchanged(value):
    return lax.all_to_all(value, "dom", split_axis=0, concat_axis=0, tiled=True)


def body(
    cells, offsets, velocities, charges, coupling, inverse_mass, lambdas, tile_lists, halo_lists, accept_flags
):
    wide = ((8, A_DEV), F32)
    state = ((16, A_DEV), F32)
    border = ((8, HALO), F32)
    turns = pltpu.VMEM((3, A_DEV), F32)
    columns = pltpu.VMEM((5, A_DEV, CLUSTER), F32)
    tiles = tile_lists[0]
    slab = jnp.asarray(slab_basis())
    square, factor = plane_gain()
    gain_rows = np.zeros((K, 8), np.float32)
    gain_rows[:, 0], gain_rows[:, 1] = square, factor
    gain_lanes = np.zeros((8, K), np.float32)
    gain_lanes[0], gain_lanes[1] = square, factor

    grid, data, move, low, high = call(
        spread_kernel,
        [
            ("s", lambdas), ("s", accept_flags), ("v", cells), ("v", offsets), ("v", velocities),
            ("v", charges[None]), ("v", coupling[None]), ("v", inverse_mass[None]), ("v", halo_lists), ("v", slab),
        ],
        [((ROWS, K), F32), wide, state, border, border],
        [pltpu.VMEM((ROWS, A_DEV), BF16), pltpu.VMEM((ROWS, A_DEV), BF16)],
    )
    grid = exchanged(grid)
    below, above = passed_along(high, "dom", 1), passed_along(low, "dom", -1)
    short, gain = call(
        own_gain_kernel,
        [
            ("s", lambdas), ("s", tiles), ("s", jnp.asarray(slab_weights())), ("v", data),
            ("v", jnp.asarray(gain_rows)), ("v", jnp.asarray(gain_lanes)),
        ],
        [wide, ((2, K, K), F32)],
        [turns, columns],
        cost=2 * 10**9,
    )
    (potential,) = call(
        mesh_kernel,
        [("v", grid), ("v", gain), ("v", jnp.asarray(basis_table()))],
        [((ROWS, K), F32)],
        [pltpu.VMEM((2 * K, K), F32)],
    )
    potential = exchanged(potential)
    (short,) = call(
        halo_kernel,
        [("s", lambdas), ("v", data), ("v", below), ("v", above), ("v", short)],
        [wide],
        [turns],
        cost=10**9,
    )
    far, data, move, low, high = call(
        gather_kernel,
        [("v", potential), ("v", data), ("v", move), ("v", short), ("v", halo_lists), ("v", slab)],
        [wide, wide, state, border, border],
        [pltpu.VMEM((8, A_DEV), F32)],
    )

    def own_call(data):
        (partial,) = call(
            own_kernel, [("s", lambdas), ("s", tiles), ("v", data)], [wide], [turns, columns], cost=2 * 10**9
        )
        return partial

    below, above = passed_along(high, "dom", 1), passed_along(low, "dom", -1)
    short = own_call(data)
    data, move, low, high = call(
        halo_step_kernel,
        [
            ("s", lambdas), ("v", data), ("v", below), ("v", above), ("v", short), ("v", far), ("v", move),
            ("v", halo_lists),
        ],
        [wide, state, border, border],
        [turns, pltpu.VMEM((8, A_DEV), F32)],
    )
    below, above = passed_along(high, "dom", 1), passed_along(low, "dom", -1)
    short = own_call(data)
    (move,) = call(
        halo_last_kernel,
        [("s", lambdas), ("v", data), ("v", below), ("v", above), ("v", short), ("v", far), ("v", move)],
        [state],
        [turns, pltpu.VMEM((8, A_DEV), F32)],
    )
    (move,) = call(first_swap_kernel, [("v", move), ("v", traded(move, 0))], [state])
    triple = (1, 3, A_DEV)
    return tuple(
        call(
            last_swap_kernel,
            [("v", move), ("v", traded(move, 1))],
            [(triple, jnp.int32), (triple, F32), (triple, F32)],
        )
    )


def solution(mesh):
    in_specs = (
        P("lam", None, "dom"),
        P("lam", None, "dom"),
        P("lam", None, "dom"),
        P("dom"),
        P("dom"),
        P("dom"),
        P("lam"),
        P("lam", "dom", None),
        P("lam", "dom", None),
        P(None, "lam"),
    )
    out_specs = (P("lam", None, "dom"), P("lam", None, "dom"), P("lam", None, "dom"))
    return jax.shard_map(body, mesh=mesh, in_specs=in_specs, out_specs=out_specs, check_vma=False)
```

```python
import functools
import math

import jax
import jax.numpy as jnp
import ml_dtypes
import numpy as np
from jax import lax
from jax.experimental import pallas as pl
from jax.experimental.pallas import tpu as pltpu
from jax.sharding import PartitionSpec as P

K = 128
CLUSTER = 128
N_DOM = 16
A_DEV = 1024
CLUSTERS = 8
HALO = 512
MODES = 32
SLAB = 24
ROWS = N_DOM * SLAB

EWALD_BETA = 0.5
COULOMB = 20.0
LJ_DEPTH = 1.0
LJ_SIGMA_SQ = 0.49
SOFT_SCALE = 0.5
SOFT_FLOOR = 0.5
STEP_DT = 0.25

F32 = jnp.float32
BF16 = jnp.bfloat16
HIGHEST = lax.Precision.HIGHEST

TURN = 2.0**32
SPAN_SQ = 2.0**-50
SPAN = 2.0**-25

SCREEN = (
    -0.0818439527,
    0.648023047,
    -2.23331568,
    4.38709699,
    -5.37737017,
    4.16223694,
    -1.81397109,
    0.0540053844,
    0.5630337,
    -5.2346482e-05,
    0.282096019,
)


def real_basis(count):
    half = count // 2
    place = np.arange(count)
    rows = []
    for k in range(half + 1):
        scale = math.sqrt((1.0 if k in (0, half) else 2.0) / count)
        rows.append(scale * np.cos(2.0 * np.pi * (k * place % count) / count))
    for k in range(1, half):
        rows.append(math.sqrt(2.0 / count) * np.sin(2.0 * np.pi * (k * place % count) / count))
    return np.stack(rows)


def halves(table):
    high = table.astype(np.float32).astype(ml_dtypes.bfloat16)
    low = (table - high.astype(np.float64)).astype(np.float32).astype(ml_dtypes.bfloat16)
    return high, low


def basis_table():
    basis = real_basis(K)
    high, low = halves(basis)
    return np.concatenate([high, low, high.T, low.T], axis=0)


def slab_basis():
    basis = real_basis(MODES)
    order = [0, MODES // 2]
    for k in range(1, MODES // 2):
        order += [k, MODES // 2 + k]
    return basis[np.array(order)].astype(np.float32)


def spline_modulus(k):
    return (3.0 / (2.0 + np.cos(2.0 * np.pi * k / K))) ** 2


def slab_weights():
    k = np.arange(K // 2 + 1)
    delta = np.arange(-MODES // 2 + 1, MODES // 2 + 1)
    folded = np.where((k == 0) | (k == K // 2), 1.0, 2.0)
    own = folded * np.exp(-np.pi**2 * (k / K) ** 2 / EWALD_BETA**2) * spline_modulus(k)
    rows = []
    for j in range(MODES // 2 + 1):
        window = np.cos(2 * np.pi * k[:, None] * delta / K) * np.cos(2 * np.pi * j * delta / MODES)
        rows.append(own * window.sum(axis=1))
    return np.stack(rows).astype(np.float32)


def plane_gain():
    k = np.concatenate([np.arange(K // 2 + 1), np.arange(1, K // 2)])
    square = (k / K) ** 2
    factor = np.exp(-np.pi**2 * square / EWALD_BETA**2) * spline_modulus(k)
    return square.astype(np.float32), factor.astype(np.float32)


def split(x):
    high = x.astype(BF16)
    return high, (x - high.astype(F32)).astype(BF16)


def dot3(left, right, dims=(((1,), (0,)), ((), ()))):
    lh, ll = left
    rh, rl = right
    dot = functools.partial(lax.dot_general, dimension_numbers=dims, preferred_element_type=F32)
    return dot(lh, rh) + (dot(lh, rl) + dot(ll, rh))


def spline_set(u):
    v = 1.0 - u
    u2 = u * u
    u3 = u2 * u
    weights = (
        v * v * v / 6.0,
        (3.0 * u3 - 6.0 * u2 + 4.0) / 6.0,
        (-3.0 * u3 + 3.0 * u2 + 3.0 * u + 1.0) / 6.0,
        u3 / 6.0,
    )
    slopes = (-0.5 * v * v, 1.5 * u2 - 2.0 * u, -1.5 * u2 + u + 0.5, 0.5 * u2)
    return weights, slopes


def chosen(distance, rows):
    out = jnp.where(distance == 3, rows[3], 0.0)
    for k in (2, 1, 0):
        out = jnp.where(distance == k, rows[k], out)
    return out


def iota_rows(rows, columns):
    return lax.broadcasted_iota(jnp.int32, (rows, columns), 0)


def fixed_turns(x):
    t = x * (1.0 / K)
    f = t - jnp.floor(t + 0.5)
    return jnp.maximum(f, -0.5) * TURN


def pair_terms(own, other, floor_value):
    ax, ay, az, qa, wa = own
    bx, by, bz, qb, wb = other
    dx = (ax - bx).astype(F32)
    dy = (ay - by).astype(F32)
    dz = (az - bz).astype(F32)
    s = (dx * dx + dy * dy + dz * dz) * SPAN_SQ + floor_value
    w = lax.rsqrt(s)
    u = w * w
    screen = jnp.full_like(w, SCREEN[0])
    for c in SCREEN[1:]:
        screen = screen * w + c
    gauss = jnp.exp2(s * (-(EWALD_BETA**2) * math.log2(math.e)))
    a = LJ_SIGMA_SQ * u
    t = a * a * a
    g = u * ((qa * qb) * (gauss * screen) + (wa * wb) * (t * (t - 0.5)))
    return g * dx, g * dy, g * dz


def own_rows(data_ref, turns, start, rows=8):
    def spread(row):
        return jnp.broadcast_to(row, (rows, CLUSTER))

    columns = pl.ds(start, CLUSTER)
    xyz = [spread(turns[i : i + 1, columns].astype(jnp.int32)) for i in range(3)]
    q = spread(data_ref[3:4, columns] * (2.0 * COULOMB))
    w = spread(data_ref[4:5, columns] * (48.0 * LJ_DEPTH))
    return (*xyz, q, w)


def write_halo(data, lists_ref, inner_ref, outer_ref):
    even = lax.axis_index("dom") % 2 == 0
    lane = lax.broadcasted_iota(jnp.int32, (8, CLUSTER), 1)
    for flip, out_ref in ((False, inner_ref), (True, outer_ref)):
        for k in range(HALO // CLUSTER):
            columns = slice(k * CLUSTER, (k + 1) * CLUSTER)
            low, high = lists_ref[0, 0:1, columns], lists_ref[0, 1:2, columns]
            row = jnp.where(even, low, high) if flip else jnp.where(even, high, low)
            index = jnp.broadcast_to(row & (CLUSTER - 1), (8, CLUSTER))
            first = data[:, 2 * k * CLUSTER : (2 * k + 1) * CLUSTER]
            second = data[:, (2 * k + 1) * CLUSTER : (2 * k + 2) * CLUSTER]
            out_ref[:, columns] = jnp.where(
                lane < CLUSTER // 2,
                jnp.take_along_axis(first, index, axis=1, mode="promise_in_bounds"),
                jnp.take_along_axis(second, index, axis=1, mode="promise_in_bounds"),
            )


def spread_kernel(
    lam_ref, flag_ref, cells_ref, off_ref, vel_ref, charge_ref, coup_ref, mass_ref, lists_ref, slab_ref,
    out_ref, data_ref, move_ref, low_ref, high_ref, mixed_high, mixed_low,
):
    weight = 1.0 - lam_ref[0] * coup_ref[...]
    charge = charge_ref[...] * weight

    for i in range(3):
        cell = cells_ref[i].astype(F32)
        move_ref[i : i + 1, :] = off_ref[i]
        move_ref[3 + i : 4 + i, :] = cell
        move_ref[8 + i : 9 + i, :] = vel_ref[i]
        data_ref[i : i + 1, :] = cell + off_ref[i]
    move_ref[6:7, :] = jnp.full((1, A_DEV), flag_ref[0, 0].astype(F32))
    move_ref[7:8, :] = jnp.full((1, A_DEV), flag_ref[0, 1].astype(F32))
    move_ref[11:16, :] = jnp.zeros((5, A_DEV), F32)
    data_ref[3:4, :] = charge
    data_ref[4:5, :] = weight
    data_ref[5:6, :] = mass_ref[...]
    data_ref[6:8, :] = jnp.zeros((2, A_DEV), F32)
    write_halo(data_ref[...], lists_ref, low_ref, high_ref)

    off = move_ref[0:3, :]
    cells = [cells_ref[i] for i in range(3)]
    weights, _ = spline_set(off)
    row = iota_rows(16, A_DEV)
    plane = jnp.where(row < 8, row, 8 + (row & 3))
    x_table = chosen(plane - (cells[0] & 7), [m[0:1] for m in weights]) * charge
    z_table = chosen((iota_rows(MODES, A_DEV) - cells[2]) & (MODES - 1), [m[2:3] for m in weights])
    z_modes = jnp.dot(slab_ref[...], z_table, precision=HIGHEST, preferred_element_type=F32)
    y_table = chosen((iota_rows(K, A_DEV) - cells[1]) & (K - 1), [m[1:2] for m in weights])

    near, far = x_table[0:8], x_table[8:16]
    upper = iota_rows(8, A_DEV) < 4
    for i in range(0, N_DOM, 2):
        pieces = []
        for k in (i, i + 1):
            first = jnp.broadcast_to(z_modes[2 * k : 2 * k + 1], (8, A_DEV))
            second = jnp.broadcast_to(z_modes[2 * k + 1 : 2 * k + 2], (8, A_DEV))
            pieces += [near * first, near * second, far * jnp.where(upper, first, second)]
        high, low = split(jnp.concatenate(pieces, axis=0))
        mixed_high[i * SLAB : (i + 2) * SLAB, :] = high
        mixed_low[i * SLAB : (i + 2) * SLAB, :] = low
    out_ref[...] = dot3((mixed_high[...], mixed_low[...]), split(y_table), (((1,), (1,)), ((), ())))


def mesh_kernel(grid_ref, gain_ref, basis_ref, inner_ref, outer_ref, out_ref, block):
    del inner_ref, outer_ref
    top = iota_rows(8, K) < 4
    for e in range(N_DOM):
        spill = grid_ref[((e - 1) % N_DOM) * SLAB + 16 : ((e - 1) % N_DOM) * SLAB + 24, :]
        turned = pltpu.roll(spill, 4, 0)
        block[8 * e : 8 * e + 8, :] = grid_ref[e * SLAB : e * SLAB + 8, :] + jnp.where(top, spill, 0.0)
        block[K + 8 * e : K + 8 * e + 8, :] = grid_ref[e * SLAB + 8 : e * SLAB + 16, :] + jnp.where(top, turned, 0.0)
    basis = (basis_ref[0:K, :], basis_ref[K : 2 * K, :])
    turned_basis = (basis_ref[2 * K : 3 * K, :], basis_ref[3 * K : 4 * K, :])
    along_y = dot3(split(block[...]), turned_basis)
    for mode in range(2):
        part = split(along_y[mode * K : (mode + 1) * K])
        scaled = dot3(basis, part) * gain_ref[mode]
        block[mode * K : (mode + 1) * K, :] = dot3(turned_basis, split(scaled))
    block[...] = dot3(split(block[...]), basis)
    for e in range(N_DOM):
        following = 8 * ((e + 1) % N_DOM)
        out_ref[e * SLAB : e * SLAB + 8, :] = block[8 * e : 8 * e + 8, :]
        out_ref[e * SLAB + 8 : e * SLAB + 16, :] = block[K + 8 * e : K + 8 * e + 8, :]
        out_ref[e * SLAB + 16 : e * SLAB + 24, :] = jnp.where(
            top,
            block[following : following + 8, :],
            pltpu.roll(block[K + following : K + following + 8, :], 4, 0),
        )


def write_gain(mode_weights_ref, rows_ref, lanes_ref, gain_ref):
    dom = lax.axis_index("dom")
    square_y, factor_y = lanes_ref[0:1, :], lanes_ref[1:2, :]
    scale = COULOMB / (math.pi * K)
    first = dom
    second = jnp.where(dom == 0, MODES // 2, dom)

    def totals(square):
        one = jnp.zeros_like(square)
        two = jnp.zeros_like(square)
        for k in range(K // 2 + 1):
            whole = square + (k / K) ** 2
            inverse = 1.0 / whole if k else jnp.where(whole > 0.0, 1.0 / jnp.where(whole > 0.0, whole, 1.0), 0.0)
            one = one + inverse * mode_weights_ref[first, k]
            two = two + inverse * mode_weights_ref[second, k]
        return one, two

    def block(start):
        rows = pl.ds(start, 8)
        square = jnp.broadcast_to(rows_ref[rows, 0:1], (8, K)) + square_y
        factor = jnp.broadcast_to(rows_ref[rows, 1:2], (8, K)) * factor_y * scale
        one, two = totals(square)
        return one * factor, two * factor

    def step(b, carry):
        start = pl.multiple_of(b * 8, 8)
        one, two = block(start)
        gain_ref[0, pl.ds(start, 8), :] = one
        gain_ref[1, pl.ds(start, 8), :] = two
        gain_ref[0, pl.ds(start + K // 2, 8), :] = one
        gain_ref[1, pl.ds(start + K // 2, 8), :] = two
        return carry

    lax.fori_loop(0, 8, step, 0)
    one, two = block(K // 2)
    gain_ref[0, K // 2 : K // 2 + 1, :] = one[0:1]
    gain_ref[1, K // 2 : K // 2 + 1, :] = two[0:1]


def listed(tiles_ref, row, cluster):
    count = jnp.int32(0)
    for slot in range(1, 4):
        count = count + jnp.where(tiles_ref[slot, 0, row] == cluster, 1, 0)
    return count.astype(F32)


def own_forces(lam_ref, tiles_ref, data_ref, force_ref, turns, near, sides, first, last):
    turns[...] = fixed_turns(data_ref[0:3, :])
    near[...] = jnp.zeros_like(near)
    sides[...] = jnp.zeros_like(sides)
    floor_value = SOFT_FLOOR + SOFT_SCALE * lam_ref[0]

    def one_cluster(b, carry):
        start = pl.multiple_of(b * CLUSTER, CLUSTER)
        lanes = pl.ds(start, CLUSTER)
        turned = jnp.concatenate([turns[:, lanes], data_ref[3:8, lanes]], axis=0).T
        others = [b, (b + 1) % CLUSTERS, (b + 2) % CLUSTERS]
        owns = [own_rows(data_ref, turns, pl.multiple_of(a * CLUSTER, CLUSTER)) for a in others]
        totals = [[jnp.zeros((8, CLUSTER), F32) for _ in range(3)] for _ in others]
        back = [None] + [listed(tiles_ref, b, a) for a in others[1:]]
        for chunk in range(CLUSTER // 8):
            part = turned[chunk * 8 : chunk * 8 + 8]
            other = [jnp.broadcast_to(part[:, i : i + 1], (8, CLUSTER)) for i in range(5)]
            other[:3] = [x.astype(jnp.int32) for x in other[:3]]
            side = []
            for j in range(3):
                terms = pair_terms(owns[j], other, floor_value)
                totals[j] = [p + q for p, q in zip(totals[j], terms)]
                if j:
                    side.append([back[j] * p for p in terms])
            for i in range(3):
                sides[pl.ds(start + chunk * 8, 8), i : i + 1] = jnp.sum(
                    side[0][i] + side[1][i], axis=1, keepdims=True
                )
        for j, a in enumerate(others):
            rows = pl.ds(pl.multiple_of(a * 8, 8), 8)
            for i in range(3):
                total = listed(tiles_ref, a, b) * totals[j][i] if j else totals[j][i]
                near[i, rows, :] = near[i, rows, :] + total
        return carry

    lax.fori_loop(first, last, one_cluster, 0)
    force_ref[...] = jnp.zeros_like(force_ref)
    for c in range(CLUSTERS):
        lanes = slice(c * CLUSTER, (c + 1) * CLUSTER)
        turned = sides[lanes, :].T
        for i in range(3):
            total = jnp.sum(near[i, c * 8 : (c + 1) * 8, :], axis=0, keepdims=True) - turned[i : i + 1]
            force_ref[i : i + 1, lanes] = SPAN * total


def own_kernel(lam_ref, tiles_ref, data_ref, force_ref, turns, near, sides):
    own_forces(lam_ref, tiles_ref, data_ref, force_ref, turns, near, sides, 0, CLUSTERS)


def gain_kernel(
    lam_ref, tiles_ref, weights_ref, data_ref, rows_ref, lanes_ref, force_ref, gain_ref, turns, near, sides
):
    write_gain(weights_ref, rows_ref, lanes_ref, gain_ref)
    own_forces(lam_ref, tiles_ref, data_ref, force_ref, turns, near, sides, 0, CLUSTERS // 2)


def add_halo_forces(lam_ref, data_ref, below_ref, above_ref, partial_ref, force_ref, turns):
    turns[...] = fixed_turns(data_ref[0:3, :])
    floor_value = SOFT_FLOOR + SOFT_SCALE * lam_ref[0]

    def one_pair(k, carry):
        start = pl.multiple_of(k * CLUSTER, CLUSTER)
        starts = [pl.multiple_of(k * (2 * CLUSTER), CLUSTER), pl.multiple_of(k * (2 * CLUSTER) + CLUSTER, CLUSTER)]
        owns = [own_rows(data_ref, turns, s) for s in starts]
        totals = [[jnp.zeros((8, CLUSTER), F32) for _ in range(3)] for _ in range(2)]
        for source in (below_ref, above_ref):
            block = source[:, pl.ds(start, CLUSTER)]
            stack = jnp.where(iota_rows(8, CLUSTER) < 3, fixed_turns(block), block)
            turned = stack.T
            for chunk in range(CLUSTER // 8):
                part = turned[chunk * 8 : chunk * 8 + 8]
                other = [jnp.broadcast_to(part[:, i : i + 1], (8, CLUSTER)) for i in range(5)]
                other[:3] = [x.astype(jnp.int32) for x in other[:3]]
                for j in range(2):
                    terms = pair_terms(owns[j], other, floor_value)
                    totals[j] = [a + b for a, b in zip(totals[j], terms)]
        for j in range(2):
            lanes = pl.ds(starts[j], CLUSTER)
            for i in range(3):
                force_ref[i : i + 1, lanes] = partial_ref[i : i + 1, lanes] + SPAN * jnp.sum(
                    totals[j][i], axis=0, keepdims=True
                )
        return carry

    lax.fori_loop(0, HALO // CLUSTER, one_pair, 0)


def rest_kernel(
    lam_ref, tiles_ref, data_ref, inner_ref, outer_ref, partial_ref, force_ref, turns, near, sides, second
):
    own_forces(lam_ref, tiles_ref, data_ref, second, turns, near, sides, CLUSTERS // 2, CLUSTERS)
    second[...] = second[...] + partial_ref[...]
    force_ref[...] = jnp.zeros_like(force_ref)
    add_halo_forces(lam_ref, data_ref, inner_ref, outer_ref, second, force_ref, turns)


def advance(force, kicks, data_ref, move_ref, lists_ref, data_out, move_out, low_ref, high_ref):
    mass = data_ref[5:6, :]
    velocity = move_ref[8:11, :]
    for _ in range(kicks):
        velocity = velocity + 0.5 * STEP_DT * force * mass
    off = move_ref[0:3, :] + STEP_DT * velocity
    move_out[...] = move_ref[...]
    move_out[0:3, :] = off
    move_out[8:11, :] = velocity
    data_out[...] = data_ref[...]
    data_out[0:3, :] = move_ref[3:6, :] + off
    write_halo(data_out[...], lists_ref, low_ref, high_ref)


def gather_kernel(
    pot_ref, data_ref, move_ref, short_ref, lists_ref, slab_ref,
    long_ref, data_out, move_out, low_ref, high_ref, force,
):
    off = move_ref[0:3, :]
    cells = move_ref[3:6, :].astype(jnp.int32)
    charge = data_ref[3:4, :]
    weights, slopes = spline_set(off)
    row = iota_rows(16, A_DEV)
    reach = jnp.where(row < 8, row, 8 + (row & 3)) - (cells[0:1] & 7)
    x_table = chosen(reach, [m[0:1] for m in weights])
    x_slope = chosen(reach, [m[0:1] for m in slopes])
    reach = (iota_rows(MODES, A_DEV) - cells[2:3]) & (MODES - 1)
    z_table = chosen(reach, [m[2:3] for m in weights])
    z_slope = chosen(reach, [m[2:3] for m in slopes])
    z_modes = jnp.dot(slab_ref[...], z_table, precision=HIGHEST, preferred_element_type=F32)
    z_tilts = jnp.dot(slab_ref[...], z_slope, precision=HIGHEST, preferred_element_type=F32)
    potential = split(pot_ref[...])
    upper = iota_rows(8, CLUSTER) < 4
    for c in range(CLUSTERS):
        lanes = slice(c * CLUSTER, (c + 1) * CLUSTER)
        reach = (iota_rows(K, CLUSTER) - cells[1:2, lanes]) & (K - 1)
        y_both = jnp.concatenate(
            [chosen(reach, [m[1:2, lanes] for m in weights]), chosen(reach, [m[1:2, lanes] for m in slopes])], axis=1
        )
        along = dot3(potential, split(y_both))
        value, tilt = along[:, :CLUSTER], along[:, CLUSTER:]
        sums = [[jnp.zeros((8, CLUSTER), F32) for _ in range(2)] for _ in range(3)]
        for i in range(N_DOM):
            pairs = []
            for table in (z_modes, z_tilts):
                first = jnp.broadcast_to(table[2 * i : 2 * i + 1, lanes], (8, CLUSTER))
                second = jnp.broadcast_to(table[2 * i + 1 : 2 * i + 2, lanes], (8, CLUSTER))
                pairs.append((first, second, jnp.where(upper, first, second)))
            for which, (source, table) in enumerate(((value, 0), (tilt, 0), (value, 1))):
                block = source[i * SLAB : (i + 1) * SLAB]
                first, second, mixed = pairs[table]
                sums[which][0] = sums[which][0] + (first * block[0:8] + second * block[8:16])
                sums[which][1] = sums[which][1] + mixed * block[16:24]
        for i in range(3):
            table = x_slope if i == 0 else x_table
            near = table[0:8, lanes] * sums[i][0] + table[8:16, lanes] * sums[i][1]
            force[i : i + 1, lanes] = -charge[:, lanes] * jnp.sum(near, axis=0, keepdims=True)
    long_ref[...] = jnp.zeros_like(long_ref)
    long_ref[0:3, :] = force[0:3, :]
    advance(
        short_ref[0:3, :] + force[0:3, :], 1, data_ref, move_ref, lists_ref, data_out, move_out, low_ref, high_ref
    )


def halo_step_kernel(
    lam_ref, data_ref, below_ref, above_ref, partial_ref, long_ref, move_ref, lists_ref,
    data_out, move_out, low_ref, high_ref, turns, force,
):
    add_halo_forces(lam_ref, data_ref, below_ref, above_ref, partial_ref, force, turns)
    total = force[0:3, :] + long_ref[0:3, :]
    advance(total, 2, data_ref, move_ref, lists_ref, data_out, move_out, low_ref, high_ref)


def halo_last_kernel(
    lam_ref, data_ref, below_ref, above_ref, partial_ref, long_ref, move_ref, state_ref, turns, force
):
    add_halo_forces(lam_ref, data_ref, below_ref, above_ref, partial_ref, force, turns)
    total = force[0:3, :] + long_ref[0:3, :]
    velocity = move_ref[8:11, :] + 0.5 * STEP_DT * total * data_ref[5:6, :]
    for i in range(3):
        state_ref[i] = move_ref[i : i + 1, :]
        state_ref[3 + i] = velocity[i : i + 1]
        state_ref[6 + i] = move_ref[3 + i : 4 + i, :]
    state_ref[9] = move_ref[6:7, :]
    state_ref[10] = move_ref[7:8, :]


def settle_kernel(here_ref, first_ref, second_ref, third_ref, cells_ref, off_ref, vel_ref):
    window = lax.axis_index("lam")
    even = window % 2 == 0
    inside = window + 1 < lax.axis_size("lam")
    outer = jnp.where(even, second_ref[10], jnp.where(inside, here_ref[10], 0.0)) == 1.0
    far = jnp.where(even, third_ref[9], second_ref[9]) == 1.0
    close = jnp.where(even, here_ref[9], first_ref[9]) == 1.0
    for i in range(9):
        row = jnp.where(
            outer,
            jnp.where(far, third_ref[i], second_ref[i]),
            jnp.where(close, first_ref[i], here_ref[i]),
        )
        if i < 3:
            off_ref[i] = row
        elif i < 6:
            vel_ref[i - 3] = row
        else:
            cells_ref[i - 6] = row.astype(jnp.int32)


PLACES = {
    "s": pl.BlockSpec(memory_space=pltpu.SMEM),
    "v": pl.BlockSpec(memory_space=pltpu.VMEM),
    "a": pl.BlockSpec(memory_space=pl.ANY),
}


def call(kernel, ins, outs, scratch=(), cost=0):
    return pl.pallas_call(
        kernel,
        out_shape=[jax.ShapeDtypeStruct(shape, dtype) for shape, dtype in outs],
        in_specs=[PLACES[place] for place, _ in ins],
        out_specs=[PLACES["v"]] * len(outs),
        scratch_shapes=list(scratch),
        compiler_params=pltpu.CompilerParams(vmem_limit_bytes=40 * 2**20),
        cost_estimate=pl.CostEstimate(flops=cost, bytes_accessed=200000, transcendentals=0),
    )(*[value for _, value in ins])


def neighbours(inner, outer):
    size = lax.axis_size("dom")
    received = []
    for value, offset in ((inner, 0), (outer, 1)):
        pairs = []
        for d in range(offset, size, 2):
            pairs += [(d, (d + 1) % size), ((d + 1) % size, d)]
        received.append(lax.ppermute(value, "dom", pairs))
    return received


def ladder_states(state):
    windows = lax.axis_size("lam")
    received = []
    for offset in (0, 1):
        pairs = []
        for w in range(offset, windows - 1, 2):
            pairs += [(w, w + 1), (w + 1, w)]
        received.append(lax.ppermute(state, "lam", pairs))
    pairs = [(w - 2, w) for w in range(2, windows, 2)] + [(w + 2, w) for w in range(1, windows - 2, 2)]
    received.append(lax.ppermute(state, "lam", pairs))
    return received


def exchanged(value):
    return lax.all_to_all(value, "dom", split_axis=0, concat_axis=0, tiled=True)


def body(
    cells, offsets, velocities, charges, coupling, inverse_mass, lambdas, tile_lists, halo_lists, accept_flags
):
    wide = ((8, A_DEV), F32)
    moving = ((16, A_DEV), F32)
    border = ((8, HALO), F32)
    turns = pltpu.VMEM((3, A_DEV), F32)
    pair_scratch = [turns, pltpu.VMEM((3, CLUSTERS * 8, CLUSTER), F32), pltpu.VMEM((A_DEV, 8), F32)]
    spare = pltpu.VMEM((8, A_DEV), F32)
    tiles = jnp.transpose(tile_lists, (2, 0, 1))
    slab = jnp.asarray(slab_basis())
    square, factor = plane_gain()
    gain_rows = np.zeros((K, 8), np.float32)
    gain_rows[:, 0], gain_rows[:, 1] = square, factor
    gain_lanes = np.zeros((8, K), np.float32)
    gain_lanes[0], gain_lanes[1] = square, factor

    def by_row(x):
        return jnp.transpose(x, (1, 0, 2))

    grid, data, move, inner, outer = call(
        spread_kernel,
        [
            ("s", lambdas), ("s", accept_flags.T), ("v", by_row(cells)), ("v", by_row(offsets)),
            ("v", by_row(velocities)), ("v", charges[None]), ("v", coupling[None]), ("v", inverse_mass[None]),
            ("v", halo_lists), ("v", slab),
        ],
        [((ROWS, K), F32), wide, moving, border, border],
        [pltpu.VMEM((ROWS, A_DEV), BF16), pltpu.VMEM((ROWS, A_DEV), BF16)],
    )
    grid = exchanged(grid)
    inner, outer = neighbours(inner, outer)
    short, gain = call(
        gain_kernel,
        [
            ("s", lambdas), ("s", tiles), ("s", jnp.asarray(slab_weights())), ("v", data),
            ("v", jnp.asarray(gain_rows)), ("v", jnp.asarray(gain_lanes)),
        ],
        [wide, ((2, K, K), F32)],
        pair_scratch,
        cost=2 * 10**9,
    )
    (potential,) = call(
        mesh_kernel,
        [("v", grid), ("v", gain), ("v", jnp.asarray(basis_table())), ("a", inner), ("a", outer)],
        [((ROWS, K), F32)],
        [pltpu.VMEM((2 * K, K), F32)],
    )
    potential = exchanged(potential)
    (short,) = call(
        rest_kernel,
        [("s", lambdas), ("s", tiles), ("v", data), ("v", inner), ("v", outer), ("v", short)],
        [wide],
        [*pair_scratch, spare],
        cost=2 * 10**9,
    )
    far, data, move, inner, outer = call(
        gather_kernel,
        [("v", potential), ("v", data), ("v", move), ("v", short), ("v", halo_lists), ("v", slab)],
        [wide, wide, moving, border, border],
        [spare],
    )

    def own_call(data):
        (partial,) = call(
            own_kernel, [("s", lambdas), ("s", tiles), ("v", data)], [wide], pair_scratch, cost=2 * 10**9
        )
        return partial

    inner, outer = neighbours(inner, outer)
    short = own_call(data)
    data, move, inner, outer = call(
        halo_step_kernel,
        [
            ("s", lambdas), ("v", data), ("v", inner), ("v", outer), ("v", short), ("v", far), ("v", move),
            ("v", halo_lists),
        ],
        [wide, moving, border, border],
        [turns, spare],
    )
    inner, outer = neighbours(inner, outer)
    short = own_call(data)
    (state,) = call(
        halo_last_kernel,
        [("s", lambdas), ("v", data), ("v", inner), ("v", outer), ("v", short), ("v", far), ("v", move)],
        [((11, 1, A_DEV), F32)],
        [turns, spare],
    )
    first, second, third = ladder_states(state)
    triple = (3, 1, A_DEV)
    out = call(
        settle_kernel,
        [("v", state), ("v", first), ("v", second), ("v", third)],
        [(triple, jnp.int32), (triple, F32), (triple, F32)],
    )
    return tuple(by_row(x) for x in out)


def solution(mesh):
    in_specs = (
        P("lam", None, "dom"),
        P("lam", None, "dom"),
        P("lam", None, "dom"),
        P("dom"),
        P("dom"),
        P("dom"),
        P("lam"),
        P("lam", "dom", None),
        P("lam", "dom", None),
        P(None, "lam"),
    )
    out_specs = (P("lam", None, "dom"), P("lam", None, "dom"), P("lam", None, "dom"))
    return jax.shard_map(body, mesh=mesh, in_specs=in_specs, out_specs=out_specs, check_vma=False)
```

```python
import functools
import math

import jax
import jax.numpy as jnp
import ml_dtypes
import numpy as np
from jax import lax
from jax.experimental import pallas as pl
from jax.experimental.pallas import tpu as pltpu
from jax.sharding import PartitionSpec as P

K = 128
CLUSTER = 128
N_DOM = 16
A_DEV = 1024
CLUSTERS = 8
HALO = 512
MODES = 32
SLAB = 24
ROWS = N_DOM * SLAB

EWALD_BETA = 0.5
COULOMB = 20.0
LJ_DEPTH = 1.0
LJ_SIGMA_SQ = 0.49
SOFT_SCALE = 0.5
SOFT_FLOOR = 0.5
STEP_DT = 0.25

F32 = jnp.float32
BF16 = jnp.bfloat16
HIGHEST = lax.Precision.HIGHEST

TURN = 2.0**32
SPAN_SQ = 2.0**-50
SPAN = 2.0**-25

SCREEN = (
    -0.0818439527,
    0.648023047,
    -2.23331568,
    4.38709699,
    -5.37737017,
    4.16223694,
    -1.81397109,
    0.0540053844,
    0.5630337,
    -5.2346482e-05,
    0.282096019,
)


def real_basis(count):
    half = count // 2
    place = np.arange(count)
    rows = []
    for k in range(half + 1):
        scale = math.sqrt((1.0 if k in (0, half) else 2.0) / count)
        rows.append(scale * np.cos(2.0 * np.pi * (k * place % count) / count))
    for k in range(1, half):
        rows.append(math.sqrt(2.0 / count) * np.sin(2.0 * np.pi * (k * place % count) / count))
    return np.stack(rows)


def halves(table):
    high = table.astype(np.float32).astype(ml_dtypes.bfloat16)
    low = (table - high.astype(np.float64)).astype(np.float32).astype(ml_dtypes.bfloat16)
    return high, low


def basis_table():
    basis = real_basis(K)
    high, low = halves(basis)
    return np.concatenate([high, low, high.T, low.T], axis=0)


def slab_basis():
    basis = real_basis(MODES)
    order = [0, MODES // 2]
    for k in range(1, MODES // 2):
        order += [k, MODES // 2 + k]
    return basis[np.array(order)].astype(np.float32)


def spline_modulus(k):
    return (3.0 / (2.0 + np.cos(2.0 * np.pi * k / K))) ** 2


def slab_weights():
    k = np.arange(K // 2 + 1)
    delta = np.arange(-MODES // 2 + 1, MODES // 2 + 1)
    folded = np.where((k == 0) | (k == K // 2), 1.0, 2.0)
    own = folded * np.exp(-np.pi**2 * (k / K) ** 2 / EWALD_BETA**2) * spline_modulus(k)
    rows = []
    for j in range(MODES // 2 + 1):
        window = np.cos(2 * np.pi * k[:, None] * delta / K) * np.cos(2 * np.pi * j * delta / MODES)
        rows.append(own * window.sum(axis=1))
    return np.stack(rows).astype(np.float32)


def plane_gain():
    k = np.concatenate([np.arange(K // 2 + 1), np.arange(1, K // 2)])
    square = (k / K) ** 2
    factor = np.exp(-np.pi**2 * square / EWALD_BETA**2) * spline_modulus(k)
    return square.astype(np.float32), factor.astype(np.float32)


def split(x):
    high = x.astype(BF16)
    return high, (x - high.astype(F32)).astype(BF16)


def dot3(left, right, dims=(((1,), (0,)), ((), ()))):
    lh, ll = left
    rh, rl = right
    dot = functools.partial(lax.dot_general, dimension_numbers=dims, preferred_element_type=F32)
    return dot(lh, rh) + (dot(lh, rl) + dot(ll, rh))


def spline_set(u):
    v = 1.0 - u
    u2 = u * u
    u3 = u2 * u
    weights = (
        v * v * v / 6.0,
        (3.0 * u3 - 6.0 * u2 + 4.0) / 6.0,
        (-3.0 * u3 + 3.0 * u2 + 3.0 * u + 1.0) / 6.0,
        u3 / 6.0,
    )
    slopes = (-0.5 * v * v, 1.5 * u2 - 2.0 * u, -1.5 * u2 + u + 0.5, 0.5 * u2)
    return weights, slopes


def chosen(distance, rows):
    out = jnp.where(distance == 3, rows[3], 0.0)
    for k in (2, 1, 0):
        out = jnp.where(distance == k, rows[k], out)
    return out


def iota_rows(rows, columns):
    return lax.broadcasted_iota(jnp.int32, (rows, columns), 0)


def fixed_turns(x):
    t = x * (1.0 / K)
    f = t - jnp.floor(t + 0.5)
    return jnp.maximum(f, -0.5) * TURN


def pair_terms(own, other, floor_value):
    ax, ay, az, qa, wa = own
    bx, by, bz, qb, wb = other
    dx = (ax - bx).astype(F32)
    dy = (ay - by).astype(F32)
    dz = (az - bz).astype(F32)
    s = (dx * dx + dy * dy + dz * dz) * SPAN_SQ + floor_value
    w = lax.rsqrt(s)
    u = w * w
    screen = jnp.full_like(w, SCREEN[0])
    for c in SCREEN[1:]:
        screen = screen * w + c
    gauss = jnp.exp2(s * (-(EWALD_BETA**2) * math.log2(math.e)))
    a = LJ_SIGMA_SQ * u
    t = a * a * a
    g = u * ((qa * qb) * (gauss * screen) + (wa * wb) * (t * (t - 0.5)))
    return g * dx, g * dy, g * dz


def own_rows(data_ref, turns, start, rows=8):
    def spread(row):
        return jnp.broadcast_to(row, (rows, CLUSTER))

    columns = pl.ds(start, CLUSTER)
    xyz = [spread(turns[i : i + 1, columns].astype(jnp.int32)) for i in range(3)]
    q = spread(data_ref[3:4, columns] * (2.0 * COULOMB))
    w = spread(data_ref[4:5, columns] * (48.0 * LJ_DEPTH))
    return (*xyz, q, w)


def write_halo(data, lists_ref, low_ref, high_ref):
    lane = lax.broadcasted_iota(jnp.int32, (8, CLUSTER), 1)
    for row, out_ref in ((0, low_ref), (1, high_ref)):
        for k in range(HALO // CLUSTER):
            columns = slice(k * CLUSTER, (k + 1) * CLUSTER)
            index = jnp.broadcast_to(lists_ref[0, row : row + 1, columns] & (CLUSTER - 1), (8, CLUSTER))
            first = data[:, 2 * k * CLUSTER : (2 * k + 1) * CLUSTER]
            second = data[:, (2 * k + 1) * CLUSTER : (2 * k + 2) * CLUSTER]
            out_ref[:, columns] = jnp.where(
                lane < CLUSTER // 2,
                jnp.take_along_axis(first, index, axis=1, mode="promise_in_bounds"),
                jnp.take_along_axis(second, index, axis=1, mode="promise_in_bounds"),
            )


def spread_kernel(
    lam_ref, cells_hbm, off_hbm, vel_hbm, charge_hbm, coup_hbm, mass_hbm, lists_hbm, slab_hbm, flag_hbm,
    out_ref, data_ref, move_ref, low_ref, high_ref, ladder_ref, mixed_high, mixed_low,
    cells_ref, off_ref, vel_ref, charge_ref, coup_ref, mass_ref, lists_ref, slab_ref, flag_ref, arrived,
):
    copies = [
        pltpu.make_async_copy(source, target, arrived.at[i])
        for i, (source, target) in enumerate(
            (
                (cells_hbm, cells_ref), (off_hbm, off_ref), (vel_hbm, vel_ref), (charge_hbm, charge_ref),
                (coup_hbm, coup_ref), (mass_hbm, mass_ref), (lists_hbm, lists_ref), (slab_hbm, slab_ref),
                (flag_hbm, flag_ref),
            )
        )
    ]
    for copy in copies:
        copy.start()
    for copy in copies:
        copy.wait()
    weight = 1.0 - lam_ref[0] * coup_ref[...]
    charge = charge_ref[...] * weight

    for i in range(3):
        cell = cells_ref[i].astype(F32)
        move_ref[i : i + 1, :] = off_ref[i]
        move_ref[3 + i : 4 + i, :] = cell
        move_ref[8 + i : 9 + i, :] = vel_ref[i]
        data_ref[i : i + 1, :] = cell + off_ref[i]
    move_ref[6:8, :] = jnp.zeros((2, A_DEV), F32)
    move_ref[11:16, :] = jnp.zeros((5, A_DEV), F32)
    data_ref[3:4, :] = charge
    data_ref[4:5, :] = weight
    data_ref[5:6, :] = mass_ref[...]
    data_ref[6:8, :] = jnp.zeros((2, A_DEV), F32)
    write_halo(data_ref[...], lists_ref, low_ref, high_ref)

    off = move_ref[0:3, :]
    cells = [cells_ref[i] for i in range(3)]
    for i in range(3):
        ladder_ref[i] = cells[i]
    half = lax.broadcasted_iota(jnp.int32, (1, A_DEV), 1) < A_DEV // 2
    ladder_ref[3] = jnp.where(half, flag_ref[0:1, 0:1], flag_ref[0:1, 1:2])
    weights, _ = spline_set(off)
    row = iota_rows(16, A_DEV)
    plane = jnp.where(row < 8, row, 8 + (row & 3))
    x_table = chosen(plane - (cells[0] & 7), [m[0:1] for m in weights]) * charge
    z_table = chosen((iota_rows(MODES, A_DEV) - cells[2]) & (MODES - 1), [m[2:3] for m in weights])
    z_modes = jnp.dot(slab_ref[...], z_table, precision=HIGHEST, preferred_element_type=F32)
    y_table = chosen((iota_rows(K, A_DEV) - cells[1]) & (K - 1), [m[1:2] for m in weights])

    near, far = x_table[0:8], x_table[8:16]
    upper = iota_rows(8, A_DEV) < 4
    for i in range(0, N_DOM, 2):
        pieces = []
        for k in (i, i + 1):
            first = jnp.broadcast_to(z_modes[2 * k : 2 * k + 1], (8, A_DEV))
            second = jnp.broadcast_to(z_modes[2 * k + 1 : 2 * k + 2], (8, A_DEV))
            pieces += [near * first, near * second, far * jnp.where(upper, first, second)]
        high, low = split(jnp.concatenate(pieces, axis=0))
        mixed_high[i * SLAB : (i + 2) * SLAB, :] = high
        mixed_low[i * SLAB : (i + 2) * SLAB, :] = low
    out_ref[...] = dot3((mixed_high[...], mixed_low[...]), split(y_table), (((1,), (1,)), ((), ())))


def mesh_kernel(grid_ref, gain_ref, basis_ref, below_ref, above_ref, out_ref, block):
    del below_ref, above_ref
    top = iota_rows(8, K) < 4
    for e in range(N_DOM):
        spill = grid_ref[((e - 1) % N_DOM) * SLAB + 16 : ((e - 1) % N_DOM) * SLAB + 24, :]
        turned = pltpu.roll(spill, 4, 0)
        block[8 * e : 8 * e + 8, :] = grid_ref[e * SLAB : e * SLAB + 8, :] + jnp.where(top, spill, 0.0)
        block[K + 8 * e : K + 8 * e + 8, :] = grid_ref[e * SLAB + 8 : e * SLAB + 16, :] + jnp.where(top, turned, 0.0)
    basis = (basis_ref[0:K, :], basis_ref[K : 2 * K, :])
    turned_basis = (basis_ref[2 * K : 3 * K, :], basis_ref[3 * K : 4 * K, :])
    along_y = dot3(split(block[...]), turned_basis)
    for mode in range(2):
        part = split(along_y[mode * K : (mode + 1) * K])
        scaled = dot3(basis, part) * gain_ref[mode]
        block[mode * K : (mode + 1) * K, :] = dot3(turned_basis, split(scaled))
    block[...] = dot3(split(block[...]), basis)
    for e in range(N_DOM):
        following = 8 * ((e + 1) % N_DOM)
        out_ref[e * SLAB : e * SLAB + 8, :] = block[8 * e : 8 * e + 8, :]
        out_ref[e * SLAB + 8 : e * SLAB + 16, :] = block[K + 8 * e : K + 8 * e + 8, :]
        out_ref[e * SLAB + 16 : e * SLAB + 24, :] = jnp.where(
            top,
            block[following : following + 8, :],
            pltpu.roll(block[K + following : K + following + 8, :], 4, 0),
        )


def write_gain(mode_weights_ref, rows_ref, lanes_ref, gain_ref):
    dom = lax.axis_index("dom")
    square_y, factor_y = lanes_ref[0:1, :], lanes_ref[1:2, :]
    scale = COULOMB / (math.pi * K)
    first = dom
    second = jnp.where(dom == 0, MODES // 2, dom)

    def totals(square):
        one = jnp.zeros_like(square)
        two = jnp.zeros_like(square)
        for k in range(K // 2 + 1):
            whole = square + (k / K) ** 2
            inverse = 1.0 / whole if k else jnp.where(whole > 0.0, 1.0 / jnp.where(whole > 0.0, whole, 1.0), 0.0)
            one = one + inverse * mode_weights_ref[first, k]
            two = two + inverse * mode_weights_ref[second, k]
        return one, two

    def block(start):
        rows = pl.ds(start, 8)
        square = jnp.broadcast_to(rows_ref[rows, 0:1], (8, K)) + square_y
        factor = jnp.broadcast_to(rows_ref[rows, 1:2], (8, K)) * factor_y * scale
        one, two = totals(square)
        return one * factor, two * factor

    def step(b, carry):
        start = pl.multiple_of(b * 8, 8)
        one, two = block(start)
        gain_ref[0, pl.ds(start, 8), :] = one
        gain_ref[1, pl.ds(start, 8), :] = two
        gain_ref[0, pl.ds(start + K // 2, 8), :] = one
        gain_ref[1, pl.ds(start + K // 2, 8), :] = two
        return carry

    lax.fori_loop(0, 8, step, 0)
    one, two = block(K // 2)
    gain_ref[0, K // 2 : K // 2 + 1, :] = one[0:1]
    gain_ref[1, K // 2 : K // 2 + 1, :] = two[0:1]


def listed(tiles_ref, row, cluster):
    count = jnp.int32(0)
    for slot in range(1, 4):
        count = count + jnp.where(tiles_ref[slot, 0, row] == cluster, 1, 0)
    return count.astype(F32)


def own_forces(lam_ref, tiles_ref, data_ref, force_ref, turns, near, sides, first, last):
    turns[...] = fixed_turns(data_ref[0:3, :])
    near[...] = jnp.zeros_like(near)
    floor_value = SOFT_FLOOR + SOFT_SCALE * lam_ref[0]

    def one_cluster(b, carry):
        start = pl.multiple_of(b * CLUSTER, CLUSTER)
        lanes = pl.ds(start, CLUSTER)
        turned = jnp.concatenate([turns[:, lanes], data_ref[3:8, lanes]], axis=0).T
        others = [b, (b + 1) % CLUSTERS, (b + 2) % CLUSTERS]
        owns = [own_rows(data_ref, turns, pl.multiple_of(a * CLUSTER, CLUSTER)) for a in others]
        totals = [[jnp.zeros((8, CLUSTER), F32) for _ in range(3)] for _ in others]
        back = [None] + [listed(tiles_ref, b, a) for a in others[1:]]
        for chunk in range(CLUSTER // 8):
            part = turned[chunk * 8 : chunk * 8 + 8]
            other = [jnp.broadcast_to(part[:, i : i + 1], (8, CLUSTER)) for i in range(5)]
            other[:3] = [x.astype(jnp.int32) for x in other[:3]]
            side = []
            for j in range(3):
                terms = pair_terms(owns[j], other, floor_value)
                totals[j] = [p + q for p, q in zip(totals[j], terms)]
                if j:
                    side.append([back[j] * p for p in terms])
            for i in range(3):
                sides[i, pl.ds(pl.multiple_of(start + chunk * 8, 8), 8), :] = side[0][i] + side[1][i]
        for j, a in enumerate(others):
            rows = pl.ds(pl.multiple_of(a * 8, 8), 8)
            for i in range(3):
                total = listed(tiles_ref, a, b) * totals[j][i] if j else totals[j][i]
                near[i, rows, :] = near[i, rows, :] + total
        return carry

    lax.fori_loop(first, last, one_cluster, 0)
    force_ref[...] = jnp.zeros_like(force_ref)
    ones = jnp.ones((8, CLUSTER), BF16)
    for c in range(CLUSTERS):
        lanes = slice(c * CLUSTER, (c + 1) * CLUSTER)
        for i in range(3):
            force_ref[i : i + 1, lanes] = SPAN * jnp.sum(near[i, c * 8 : (c + 1) * 8, :], axis=0, keepdims=True)
    rows = slice(first * CLUSTER, last * CLUSTER)
    for i in range(3):
        rest = sides[i, rows, :]
        total = jnp.zeros((8, (last - first) * CLUSTER), F32)
        for _ in range(3):
            part = rest.astype(BF16)
            rest = rest - part.astype(F32)
            total = total + lax.dot_general(ones, part, (((1,), (1,)), ((), ())), preferred_element_type=F32)
        force_ref[i : i + 1, rows] = force_ref[i : i + 1, rows] - SPAN * total[0:1]


def own_kernel(lam_ref, tiles_ref, data_ref, force_ref, turns, near, sides):
    own_forces(lam_ref, tiles_ref, data_ref, force_ref, turns, near, sides, 0, CLUSTERS)


def gain_kernel(
    lam_ref, tiles_ref, weights_ref, data_ref, rows_ref, lanes_ref, force_ref, gain_ref, turns, near, sides
):
    write_gain(weights_ref, rows_ref, lanes_ref, gain_ref)
    own_forces(lam_ref, tiles_ref, data_ref, force_ref, turns, near, sides, 0, CLUSTERS // 2)


def add_halo_forces(lam_ref, data_ref, below_ref, above_ref, partial_ref, force_ref, turns):
    turns[...] = fixed_turns(data_ref[0:3, :])
    floor_value = SOFT_FLOOR + SOFT_SCALE * lam_ref[0]

    def one_pair(k, carry):
        start = pl.multiple_of(k * CLUSTER, CLUSTER)
        starts = [pl.multiple_of(k * (2 * CLUSTER), CLUSTER), pl.multiple_of(k * (2 * CLUSTER) + CLUSTER, CLUSTER)]
        owns = [own_rows(data_ref, turns, s) for s in starts]
        totals = [[jnp.zeros((8, CLUSTER), F32) for _ in range(3)] for _ in range(2)]
        for source in (below_ref, above_ref):
            block = source[:, pl.ds(start, CLUSTER)]
            stack = jnp.where(iota_rows(8, CLUSTER) < 3, fixed_turns(block), block)
            turned = stack.T
            for chunk in range(CLUSTER // 8):
                part = turned[chunk * 8 : chunk * 8 + 8]
                other = [jnp.broadcast_to(part[:, i : i + 1], (8, CLUSTER)) for i in range(5)]
                other[:3] = [x.astype(jnp.int32) for x in other[:3]]
                for j in range(2):
                    terms = pair_terms(owns[j], other, floor_value)
                    totals[j] = [a + b for a, b in zip(totals[j], terms)]
        for j in range(2):
            lanes = pl.ds(starts[j], CLUSTER)
            for i in range(3):
                force_ref[i : i + 1, lanes] = partial_ref[i : i + 1, lanes] + SPAN * jnp.sum(
                    totals[j][i], axis=0, keepdims=True
                )
        return carry

    lax.fori_loop(0, HALO // CLUSTER, one_pair, 0)


def rest_kernel(
    lam_ref, tiles_ref, data_ref, below_ref, above_ref, partial_ref, force_ref, turns, near, sides, second
):
    own_forces(lam_ref, tiles_ref, data_ref, second, turns, near, sides, CLUSTERS // 2, CLUSTERS)
    second[...] = second[...] + partial_ref[...]
    force_ref[...] = jnp.zeros_like(force_ref)
    add_halo_forces(lam_ref, data_ref, below_ref, above_ref, second, force_ref, turns)


def advance(force, kicks, data_ref, move_ref, lists_ref, data_out, move_out, low_ref, high_ref, off_ref=None):
    mass = data_ref[5:6, :]
    velocity = move_ref[8:11, :]
    for _ in range(kicks):
        velocity = velocity + 0.5 * STEP_DT * force * mass
    off = move_ref[0:3, :] + STEP_DT * velocity
    move_out[...] = move_ref[...]
    move_out[0:3, :] = off
    move_out[8:11, :] = velocity
    data_out[...] = data_ref[...]
    data_out[0:3, :] = move_ref[3:6, :] + off
    if off_ref is not None:
        for i in range(3):
            off_ref[i] = off[i : i + 1]
    write_halo(data_out[...], lists_ref, low_ref, high_ref)


def gather_kernel(
    pot_ref, data_ref, move_ref, short_ref, lists_ref, slab_ref,
    long_ref, data_out, move_out, low_ref, high_ref, force,
):
    off = move_ref[0:3, :]
    cells = move_ref[3:6, :].astype(jnp.int32)
    charge = data_ref[3:4, :]
    weights, slopes = spline_set(off)
    row = iota_rows(16, A_DEV)
    reach = jnp.where(row < 8, row, 8 + (row & 3)) - (cells[0:1] & 7)
    x_table = chosen(reach, [m[0:1] for m in weights])
    x_slope = chosen(reach, [m[0:1] for m in slopes])
    reach = (iota_rows(MODES, A_DEV) - cells[2:3]) & (MODES - 1)
    z_table = chosen(reach, [m[2:3] for m in weights])
    z_slope = chosen(reach, [m[2:3] for m in slopes])
    z_modes = jnp.dot(slab_ref[...], z_table, precision=HIGHEST, preferred_element_type=F32)
    z_tilts = jnp.dot(slab_ref[...], z_slope, precision=HIGHEST, preferred_element_type=F32)
    potential = split(pot_ref[...])
    upper = iota_rows(8, CLUSTER) < 4
    for c in range(CLUSTERS):
        lanes = slice(c * CLUSTER, (c + 1) * CLUSTER)
        reach = (iota_rows(K, CLUSTER) - cells[1:2, lanes]) & (K - 1)
        y_both = jnp.concatenate(
            [chosen(reach, [m[1:2, lanes] for m in weights]), chosen(reach, [m[1:2, lanes] for m in slopes])], axis=1
        )
        along = dot3(potential, split(y_both))
        value, tilt = along[:, :CLUSTER], along[:, CLUSTER:]
        sums = [[jnp.zeros((8, CLUSTER), F32) for _ in range(2)] for _ in range(3)]
        for i in range(N_DOM):
            pairs = []
            for table in (z_modes, z_tilts):
                first = jnp.broadcast_to(table[2 * i : 2 * i + 1, lanes], (8, CLUSTER))
                second = jnp.broadcast_to(table[2 * i + 1 : 2 * i + 2, lanes], (8, CLUSTER))
                pairs.append((first, second, jnp.where(upper, first, second)))
            for which, (source, table) in enumerate(((value, 0), (tilt, 0), (value, 1))):
                block = source[i * SLAB : (i + 1) * SLAB]
                first, second, mixed = pairs[table]
                sums[which][0] = sums[which][0] + (first * block[0:8] + second * block[8:16])
                sums[which][1] = sums[which][1] + mixed * block[16:24]
        for i in range(3):
            table = x_slope if i == 0 else x_table
            near = table[0:8, lanes] * sums[i][0] + table[8:16, lanes] * sums[i][1]
            force[i : i + 1, lanes] = -charge[:, lanes] * jnp.sum(near, axis=0, keepdims=True)
    long_ref[...] = jnp.zeros_like(long_ref)
    long_ref[0:3, :] = force[0:3, :]
    advance(
        short_ref[0:3, :] + force[0:3, :], 1, data_ref, move_ref, lists_ref, data_out, move_out, low_ref, high_ref
    )


def halo_step_kernel(
    lam_ref, data_ref, below_ref, above_ref, partial_ref, long_ref, move_ref, lists_ref, ladder_ref,
    data_out, move_out, low_ref, high_ref, off_ref, turns, force,
):
    del ladder_ref
    add_halo_forces(lam_ref, data_ref, below_ref, above_ref, partial_ref, force, turns)
    total = force[0:3, :] + long_ref[0:3, :]
    advance(total, 2, data_ref, move_ref, lists_ref, data_out, move_out, low_ref, high_ref, off_ref)


def halo_last_kernel(
    lam_ref, data_ref, below_ref, above_ref, partial_ref, long_ref, move_ref, offsets_ref, velocity_ref, turns, force
):
    del offsets_ref
    add_halo_forces(lam_ref, data_ref, below_ref, above_ref, partial_ref, force, turns)
    total = force[0:3, :] + long_ref[0:3, :]
    velocity = move_ref[8:11, :] + 0.5 * STEP_DT * total * data_ref[5:6, :]
    for i in range(3):
        velocity_ref[i] = velocity[i : i + 1]


def settle_kernel(ladder_ref, offsets_ref, vel_hbm, cells_ref, off_ref, vel_ref, arrived, done):
    window = lax.axis_index("lam")
    windows = lax.axis_size("lam")

    def partner(w, round_index):
        low = jnp.where(w % 2 == round_index % 2, w, w - 1)
        inside = jnp.logical_and(low >= 0, low + 1 < windows)
        flag = jnp.max(ladder_ref[jnp.maximum(low, 0), 3, :, round_index * (A_DEV // 2) : (round_index + 1) * (A_DEV // 2)])
        return jnp.where(jnp.logical_and(inside, flag == 1), 2 * low + 1 - w, w)

    source = partner(partner(window, 1), 0)
    copy = pltpu.make_async_copy(vel_hbm.at[source], arrived, done)
    copy.start()
    for i in range(3):
        cells_ref[i] = ladder_ref[source, i]
        off_ref[i] = offsets_ref[source, i]
    copy.wait()
    vel_ref[...] = arrived[...]


PLACES = {
    "s": pl.BlockSpec(memory_space=pltpu.SMEM),
    "v": pl.BlockSpec(memory_space=pltpu.VMEM),
    "a": pl.BlockSpec(memory_space=pl.ANY),
}


def call(kernel, ins, outs, scratch=(), cost=0, limit=40):
    return pl.pallas_call(
        kernel,
        out_shape=[jax.ShapeDtypeStruct(shape, dtype) for shape, dtype in outs],
        in_specs=[PLACES[place] for place, _ in ins],
        out_specs=[PLACES["v"]] * len(outs),
        scratch_shapes=list(scratch),
        compiler_params=pltpu.CompilerParams(vmem_limit_bytes=limit * 2**20),
        cost_estimate=pl.CostEstimate(flops=cost, bytes_accessed=200000, transcendentals=0),
    )(*[value for _, value in ins])


def neighbours(low, high):
    size = lax.axis_size("dom")
    below = lax.ppermute(high, "dom", [(i, (i + 1) % size) for i in range(size)])
    above = lax.ppermute(low, "dom", [(i, (i - 1) % size) for i in range(size)])
    return below, above


def exchanged(value):
    return lax.all_to_all(value, "dom", split_axis=0, concat_axis=0, tiled=True)


def body(
    cells, offsets, velocities, charges, coupling, inverse_mass, lambdas, tile_lists, halo_lists, accept_flags
):
    wide = ((8, A_DEV), F32)
    moving = ((16, A_DEV), F32)
    border = ((8, HALO), F32)
    turns = pltpu.VMEM((3, A_DEV), F32)
    pair_scratch = [turns, pltpu.VMEM((3, CLUSTERS * 8, CLUSTER), F32), pltpu.VMEM((3, A_DEV, CLUSTER), F32)]
    spare = pltpu.VMEM((8, A_DEV), F32)
    tiles = jnp.transpose(tile_lists, (2, 0, 1))
    slab = jnp.asarray(slab_basis())
    square, factor = plane_gain()
    gain_rows = np.zeros((K, 8), np.float32)
    gain_rows[:, 0], gain_rows[:, 1] = square, factor
    gain_lanes = np.zeros((8, K), np.float32)
    gain_lanes[0], gain_lanes[1] = square, factor

    triple = (3, 1, A_DEV)

    def by_row(x):
        return jnp.transpose(x, (1, 0, 2))

    def everywhere(x):
        return lax.all_gather(x, "lam", axis=0, tiled=False)


    grid, data, move, low, high, ladder = call(
        spread_kernel,
        [
            ("s", lambdas), ("a", by_row(cells)), ("a", by_row(offsets)), ("a", by_row(velocities)),
            ("a", charges[None]), ("a", coupling[None]), ("a", inverse_mass[None]), ("a", halo_lists), ("a", slab),
            ("a", accept_flags.T),
        ],
        [((ROWS, K), F32), wide, moving, border, border, ((4, 1, A_DEV), jnp.int32)],
        [
            pltpu.VMEM((ROWS, A_DEV), BF16), pltpu.VMEM((ROWS, A_DEV), BF16),
            pltpu.VMEM((3, 1, A_DEV), jnp.int32), pltpu.VMEM((3, 1, A_DEV), F32), pltpu.VMEM((3, 1, A_DEV), F32),
            pltpu.VMEM((1, A_DEV), F32), pltpu.VMEM((1, A_DEV), F32), pltpu.VMEM((1, A_DEV), F32),
            pltpu.VMEM((1, 2, HALO), jnp.int32), pltpu.VMEM((MODES, MODES), F32), pltpu.VMEM((1, 2), jnp.int32),
            pltpu.SemaphoreType.DMA((9,)),
        ],
        limit=60,
    )
    ladder = everywhere(ladder)
    grid = exchanged(grid)
    below, above = neighbours(low, high)
    short, gain = call(
        gain_kernel,
        [
            ("s", lambdas), ("s", tiles), ("s", jnp.asarray(slab_weights())), ("v", data),
            ("v", jnp.asarray(gain_rows)), ("v", jnp.asarray(gain_lanes)),
        ],
        [wide, ((2, K, K), F32)],
        pair_scratch,
        cost=2 * 10**9,
    )
    (potential,) = call(
        mesh_kernel,
        [("v", grid), ("v", gain), ("v", jnp.asarray(basis_table())), ("a", below), ("a", above)],
        [((ROWS, K), F32)],
        [pltpu.VMEM((2 * K, K), F32)],
    )
    potential = exchanged(potential)
    (short,) = call(
        rest_kernel,
        [("s", lambdas), ("s", tiles), ("v", data), ("v", below), ("v", above), ("v", short)],
        [wide],
        [*pair_scratch, spare],
        cost=2 * 10**9,
    )
    far, data, move, low, high = call(
        gather_kernel,
        [("v", potential), ("v", data), ("v", move), ("v", short), ("v", halo_lists), ("v", slab)],
        [wide, wide, moving, border, border],
        [spare],
    )

    def own_call(data):
        (partial,) = call(
            own_kernel, [("s", lambdas), ("s", tiles), ("v", data)], [wide], pair_scratch, cost=2 * 10**9
        )
        return partial

    below, above = neighbours(low, high)
    short = own_call(data)
    data, move, low, high, offset = call(
        halo_step_kernel,
        [
            ("s", lambdas), ("v", data), ("v", below), ("v", above), ("v", short), ("v", far), ("v", move),
            ("v", halo_lists), ("a", ladder),
        ],
        [wide, moving, border, border, (triple, F32)],
        [turns, spare],
    )
    all_offsets = everywhere(offset)
    below, above = neighbours(low, high)
    short = own_call(data)
    (velocity,) = call(
        halo_last_kernel,
        [
            ("s", lambdas), ("v", data), ("v", below), ("v", above), ("v", short), ("v", far), ("v", move),
            ("a", all_offsets),
        ],
        [(triple, F32)],
        [turns, spare],
    )
    out = call(
        settle_kernel,
        [("v", ladder), ("v", all_offsets), ("a", everywhere(velocity))],
        [(triple, jnp.int32), (triple, F32), (triple, F32)],
        [pltpu.VMEM(triple, F32), pltpu.SemaphoreType.DMA],
        limit=60,
    )
    return tuple(by_row(x) for x in out)


def solution(mesh):
    in_specs = (
        P("lam", None, "dom"),
        P("lam", None, "dom"),
        P("lam", None, "dom"),
        P("dom"),
        P("dom"),
        P("dom"),
        P("lam"),
        P("lam", "dom", None),
        P("lam", "dom", None),
        P(None, "lam"),
    )
    out_specs = (P("lam", None, "dom"), P("lam", None, "dom"), P("lam", None, "dom"))
    return jax.shard_map(body, mesh=mesh, in_specs=in_specs, out_specs=out_specs, check_vma=False)
```

```python
import functools
import math

import jax
import jax.numpy as jnp
import ml_dtypes
import numpy as np
from jax import lax
from jax.experimental import pallas as pl
from jax.experimental.pallas import tpu as pltpu
from jax.sharding import PartitionSpec as P

K = 128
CLUSTER = 128
N_DOM = 16
A_DEV = 1024
CLUSTERS = 8
HALO = 512
MODES = 32
SLAB = 24
ROWS = N_DOM * SLAB

EWALD_BETA = 0.5
COULOMB = 20.0
LJ_DEPTH = 1.0
LJ_SIGMA_SQ = 0.49
SOFT_SCALE = 0.5
SOFT_FLOOR = 0.5
STEP_DT = 0.25

F32 = jnp.float32
BF16 = jnp.bfloat16
HIGHEST = lax.Precision.HIGHEST

TURN = 2.0**32
SPAN_SQ = 2.0**-50
SPAN = 2.0**-25

SCREEN = (
    -0.0818439527,
    0.648023047,
    -2.23331568,
    4.38709699,
    -5.37737017,
    4.16223694,
    -1.81397109,
    0.0540053844,
    0.5630337,
    -5.2346482e-05,
    0.282096019,
)


def real_basis(count):
    half = count // 2
    place = np.arange(count)
    rows = []
    for k in range(half + 1):
        scale = math.sqrt((1.0 if k in (0, half) else 2.0) / count)
        rows.append(scale * np.cos(2.0 * np.pi * (k * place % count) / count))
    for k in range(1, half):
        rows.append(math.sqrt(2.0 / count) * np.sin(2.0 * np.pi * (k * place % count) / count))
    return np.stack(rows)


def halves(table):
    high = table.astype(np.float32).astype(ml_dtypes.bfloat16)
    low = (table - high.astype(np.float64)).astype(np.float32).astype(ml_dtypes.bfloat16)
    return high, low


def basis_table():
    basis = real_basis(K)
    high, low = halves(basis)
    return np.concatenate([high, low, high.T, low.T], axis=0)


def slab_basis():
    basis = real_basis(MODES)
    order = [0, MODES // 2]
    for k in range(1, MODES // 2):
        order += [k, MODES // 2 + k]
    return basis[np.array(order)].astype(np.float32)


def spline_modulus(k):
    return (3.0 / (2.0 + np.cos(2.0 * np.pi * k / K))) ** 2


def slab_weights():
    k = np.arange(K // 2 + 1)
    delta = np.arange(-MODES // 2 + 1, MODES // 2 + 1)
    folded = np.where((k == 0) | (k == K // 2), 1.0, 2.0)
    own = folded * np.exp(-np.pi**2 * (k / K) ** 2 / EWALD_BETA**2) * spline_modulus(k)
    rows = []
    for j in range(MODES // 2 + 1):
        window = np.cos(2 * np.pi * k[:, None] * delta / K) * np.cos(2 * np.pi * j * delta / MODES)
        rows.append(own * window.sum(axis=1))
    return np.stack(rows).astype(np.float32)


def plane_gain():
    k = np.concatenate([np.arange(K // 2 + 1), np.arange(1, K // 2)])
    square = (k / K) ** 2
    factor = np.exp(-np.pi**2 * square / EWALD_BETA**2) * spline_modulus(k)
    return square.astype(np.float32), factor.astype(np.float32)


def split(x):
    high = x.astype(BF16)
    return high, (x - high.astype(F32)).astype(BF16)


def dot3(left, right, dims=(((1,), (0,)), ((), ()))):
    lh, ll = left
    rh, rl = right
    dot = functools.partial(lax.dot_general, dimension_numbers=dims, preferred_element_type=F32)
    return dot(lh, rh) + (dot(lh, rl) + dot(ll, rh))


def spline_set(u):
    v = 1.0 - u
    u2 = u * u
    u3 = u2 * u
    weights = (
        v * v * v / 6.0,
        (3.0 * u3 - 6.0 * u2 + 4.0) / 6.0,
        (-3.0 * u3 + 3.0 * u2 + 3.0 * u + 1.0) / 6.0,
        u3 / 6.0,
    )
    slopes = (-0.5 * v * v, 1.5 * u2 - 2.0 * u, -1.5 * u2 + u + 0.5, 0.5 * u2)
    return weights, slopes


def chosen(distance, rows):
    out = jnp.where(distance == 3, rows[3], 0.0)
    for k in (2, 1, 0):
        out = jnp.where(distance == k, rows[k], out)
    return out


def iota_rows(rows, columns):
    return lax.broadcasted_iota(jnp.int32, (rows, columns), 0)


def fixed_turns(x):
    t = x * (1.0 / K)
    f = t - jnp.floor(t + 0.5)
    return jnp.maximum(f, -0.5) * TURN


def pair_terms(own, other, floor_value):
    ax, ay, az, qa, wa = own
    bx, by, bz, qb, wb = other
    dx = (ax - bx).astype(F32)
    dy = (ay - by).astype(F32)
    dz = (az - bz).astype(F32)
    s = (dx * dx + dy * dy + dz * dz) * SPAN_SQ + floor_value
    w = lax.rsqrt(s)
    u = w * w
    screen = jnp.full_like(w, SCREEN[0])
    for c in SCREEN[1:]:
        screen = screen * w + c
    gauss = jnp.exp2(s * (-(EWALD_BETA**2) * math.log2(math.e)))
    t = u * u * u
    g = u * ((qa * qb) * (gauss * screen) + (wa * wb) * (t * (t - 0.5 / LJ_SIGMA_SQ**3)))
    return g * dx, g * dy, g * dz


def own_rows(data_ref, turns, start, rows=8):
    def spread(row):
        return jnp.broadcast_to(row, (rows, CLUSTER))

    columns = pl.ds(start, CLUSTER)
    xyz = [spread(turns[i : i + 1, columns].astype(jnp.int32)) for i in range(3)]
    q = spread(data_ref[3:4, columns] * (2.0 * COULOMB))
    w = spread(data_ref[4:5, columns] * (48.0 * LJ_DEPTH * LJ_SIGMA_SQ**6))
    return (*xyz, q, w)


def write_halo(data, lists_ref, low_ref, high_ref):
    lane = lax.broadcasted_iota(jnp.int32, (8, CLUSTER), 1)
    for row, out_ref in ((0, low_ref), (1, high_ref)):
        for k in range(HALO // CLUSTER):
            columns = slice(k * CLUSTER, (k + 1) * CLUSTER)
            index = jnp.broadcast_to(lists_ref[0, row : row + 1, columns] & (CLUSTER - 1), (8, CLUSTER))
            first = data[:, 2 * k * CLUSTER : (2 * k + 1) * CLUSTER]
            second = data[:, (2 * k + 1) * CLUSTER : (2 * k + 2) * CLUSTER]
            out_ref[:, columns] = jnp.where(
                lane < CLUSTER // 2,
                jnp.take_along_axis(first, index, axis=1, mode="promise_in_bounds"),
                jnp.take_along_axis(second, index, axis=1, mode="promise_in_bounds"),
            )


def spread_kernel(
    lam_ref, cells_hbm, off_hbm, vel_hbm, charge_hbm, coup_hbm, mass_hbm, lists_hbm, slab_hbm, flag_hbm,
    out_ref, data_ref, move_ref, low_ref, high_ref, mixed_high, mixed_low,
    cells_ref, off_ref, vel_ref, charge_ref, coup_ref, mass_ref, lists_ref, slab_ref, flag_ref, arrived,
):
    copies = [
        pltpu.make_async_copy(source, target, arrived.at[i])
        for i, (source, target) in enumerate(
            (
                (cells_hbm, cells_ref), (off_hbm, off_ref), (vel_hbm, vel_ref), (charge_hbm, charge_ref),
                (coup_hbm, coup_ref), (mass_hbm, mass_ref), (lists_hbm, lists_ref), (slab_hbm, slab_ref),
                (flag_hbm, flag_ref),
            )
        )
    ]
    for copy in copies:
        copy.start()
    for copy in copies:
        copy.wait()
    weight = 1.0 - lam_ref[0] * coup_ref[...]
    charge = charge_ref[...] * weight

    for i in range(3):
        cell = cells_ref[i].astype(F32)
        move_ref[i : i + 1, :] = off_ref[i]
        move_ref[3 + i : 4 + i, :] = cell
        move_ref[8 + i : 9 + i, :] = vel_ref[i]
        data_ref[i : i + 1, :] = cell + off_ref[i]
    move_ref[6:7, :] = jnp.broadcast_to(flag_ref[0:1, 0:1].astype(F32), (1, A_DEV))
    move_ref[7:8, :] = jnp.broadcast_to(flag_ref[0:1, 1:2].astype(F32), (1, A_DEV))
    move_ref[11:16, :] = jnp.zeros((5, A_DEV), F32)
    data_ref[3:4, :] = charge
    data_ref[4:5, :] = weight
    data_ref[5:6, :] = mass_ref[...]
    data_ref[6:8, :] = jnp.zeros((2, A_DEV), F32)
    write_halo(data_ref[...], lists_ref, low_ref, high_ref)

    off = move_ref[0:3, :]
    cells = [cells_ref[i] for i in range(3)]
    weights, _ = spline_set(off)
    row = iota_rows(16, A_DEV)
    plane = jnp.where(row < 8, row, 8 + (row & 3))
    x_table = chosen(plane - (cells[0] & 7), [m[0:1] for m in weights]) * charge
    z_table = chosen((iota_rows(MODES, A_DEV) - cells[2]) & (MODES - 1), [m[2:3] for m in weights])
    z_modes = jnp.dot(slab_ref[...], z_table, precision=HIGHEST, preferred_element_type=F32)
    y_table = chosen((iota_rows(K, A_DEV) - cells[1]) & (K - 1), [m[1:2] for m in weights])

    near, far = x_table[0:8], x_table[8:16]
    upper = iota_rows(8, A_DEV) < 4
    for i in range(0, N_DOM, 2):
        pieces = []
        for k in (i, i + 1):
            first = jnp.broadcast_to(z_modes[2 * k : 2 * k + 1], (8, A_DEV))
            second = jnp.broadcast_to(z_modes[2 * k + 1 : 2 * k + 2], (8, A_DEV))
            pieces += [near * first, near * second, far * jnp.where(upper, first, second)]
        high, low = split(jnp.concatenate(pieces, axis=0))
        mixed_high[i * SLAB : (i + 2) * SLAB, :] = high
        mixed_low[i * SLAB : (i + 2) * SLAB, :] = low
    out_ref[...] = dot3((mixed_high[...], mixed_low[...]), split(y_table), (((1,), (1,)), ((), ())))


def mesh_kernel(grid_ref, gain_ref, basis_ref, below_ref, above_ref, out_ref, block):
    del below_ref, above_ref
    top = iota_rows(8, K) < 4
    for e in range(N_DOM):
        spill = grid_ref[((e - 1) % N_DOM) * SLAB + 16 : ((e - 1) % N_DOM) * SLAB + 24, :]
        turned = pltpu.roll(spill, 4, 0)
        block[8 * e : 8 * e + 8, :] = grid_ref[e * SLAB : e * SLAB + 8, :] + jnp.where(top, spill, 0.0)
        block[K + 8 * e : K + 8 * e + 8, :] = grid_ref[e * SLAB + 8 : e * SLAB + 16, :] + jnp.where(top, turned, 0.0)
    basis = (basis_ref[0:K, :], basis_ref[K : 2 * K, :])
    turned_basis = (basis_ref[2 * K : 3 * K, :], basis_ref[3 * K : 4 * K, :])
    along_y = dot3(split(block[...]), turned_basis)
    for mode in range(2):
        part = split(along_y[mode * K : (mode + 1) * K])
        scaled = dot3(basis, part) * gain_ref[mode]
        block[mode * K : (mode + 1) * K, :] = dot3(turned_basis, split(scaled))
    block[...] = dot3(split(block[...]), basis)
    for e in range(N_DOM):
        following = 8 * ((e + 1) % N_DOM)
        out_ref[e * SLAB : e * SLAB + 8, :] = block[8 * e : 8 * e + 8, :]
        out_ref[e * SLAB + 8 : e * SLAB + 16, :] = block[K + 8 * e : K + 8 * e + 8, :]
        out_ref[e * SLAB + 16 : e * SLAB + 24, :] = jnp.where(
            top,
            block[following : following + 8, :],
            pltpu.roll(block[K + following : K + following + 8, :], 4, 0),
        )


def write_gain(mode_weights_ref, rows_ref, lanes_ref, gain_ref):
    dom = lax.axis_index("dom")
    square_y, factor_y = lanes_ref[0:1, :], lanes_ref[1:2, :]
    scale = COULOMB / (math.pi * K)
    first = dom
    second = jnp.where(dom == 0, MODES // 2, dom)

    def totals(square):
        one = jnp.zeros_like(square)
        two = jnp.zeros_like(square)
        for k in range(K // 2 + 1):
            whole = square + (k / K) ** 2
            inverse = 1.0 / whole if k else jnp.where(whole > 0.0, 1.0 / jnp.where(whole > 0.0, whole, 1.0), 0.0)
            one = one + inverse * mode_weights_ref[first, k]
            two = two + inverse * mode_weights_ref[second, k]
        return one, two

    def block(start):
        rows = pl.ds(start, 8)
        square = jnp.broadcast_to(rows_ref[rows, 0:1], (8, K)) + square_y
        factor = jnp.broadcast_to(rows_ref[rows, 1:2], (8, K)) * factor_y * scale
        one, two = totals(square)
        return one * factor, two * factor

    def step(b, carry):
        start = pl.multiple_of(b * 8, 8)
        one, two = block(start)
        gain_ref[0, pl.ds(start, 8), :] = one
        gain_ref[1, pl.ds(start, 8), :] = two
        gain_ref[0, pl.ds(start + K // 2, 8), :] = one
        gain_ref[1, pl.ds(start + K // 2, 8), :] = two
        return carry

    lax.fori_loop(0, 8, step, 0)
    one, two = block(K // 2)
    gain_ref[0, K // 2 : K // 2 + 1, :] = one[0:1]
    gain_ref[1, K // 2 : K // 2 + 1, :] = two[0:1]


def listed(tiles_ref, row, cluster):
    count = jnp.int32(0)
    for slot in range(1, 4):
        count = count + jnp.where(tiles_ref[slot, 0, row] == cluster, 1, 0)
    return count.astype(F32)


def own_forces(lam_ref, tiles_ref, data_ref, force_ref, turns, near, sides, first, last):
    turns[...] = fixed_turns(data_ref[0:3, :])
    near[...] = jnp.zeros_like(near)
    floor_value = SOFT_FLOOR + SOFT_SCALE * lam_ref[0]

    def one_cluster(b, carry):
        start = pl.multiple_of(b * CLUSTER, CLUSTER)
        lanes = pl.ds(start, CLUSTER)
        turned = jnp.concatenate([turns[:, lanes], data_ref[3:8, lanes]], axis=0).T
        others = [b, (b + 1) % CLUSTERS, (b + 2) % CLUSTERS]
        owns = [own_rows(data_ref, turns, pl.multiple_of(a * CLUSTER, CLUSTER)) for a in others]
        totals = [[jnp.zeros((8, CLUSTER), F32) for _ in range(3)] for _ in others]
        back = [None] + [listed(tiles_ref, b, a) for a in others[1:]]
        for chunk in range(CLUSTER // 8):
            part = turned[chunk * 8 : chunk * 8 + 8]
            other = [jnp.broadcast_to(part[:, i : i + 1], (8, CLUSTER)) for i in range(5)]
            other[:3] = [x.astype(jnp.int32) for x in other[:3]]
            side = []
            for j in range(3):
                terms = pair_terms(owns[j], other, floor_value)
                totals[j] = [p + q for p, q in zip(totals[j], terms)]
                if j:
                    side.append([back[j] * p for p in terms])
            for i in range(3):
                sides[i, pl.ds(pl.multiple_of(start + chunk * 8, 8), 8), :] = side[0][i] + side[1][i]
        for j, a in enumerate(others):
            rows = pl.ds(pl.multiple_of(a * 8, 8), 8)
            for i in range(3):
                total = listed(tiles_ref, a, b) * totals[j][i] if j else totals[j][i]
                near[i, rows, :] = near[i, rows, :] + total
        return carry

    lax.fori_loop(first, last, one_cluster, 0)
    force_ref[...] = jnp.zeros_like(force_ref)
    ones = jnp.ones((8, CLUSTER), BF16)
    for c in range(CLUSTERS):
        lanes = slice(c * CLUSTER, (c + 1) * CLUSTER)
        for i in range(3):
            force_ref[i : i + 1, lanes] = SPAN * jnp.sum(near[i, c * 8 : (c + 1) * 8, :], axis=0, keepdims=True)
    rows = slice(first * CLUSTER, last * CLUSTER)
    for i in range(3):
        rest = sides[i, rows, :]
        total = jnp.zeros((8, (last - first) * CLUSTER), F32)
        for _ in range(3):
            part = rest.astype(BF16)
            rest = rest - part.astype(F32)
            total = total + lax.dot_general(ones, part, (((1,), (1,)), ((), ())), preferred_element_type=F32)
        force_ref[i : i + 1, rows] = force_ref[i : i + 1, rows] - SPAN * total[0:1]


def own_kernel(lam_ref, tiles_ref, data_ref, force_ref, turns, near, sides):
    own_forces(lam_ref, tiles_ref, data_ref, force_ref, turns, near, sides, 0, CLUSTERS)


def gain_kernel(
    lam_ref, tiles_ref, weights_ref, data_ref, rows_ref, lanes_ref, force_ref, gain_ref, turns, near, sides
):
    write_gain(weights_ref, rows_ref, lanes_ref, gain_ref)
    own_forces(lam_ref, tiles_ref, data_ref, force_ref, turns, near, sides, 0, CLUSTERS // 2)


def add_halo_forces(lam_ref, data_ref, below_ref, above_ref, partial_ref, force_ref, turns):
    turns[...] = fixed_turns(data_ref[0:3, :])
    floor_value = SOFT_FLOOR + SOFT_SCALE * lam_ref[0]

    def one_pair(k, carry):
        start = pl.multiple_of(k * CLUSTER, CLUSTER)
        starts = [pl.multiple_of(k * (2 * CLUSTER), CLUSTER), pl.multiple_of(k * (2 * CLUSTER) + CLUSTER, CLUSTER)]
        owns = [own_rows(data_ref, turns, s) for s in starts]
        totals = [[jnp.zeros((8, CLUSTER), F32) for _ in range(3)] for _ in range(2)]
        for source in (below_ref, above_ref):
            block = source[:, pl.ds(start, CLUSTER)]
            stack = jnp.where(iota_rows(8, CLUSTER) < 3, fixed_turns(block), block)
            turned = stack.T
            for chunk in range(CLUSTER // 8):
                part = turned[chunk * 8 : chunk * 8 + 8]
                other = [jnp.broadcast_to(part[:, i : i + 1], (8, CLUSTER)) for i in range(5)]
                other[:3] = [x.astype(jnp.int32) for x in other[:3]]
                for j in range(2):
                    terms = pair_terms(owns[j], other, floor_value)
                    totals[j] = [a + b for a, b in zip(totals[j], terms)]
        for j in range(2):
            lanes = pl.ds(starts[j], CLUSTER)
            for i in range(3):
                force_ref[i : i + 1, lanes] = partial_ref[i : i + 1, lanes] + SPAN * jnp.sum(
                    totals[j][i], axis=0, keepdims=True
                )
        return carry

    lax.fori_loop(0, HALO // CLUSTER, one_pair, 0)


def rest_kernel(
    lam_ref, tiles_ref, data_ref, below_ref, above_ref, partial_ref, force_ref, turns, near, sides, second
):
    own_forces(lam_ref, tiles_ref, data_ref, second, turns, near, sides, CLUSTERS // 2, CLUSTERS)
    second[...] = second[...] + partial_ref[...]
    force_ref[...] = jnp.zeros_like(force_ref)
    add_halo_forces(lam_ref, data_ref, below_ref, above_ref, second, force_ref, turns)


def advance(force, kicks, data_ref, move_ref, lists_ref, data_out, move_out, low_ref, high_ref):
    mass = data_ref[5:6, :]
    velocity = move_ref[8:11, :]
    for _ in range(kicks):
        velocity = velocity + 0.5 * STEP_DT * force * mass
    off = move_ref[0:3, :] + STEP_DT * velocity
    move_out[...] = move_ref[...]
    move_out[0:3, :] = off
    move_out[8:11, :] = velocity
    data_out[...] = data_ref[...]
    data_out[0:3, :] = move_ref[3:6, :] + off
    write_halo(data_out[...], lists_ref, low_ref, high_ref)


def gather_kernel(
    pot_ref, data_ref, move_ref, short_ref, lists_ref, slab_ref,
    long_ref, data_out, move_out, low_ref, high_ref, force,
):
    off = move_ref[0:3, :]
    cells = move_ref[3:6, :].astype(jnp.int32)
    charge = data_ref[3:4, :]
    weights, slopes = spline_set(off)
    row = iota_rows(16, A_DEV)
    reach = jnp.where(row < 8, row, 8 + (row & 3)) - (cells[0:1] & 7)
    x_table = chosen(reach, [m[0:1] for m in weights])
    x_slope = chosen(reach, [m[0:1] for m in slopes])
    reach = (iota_rows(MODES, A_DEV) - cells[2:3]) & (MODES - 1)
    z_table = chosen(reach, [m[2:3] for m in weights])
    z_slope = chosen(reach, [m[2:3] for m in slopes])
    z_modes = jnp.dot(slab_ref[...], z_table, precision=HIGHEST, preferred_element_type=F32)
    z_tilts = jnp.dot(slab_ref[...], z_slope, precision=HIGHEST, preferred_element_type=F32)
    potential = split(pot_ref[...])
    upper = iota_rows(8, CLUSTER) < 4
    for c in range(CLUSTERS):
        lanes = slice(c * CLUSTER, (c + 1) * CLUSTER)
        reach = (iota_rows(K, CLUSTER) - cells[1:2, lanes]) & (K - 1)
        y_both = jnp.concatenate(
            [chosen(reach, [m[1:2, lanes] for m in weights]), chosen(reach, [m[1:2, lanes] for m in slopes])], axis=1
        )
        along = dot3(potential, split(y_both))
        value, tilt = along[:, :CLUSTER], along[:, CLUSTER:]
        sums = [[jnp.zeros((8, CLUSTER), F32) for _ in range(2)] for _ in range(3)]
        for i in range(N_DOM):
            pairs = []
            for table in (z_modes, z_tilts):
                first = jnp.broadcast_to(table[2 * i : 2 * i + 1, lanes], (8, CLUSTER))
                second = jnp.broadcast_to(table[2 * i + 1 : 2 * i + 2, lanes], (8, CLUSTER))
                pairs.append((first, second, jnp.where(upper, first, second)))
            for which, (source, table) in enumerate(((value, 0), (tilt, 0), (value, 1))):
                block = source[i * SLAB : (i + 1) * SLAB]
                first, second, mixed = pairs[table]
                sums[which][0] = sums[which][0] + (first * block[0:8] + second * block[8:16])
                sums[which][1] = sums[which][1] + mixed * block[16:24]
        for i in range(3):
            table = x_slope if i == 0 else x_table
            near = table[0:8, lanes] * sums[i][0] + table[8:16, lanes] * sums[i][1]
            force[i : i + 1, lanes] = -charge[:, lanes] * jnp.sum(near, axis=0, keepdims=True)
    long_ref[...] = jnp.zeros_like(long_ref)
    long_ref[0:3, :] = force[0:3, :]
    advance(
        short_ref[0:3, :] + force[0:3, :], 1, data_ref, move_ref, lists_ref, data_out, move_out, low_ref, high_ref
    )


def halo_step_kernel(
    lam_ref, data_ref, below_ref, above_ref, partial_ref, long_ref, move_ref, lists_ref,
    data_out, move_out, low_ref, high_ref, turns, force,
):
    add_halo_forces(lam_ref, data_ref, below_ref, above_ref, partial_ref, force, turns)
    total = force[0:3, :] + long_ref[0:3, :]
    advance(total, 2, data_ref, move_ref, lists_ref, data_out, move_out, low_ref, high_ref)


def halo_last_kernel(
    lam_ref, data_ref, below_ref, above_ref, partial_ref, long_ref, move_ref, state_ref, turns, force
):
    add_halo_forces(lam_ref, data_ref, below_ref, above_ref, partial_ref, force, turns)
    total = force[0:3, :] + long_ref[0:3, :]
    velocity = move_ref[8:11, :] + 0.5 * STEP_DT * total * data_ref[5:6, :]
    for i in range(3):
        state_ref[i] = move_ref[i : i + 1, :]
        state_ref[3 + i] = velocity[i : i + 1]
        state_ref[6 + i] = move_ref[3 + i : 4 + i, :]
    for i in range(2):
        state_ref[9 + i] = move_ref[6 + i : 7 + i, :]


def settle_kernel(here_ref, third_ref, second_ref, first_ref, cells_ref, off_ref, vel_ref):
    even = lax.axis_index("lam") % 2 == 0
    inside = lax.axis_index("lam") + 1 < lax.axis_size("lam")
    outer = jnp.where(even, second_ref[10], jnp.where(inside, here_ref[10], 0.0)) == 1.0
    far = jnp.where(even, third_ref[9], second_ref[9]) == 1.0
    close = jnp.where(even, here_ref[9], first_ref[9]) == 1.0
    for i in range(9):
        row = jnp.where(
            outer,
            jnp.where(far, third_ref[i], second_ref[i]),
            jnp.where(close, first_ref[i], here_ref[i]),
        )
        if i < 3:
            off_ref[i] = row
        elif i < 6:
            vel_ref[i - 3] = row
        else:
            cells_ref[i - 6] = row.astype(jnp.int32)


PLACES = {
    "s": pl.BlockSpec(memory_space=pltpu.SMEM),
    "v": pl.BlockSpec(memory_space=pltpu.VMEM),
    "a": pl.BlockSpec(memory_space=pl.ANY),
}


def call(kernel, ins, outs, scratch=(), cost=0, limit=40):
    return pl.pallas_call(
        kernel,
        out_shape=[jax.ShapeDtypeStruct(shape, dtype) for shape, dtype in outs],
        in_specs=[PLACES[place] for place, _ in ins],
        out_specs=[PLACES["v"]] * len(outs),
        scratch_shapes=list(scratch),
        compiler_params=pltpu.CompilerParams(vmem_limit_bytes=limit * 2**20),
        cost_estimate=pl.CostEstimate(flops=cost, bytes_accessed=200000, transcendentals=0),
    )(*[value for _, value in ins])


def neighbours(low, high):
    size = lax.axis_size("dom")
    below = lax.ppermute(high, "dom", [(i, (i + 1) % size) for i in range(size)])
    above = lax.ppermute(low, "dom", [(i, (i - 1) % size) for i in range(size)])
    return below, above


def ladder_states(state):
    windows = lax.axis_size("lam")
    pairs = [(w - 2, w) for w in range(2, windows, 2)] + [(w + 2, w) for w in range(1, windows - 2, 2)]
    received = [lax.ppermute(state, "lam", pairs)]
    for offset in (1, 0):
        pairs = []
        for w in range(offset, windows - 1, 2):
            pairs += [(w, w + 1), (w + 1, w)]
        received.append(lax.ppermute(state, "lam", pairs))
    return received


def exchanged(value):
    return lax.all_to_all(value, "dom", split_axis=0, concat_axis=0, tiled=True)


def body(
    cells, offsets, velocities, charges, coupling, inverse_mass, lambdas, tile_lists, halo_lists, accept_flags
):
    wide = ((8, A_DEV), F32)
    moving = ((16, A_DEV), F32)
    border = ((8, HALO), F32)
    turns = pltpu.VMEM((3, A_DEV), F32)
    pair_scratch = [turns, pltpu.VMEM((3, CLUSTERS * 8, CLUSTER), F32), pltpu.VMEM((3, A_DEV, CLUSTER), F32)]
    spare = pltpu.VMEM((8, A_DEV), F32)
    tiles = jnp.transpose(tile_lists, (2, 0, 1))
    slab = jnp.asarray(slab_basis())
    square, factor = plane_gain()
    gain_rows = np.zeros((K, 8), np.float32)
    gain_rows[:, 0], gain_rows[:, 1] = square, factor
    gain_lanes = np.zeros((8, K), np.float32)
    gain_lanes[0], gain_lanes[1] = square, factor

    triple = (3, 1, A_DEV)

    def by_row(x):
        return jnp.transpose(x, (1, 0, 2))


    grid, data, move, low, high = call(
        spread_kernel,
        [
            ("s", lambdas), ("a", by_row(cells)), ("a", by_row(offsets)), ("a", by_row(velocities)),
            ("a", charges[None]), ("a", coupling[None]), ("a", inverse_mass[None]), ("a", halo_lists), ("a", slab),
            ("a", accept_flags.T),
        ],
        [((ROWS, K), F32), wide, moving, border, border],
        [
            pltpu.VMEM((ROWS, A_DEV), BF16), pltpu.VMEM((ROWS, A_DEV), BF16),
            pltpu.VMEM((3, 1, A_DEV), jnp.int32), pltpu.VMEM((3, 1, A_DEV), F32), pltpu.VMEM((3, 1, A_DEV), F32),
            pltpu.VMEM((1, A_DEV), F32), pltpu.VMEM((1, A_DEV), F32), pltpu.VMEM((1, A_DEV), F32),
            pltpu.VMEM((1, 2, HALO), jnp.int32), pltpu.VMEM((MODES, MODES), F32), pltpu.VMEM((1, 2), jnp.int32),
            pltpu.SemaphoreType.DMA((9,)),
        ],
        limit=60,
    )
    grid = exchanged(grid)
    below, above = neighbours(low, high)
    short, gain = call(
        gain_kernel,
        [
            ("s", lambdas), ("s", tiles), ("s", jnp.asarray(slab_weights())), ("v", data),
            ("v", jnp.asarray(gain_rows)), ("v", jnp.asarray(gain_lanes)),
        ],
        [wide, ((2, K, K), F32)],
        pair_scratch,
        cost=2 * 10**9,
    )
    (potential,) = call(
        mesh_kernel,
        [("v", grid), ("v", gain), ("v", jnp.asarray(basis_table())), ("a", below), ("a", above)],
        [((ROWS, K), F32)],
        [pltpu.VMEM((2 * K, K), F32)],
    )
    potential = exchanged(potential)
    (short,) = call(
        rest_kernel,
        [("s", lambdas), ("s", tiles), ("v", data), ("v", below), ("v", above), ("v", short)],
        [wide],
        [*pair_scratch, spare],
        cost=2 * 10**9,
    )
    far, data, move, low, high = call(
        gather_kernel,
        [("v", potential), ("v", data), ("v", move), ("v", short), ("v", halo_lists), ("v", slab)],
        [wide, wide, moving, border, border],
        [spare],
    )

    def own_call(data):
        (partial,) = call(
            own_kernel, [("s", lambdas), ("s", tiles), ("v", data)], [wide], pair_scratch, cost=2 * 10**9
        )
        return partial

    below, above = neighbours(low, high)
    short = own_call(data)
    data, move, low, high = call(
        halo_step_kernel,
        [
            ("s", lambdas), ("v", data), ("v", below), ("v", above), ("v", short), ("v", far), ("v", move),
            ("v", halo_lists),
        ],
        [wide, moving, border, border],
        [turns, spare],
    )
    below, above = neighbours(low, high)
    short = own_call(data)
    (state,) = call(
        halo_last_kernel,
        [
            ("s", lambdas), ("v", data), ("v", below), ("v", above), ("v", short), ("v", far), ("v", move),
        ],
        [((11, 1, A_DEV), F32)],
        [turns, spare],
    )
    out = call(
        settle_kernel,
        [("v", state), *(("v", x) for x in ladder_states(state))],
        [(triple, jnp.int32), (triple, F32), (triple, F32)],
    )
    return tuple(by_row(x) for x in out)


def solution(mesh):
    in_specs = (
        P("lam", None, "dom"),
        P("lam", None, "dom"),
        P("lam", None, "dom"),
        P("dom"),
        P("dom"),
        P("dom"),
        P("lam"),
        P("lam", "dom", None),
        P("lam", "dom", None),
        P(None, "lam"),
    )
    out_specs = (P("lam", None, "dom"), P("lam", None, "dom"), P("lam", None, "dom"))
    return jax.shard_map(body, mesh=mesh, in_specs=in_specs, out_specs=out_specs, check_vma=False)
```

```python
import functools
import math

import jax
import jax.numpy as jnp
import ml_dtypes
import numpy as np
from jax import lax
from jax.experimental import pallas as pl
from jax.experimental.pallas import tpu as pltpu
from jax.sharding import PartitionSpec as P

K = 128
CLUSTER = 128
N_DOM = 16
A_DEV = 1024
CLUSTERS = 8
HALO = 512
MODES = 32
SLAB = 24
ROWS = N_DOM * SLAB

EWALD_BETA = 0.5
COULOMB = 20.0
LJ_DEPTH = 1.0
LJ_SIGMA_SQ = 0.49
SOFT_SCALE = 0.5
SOFT_FLOOR = 0.5
STEP_DT = 0.25

F32 = jnp.float32
BF16 = jnp.bfloat16
HIGHEST = lax.Precision.HIGHEST

TURN = 2.0**32
SPAN_SQ = 2.0**-50
SPAN = 2.0**-25

SCREEN = (
    -0.0818439527,
    0.648023047,
    -2.23331568,
    4.38709699,
    -5.37737017,
    4.16223694,
    -1.81397109,
    0.0540053844,
    0.5630337,
    -5.2346482e-05,
    0.282096019,
)


def real_basis(count):
    half = count // 2
    place = np.arange(count)
    rows = []
    for k in range(half + 1):
        scale = math.sqrt((1.0 if k in (0, half) else 2.0) / count)
        rows.append(scale * np.cos(2.0 * np.pi * (k * place % count) / count))
    for k in range(1, half):
        rows.append(math.sqrt(2.0 / count) * np.sin(2.0 * np.pi * (k * place % count) / count))
    return np.stack(rows)


def halves(table):
    high = table.astype(np.float32).astype(ml_dtypes.bfloat16)
    low = (table - high.astype(np.float64)).astype(np.float32).astype(ml_dtypes.bfloat16)
    return high, low


def basis_table():
    basis = real_basis(K)
    high, low = halves(basis)
    return np.concatenate([high, low, high.T, low.T], axis=0)


def slab_basis():
    basis = real_basis(MODES)
    order = [0, MODES // 2]
    for k in range(1, MODES // 2):
        order += [k, MODES // 2 + k]
    return basis[np.array(order)].astype(np.float32)


def spline_modulus(k):
    return (3.0 / (2.0 + np.cos(2.0 * np.pi * k / K))) ** 2


def slab_weights():
    k = np.arange(K // 2 + 1)
    delta = np.arange(-MODES // 2 + 1, MODES // 2 + 1)
    folded = np.where((k == 0) | (k == K // 2), 1.0, 2.0)
    own = folded * np.exp(-np.pi**2 * (k / K) ** 2 / EWALD_BETA**2) * spline_modulus(k)
    rows = []
    for j in range(MODES // 2 + 1):
        window = np.cos(2 * np.pi * k[:, None] * delta / K) * np.cos(2 * np.pi * j * delta / MODES)
        rows.append(own * window.sum(axis=1))
    return np.stack(rows).astype(np.float32)


def plane_gain():
    k = np.concatenate([np.arange(K // 2 + 1), np.arange(1, K // 2)])
    square = (k / K) ** 2
    factor = np.exp(-np.pi**2 * square / EWALD_BETA**2) * spline_modulus(k)
    return square.astype(np.float32), factor.astype(np.float32)


def split(x):
    high = x.astype(BF16)
    return high, (x - high.astype(F32)).astype(BF16)


def dot3(left, right, dims=(((1,), (0,)), ((), ()))):
    lh, ll = left
    rh, rl = right
    dot = functools.partial(lax.dot_general, dimension_numbers=dims, preferred_element_type=F32)
    return dot(lh, rh) + (dot(lh, rl) + dot(ll, rh))


def spline_set(u):
    v = 1.0 - u
    u2 = u * u
    u3 = u2 * u
    weights = (
        v * v * v / 6.0,
        (3.0 * u3 - 6.0 * u2 + 4.0) / 6.0,
        (-3.0 * u3 + 3.0 * u2 + 3.0 * u + 1.0) / 6.0,
        u3 / 6.0,
    )
    slopes = (-0.5 * v * v, 1.5 * u2 - 2.0 * u, -1.5 * u2 + u + 0.5, 0.5 * u2)
    return weights, slopes


def chosen(distance, rows):
    out = jnp.where(distance == 3, rows[3], 0.0)
    for k in (2, 1, 0):
        out = jnp.where(distance == k, rows[k], out)
    return out


def iota_rows(rows, columns):
    return lax.broadcasted_iota(jnp.int32, (rows, columns), 0)


def fixed_turns(x):
    t = x * (1.0 / K)
    f = t - jnp.floor(t + 0.5)
    return jnp.maximum(f, -0.5) * TURN


def pair_terms(own, other, floor_value):
    ax, ay, az, qa, wa = own
    bx, by, bz, qb, wb = other
    dx = (ax - bx).astype(F32)
    dy = (ay - by).astype(F32)
    dz = (az - bz).astype(F32)
    s = (dx * dx + dy * dy + dz * dz) * SPAN_SQ + floor_value
    w = lax.rsqrt(s)
    u = w * w
    screen = jnp.full_like(w, SCREEN[0])
    for c in SCREEN[1:]:
        screen = screen * w + c
    gauss = jnp.exp2(s * (-(EWALD_BETA**2) * math.log2(math.e)))
    t = u * u * u
    g = u * ((qa * qb) * (gauss * screen) + (wa * wb) * (t * (t - 0.5 / LJ_SIGMA_SQ**3)))
    return g * dx, g * dy, g * dz


def own_rows(data_ref, turns, start, rows=8):
    def spread(row):
        return jnp.broadcast_to(row, (rows, CLUSTER))

    columns = pl.ds(start, CLUSTER)
    xyz = [spread(turns[i : i + 1, columns].astype(jnp.int32)) for i in range(3)]
    q = spread(data_ref[3:4, columns] * (2.0 * COULOMB))
    w = spread(data_ref[4:5, columns] * (48.0 * LJ_DEPTH * LJ_SIGMA_SQ**6))
    return (*xyz, q, w)


def write_halo(data, lists_ref, low_ref, high_ref):
    lane = lax.broadcasted_iota(jnp.int32, (8, CLUSTER), 1)
    for row, out_ref in ((0, low_ref), (1, high_ref)):
        for k in range(HALO // CLUSTER):
            columns = slice(k * CLUSTER, (k + 1) * CLUSTER)
            index = jnp.broadcast_to(lists_ref[0, row : row + 1, columns] & (CLUSTER - 1), (8, CLUSTER))
            first = data[:, 2 * k * CLUSTER : (2 * k + 1) * CLUSTER]
            second = data[:, (2 * k + 1) * CLUSTER : (2 * k + 2) * CLUSTER]
            out_ref[:, columns] = jnp.where(
                lane < CLUSTER // 2,
                jnp.take_along_axis(first, index, axis=1, mode="promise_in_bounds"),
                jnp.take_along_axis(second, index, axis=1, mode="promise_in_bounds"),
            )


def spread_kernel(
    lam_ref, cells_hbm, off_hbm, vel_hbm, charge_hbm, coup_hbm, mass_hbm, lists_hbm, slab_hbm, flag_hbm,
    out_ref, data_ref, move_ref, low_ref, high_ref, mixed_high, mixed_low,
    cells_ref, off_ref, vel_ref, charge_ref, coup_ref, mass_ref, lists_ref, slab_ref, flag_ref, arrived,
):
    copies = [
        pltpu.make_async_copy(source, target, arrived.at[i])
        for i, (source, target) in enumerate(
            (
                (cells_hbm, cells_ref), (off_hbm, off_ref), (vel_hbm, vel_ref), (charge_hbm, charge_ref),
                (coup_hbm, coup_ref), (mass_hbm, mass_ref), (lists_hbm, lists_ref), (slab_hbm, slab_ref),
                (flag_hbm, flag_ref),
            )
        )
    ]
    for copy in copies:
        copy.start()
    for copy in copies:
        copy.wait()
    weight = 1.0 - lam_ref[0] * coup_ref[...]
    charge = charge_ref[...] * weight

    for i in range(3):
        cell = cells_ref[i].astype(F32)
        move_ref[i : i + 1, :] = off_ref[i]
        move_ref[3 + i : 4 + i, :] = cell
        move_ref[8 + i : 9 + i, :] = vel_ref[i]
        data_ref[i : i + 1, :] = cell + off_ref[i]
    move_ref[6:7, :] = jnp.broadcast_to(flag_ref[0:1, 0:1].astype(F32), (1, A_DEV))
    move_ref[7:8, :] = jnp.broadcast_to(flag_ref[0:1, 1:2].astype(F32), (1, A_DEV))
    move_ref[11:16, :] = jnp.zeros((5, A_DEV), F32)
    data_ref[3:4, :] = charge
    data_ref[4:5, :] = weight
    data_ref[5:6, :] = mass_ref[...]
    data_ref[6:8, :] = jnp.zeros((2, A_DEV), F32)
    write_halo(data_ref[...], lists_ref, low_ref, high_ref)

    off = move_ref[0:3, :]
    cells = [cells_ref[i] for i in range(3)]
    weights, _ = spline_set(off)
    row = iota_rows(16, A_DEV)
    plane = jnp.where(row < 8, row, 8 + (row & 3))
    x_table = chosen(plane - (cells[0] & 7), [m[0:1] for m in weights]) * charge
    z_table = chosen((iota_rows(MODES, A_DEV) - cells[2]) & (MODES - 1), [m[2:3] for m in weights])
    z_modes = jnp.dot(slab_ref[...], z_table, precision=HIGHEST, preferred_element_type=F32)
    y_table = chosen((iota_rows(K, A_DEV) - cells[1]) & (K - 1), [m[1:2] for m in weights])

    near, far = x_table[0:8], x_table[8:16]
    upper = iota_rows(8, A_DEV) < 4
    for i in range(0, N_DOM, 2):
        pieces = []
        for k in (i, i + 1):
            first = jnp.broadcast_to(z_modes[2 * k : 2 * k + 1], (8, A_DEV))
            second = jnp.broadcast_to(z_modes[2 * k + 1 : 2 * k + 2], (8, A_DEV))
            pieces += [near * first, near * second, far * jnp.where(upper, first, second)]
        high, low = split(jnp.concatenate(pieces, axis=0))
        mixed_high[i * SLAB : (i + 2) * SLAB, :] = high
        mixed_low[i * SLAB : (i + 2) * SLAB, :] = low
    out_ref[...] = dot3((mixed_high[...], mixed_low[...]), split(y_table), (((1,), (1,)), ((), ())))


def mesh_kernel(grid_ref, gain_ref, basis_ref, below_ref, above_ref, out_ref, block):
    del below_ref, above_ref
    top = iota_rows(8, K) < 4
    for e in range(N_DOM):
        spill = grid_ref[((e - 1) % N_DOM) * SLAB + 16 : ((e - 1) % N_DOM) * SLAB + 24, :]
        turned = pltpu.roll(spill, 4, 0)
        block[8 * e : 8 * e + 8, :] = grid_ref[e * SLAB : e * SLAB + 8, :] + jnp.where(top, spill, 0.0)
        block[K + 8 * e : K + 8 * e + 8, :] = grid_ref[e * SLAB + 8 : e * SLAB + 16, :] + jnp.where(top, turned, 0.0)
    basis = (basis_ref[0:K, :], basis_ref[K : 2 * K, :])
    turned_basis = (basis_ref[2 * K : 3 * K, :], basis_ref[3 * K : 4 * K, :])
    along_y = dot3(split(block[...]), turned_basis)
    for mode in range(2):
        part = split(along_y[mode * K : (mode + 1) * K])
        scaled = dot3(basis, part) * gain_ref[mode]
        block[mode * K : (mode + 1) * K, :] = dot3(turned_basis, split(scaled))
    block[...] = dot3(split(block[...]), basis)
    for e in range(N_DOM):
        following = 8 * ((e + 1) % N_DOM)
        out_ref[e * SLAB : e * SLAB + 8, :] = block[8 * e : 8 * e + 8, :]
        out_ref[e * SLAB + 8 : e * SLAB + 16, :] = block[K + 8 * e : K + 8 * e + 8, :]
        out_ref[e * SLAB + 16 : e * SLAB + 24, :] = jnp.where(
            top,
            block[following : following + 8, :],
            pltpu.roll(block[K + following : K + following + 8, :], 4, 0),
        )


def write_gain(mode_weights_ref, rows_ref, lanes_ref, gain_ref):
    dom = lax.axis_index("dom")
    square_y, factor_y = lanes_ref[0:1, :], lanes_ref[1:2, :]
    scale = COULOMB / (math.pi * K)
    first = dom
    second = jnp.where(dom == 0, MODES // 2, dom)

    def totals(square):
        one = jnp.zeros_like(square)
        two = jnp.zeros_like(square)
        for k in range(K // 2 + 1):
            whole = square + (k / K) ** 2
            inverse = 1.0 / whole if k else jnp.where(whole > 0.0, 1.0 / jnp.where(whole > 0.0, whole, 1.0), 0.0)
            one = one + inverse * mode_weights_ref[first, k]
            two = two + inverse * mode_weights_ref[second, k]
        return one, two

    def block(start):
        rows = pl.ds(start, 8)
        square = jnp.broadcast_to(rows_ref[rows, 0:1], (8, K)) + square_y
        factor = jnp.broadcast_to(rows_ref[rows, 1:2], (8, K)) * factor_y * scale
        one, two = totals(square)
        return one * factor, two * factor

    def step(b, carry):
        start = pl.multiple_of(b * 8, 8)
        one, two = block(start)
        gain_ref[0, pl.ds(start, 8), :] = one
        gain_ref[1, pl.ds(start, 8), :] = two
        gain_ref[0, pl.ds(start + K // 2, 8), :] = one
        gain_ref[1, pl.ds(start + K // 2, 8), :] = two
        return carry

    lax.fori_loop(0, 8, step, 0)
    one, two = block(K // 2)
    gain_ref[0, K // 2 : K // 2 + 1, :] = one[0:1]
    gain_ref[1, K // 2 : K // 2 + 1, :] = two[0:1]


def listed(tiles_ref, row, cluster):
    count = jnp.int32(0)
    for slot in range(1, 4):
        count = count + jnp.where(tiles_ref[slot, 0, row] == cluster, 1, 0)
    return count.astype(F32)


def own_forces(lam_ref, tiles_ref, data_ref, force_ref, turns, near, sides, columns, places, factors, first, last):
    turns[...] = fixed_turns(data_ref[0:3, :])
    near[...] = jnp.zeros_like(near)
    floor_value = SOFT_FLOOR + SOFT_SCALE * lam_ref[0]
    for b in range(first, last):
        lanes = slice(b * CLUSTER, (b + 1) * CLUSTER)
        columns[lanes, :] = jnp.concatenate([turns[:, lanes], data_ref[3:8, lanes]], axis=0).T

    def one_cluster(b, carry):
        start = pl.multiple_of(b * CLUSTER, CLUSTER)
        for j in range(3):
            a = b if j == 0 else (b + j) % CLUSTERS
            own = own_rows(data_ref, turns, pl.multiple_of(a * CLUSTER, CLUSTER))
            total = [jnp.zeros((8, CLUSTER), F32) for _ in range(3)]
            back = listed(tiles_ref, b, a) if j else None
            for chunk in range(CLUSTER // 8):
                here = slice(chunk * 8, chunk * 8 + 8)
                rows = pl.ds(pl.multiple_of(start + chunk * 8, 8), 8)
                if j == 0:
                    part = columns[rows, :]
                    other = [jnp.broadcast_to(part[:, i : i + 1], (8, CLUSTER)) for i in range(5)]
                    other[:3] = [x.astype(jnp.int32) for x in other[:3]]
                    for i in range(3):
                        places[i, here, :] = other[i]
                    for i in range(2):
                        factors[i, here, :] = other[3 + i]
                else:
                    other = [places[i, here, :] for i in range(3)] + [factors[i, here, :] for i in range(2)]
                terms = pair_terms(own, other, floor_value)
                total = [p + q for p, q in zip(total, terms)]
                for i in range(3):
                    if j == 1:
                        sides[i, rows, :] = back * terms[i]
                    elif j == 2:
                        sides[i, rows, :] = sides[i, rows, :] + back * terms[i]
            rows = pl.ds(pl.multiple_of(a * 8, 8), 8)
            for i in range(3):
                near[i, rows, :] = near[i, rows, :] + (listed(tiles_ref, a, b) * total[i] if j else total[i])
        return carry

    lax.fori_loop(first, last, one_cluster, 0)
    force_ref[...] = jnp.zeros_like(force_ref)
    ones = jnp.ones((8, CLUSTER), BF16)
    for c in range(CLUSTERS):
        lanes = slice(c * CLUSTER, (c + 1) * CLUSTER)
        for i in range(3):
            force_ref[i : i + 1, lanes] = SPAN * jnp.sum(near[i, c * 8 : (c + 1) * 8, :], axis=0, keepdims=True)
    rows = slice(first * CLUSTER, last * CLUSTER)
    for i in range(3):
        rest = sides[i, rows, :]
        total = jnp.zeros((8, (last - first) * CLUSTER), F32)
        for _ in range(3):
            part = rest.astype(BF16)
            rest = rest - part.astype(F32)
            total = total + lax.dot_general(ones, part, (((1,), (1,)), ((), ())), preferred_element_type=F32)
        force_ref[i : i + 1, rows] = force_ref[i : i + 1, rows] - SPAN * total[0:1]


def own_kernel(lam_ref, tiles_ref, data_ref, force_ref, turns, near, sides, *kept):
    own_forces(lam_ref, tiles_ref, data_ref, force_ref, turns, near, sides, *kept, 0, CLUSTERS)


def gain_kernel(
    lam_ref, tiles_ref, weights_ref, data_ref, rows_ref, lanes_ref, force_ref, gain_ref, turns, near, sides, *kept
):
    write_gain(weights_ref, rows_ref, lanes_ref, gain_ref)
    own_forces(lam_ref, tiles_ref, data_ref, force_ref, turns, near, sides, *kept, 0, CLUSTERS // 2)


def add_halo_forces(lam_ref, data_ref, below_ref, above_ref, partial_ref, force_ref, turns):
    turns[...] = fixed_turns(data_ref[0:3, :])
    floor_value = SOFT_FLOOR + SOFT_SCALE * lam_ref[0]

    def one_pair(k, carry):
        start = pl.multiple_of(k * CLUSTER, CLUSTER)
        starts = [pl.multiple_of(k * (2 * CLUSTER), CLUSTER), pl.multiple_of(k * (2 * CLUSTER) + CLUSTER, CLUSTER)]
        owns = [own_rows(data_ref, turns, s) for s in starts]
        totals = [[jnp.zeros((8, CLUSTER), F32) for _ in range(3)] for _ in range(2)]
        for source in (below_ref, above_ref):
            block = source[:, pl.ds(start, CLUSTER)]
            stack = jnp.where(iota_rows(8, CLUSTER) < 3, fixed_turns(block), block)
            turned = stack.T
            for chunk in range(CLUSTER // 8):
                part = turned[chunk * 8 : chunk * 8 + 8]
                other = [jnp.broadcast_to(part[:, i : i + 1], (8, CLUSTER)) for i in range(5)]
                other[:3] = [x.astype(jnp.int32) for x in other[:3]]
                for j in range(2):
                    terms = pair_terms(owns[j], other, floor_value)
                    totals[j] = [a + b for a, b in zip(totals[j], terms)]
        for j in range(2):
            lanes = pl.ds(starts[j], CLUSTER)
            for i in range(3):
                force_ref[i : i + 1, lanes] = partial_ref[i : i + 1, lanes] + SPAN * jnp.sum(
                    totals[j][i], axis=0, keepdims=True
                )
        return carry

    lax.fori_loop(0, HALO // CLUSTER, one_pair, 0)


def rest_kernel(
    lam_ref, tiles_ref, data_ref, below_ref, above_ref, partial_ref, force_ref, second, turns, near, sides, *kept
):
    own_forces(lam_ref, tiles_ref, data_ref, second, turns, near, sides, *kept, CLUSTERS // 2, CLUSTERS)
    second[...] = second[...] + partial_ref[...]
    force_ref[...] = jnp.zeros_like(force_ref)
    add_halo_forces(lam_ref, data_ref, below_ref, above_ref, second, force_ref, turns)


def advance(force, kicks, data_ref, move_ref, lists_ref, data_out, move_out, low_ref, high_ref):
    mass = data_ref[5:6, :]
    velocity = move_ref[8:11, :]
    for _ in range(kicks):
        velocity = velocity + 0.5 * STEP_DT * force * mass
    off = move_ref[0:3, :] + STEP_DT * velocity
    move_out[...] = move_ref[...]
    move_out[0:3, :] = off
    move_out[8:11, :] = velocity
    data_out[...] = data_ref[...]
    data_out[0:3, :] = move_ref[3:6, :] + off
    write_halo(data_out[...], lists_ref, low_ref, high_ref)


def gather_kernel(
    pot_ref, data_ref, move_ref, short_ref, lists_ref, slab_ref,
    long_ref, data_out, move_out, low_ref, high_ref, force,
):
    off = move_ref[0:3, :]
    cells = move_ref[3:6, :].astype(jnp.int32)
    charge = data_ref[3:4, :]
    weights, slopes = spline_set(off)
    row = iota_rows(16, A_DEV)
    reach = jnp.where(row < 8, row, 8 + (row & 3)) - (cells[0:1] & 7)
    x_table = chosen(reach, [m[0:1] for m in weights])
    x_slope = chosen(reach, [m[0:1] for m in slopes])
    reach = (iota_rows(MODES, A_DEV) - cells[2:3]) & (MODES - 1)
    z_table = chosen(reach, [m[2:3] for m in weights])
    z_slope = chosen(reach, [m[2:3] for m in slopes])
    z_modes = jnp.dot(slab_ref[...], z_table, precision=HIGHEST, preferred_element_type=F32)
    z_tilts = jnp.dot(slab_ref[...], z_slope, precision=HIGHEST, preferred_element_type=F32)
    potential = split(pot_ref[...])
    upper = iota_rows(8, CLUSTER) < 4
    for c in range(CLUSTERS):
        lanes = slice(c * CLUSTER, (c + 1) * CLUSTER)
        reach = (iota_rows(K, CLUSTER) - cells[1:2, lanes]) & (K - 1)
        y_both = jnp.concatenate(
            [chosen(reach, [m[1:2, lanes] for m in weights]), chosen(reach, [m[1:2, lanes] for m in slopes])], axis=1
        )
        along = dot3(potential, split(y_both))
        value, tilt = along[:, :CLUSTER], along[:, CLUSTER:]
        sums = [[jnp.zeros((8, CLUSTER), F32) for _ in range(2)] for _ in range(3)]
        for i in range(N_DOM):
            pairs = []
            for table in (z_modes, z_tilts):
                first = jnp.broadcast_to(table[2 * i : 2 * i + 1, lanes], (8, CLUSTER))
                second = jnp.broadcast_to(table[2 * i + 1 : 2 * i + 2, lanes], (8, CLUSTER))
                pairs.append((first, second, jnp.where(upper, first, second)))
            for which, (source, table) in enumerate(((value, 0), (tilt, 0), (value, 1))):
                block = source[i * SLAB : (i + 1) * SLAB]
                first, second, mixed = pairs[table]
                sums[which][0] = sums[which][0] + (first * block[0:8] + second * block[8:16])
                sums[which][1] = sums[which][1] + mixed * block[16:24]
        for i in range(3):
            table = x_slope if i == 0 else x_table
            near = table[0:8, lanes] * sums[i][0] + table[8:16, lanes] * sums[i][1]
            force[i : i + 1, lanes] = -charge[:, lanes] * jnp.sum(near, axis=0, keepdims=True)
    long_ref[...] = jnp.zeros_like(long_ref)
    long_ref[0:3, :] = force[0:3, :]
    advance(
        short_ref[0:3, :] + force[0:3, :], 1, data_ref, move_ref, lists_ref, data_out, move_out, low_ref, high_ref
    )


def halo_step_kernel(
    lam_ref, data_ref, below_ref, above_ref, partial_ref, long_ref, move_ref, lists_ref,
    data_out, move_out, low_ref, high_ref, turns, force,
):
    add_halo_forces(lam_ref, data_ref, below_ref, above_ref, partial_ref, force, turns)
    total = force[0:3, :] + long_ref[0:3, :]
    advance(total, 2, data_ref, move_ref, lists_ref, data_out, move_out, low_ref, high_ref)


def halo_last_kernel(
    lam_ref, data_ref, below_ref, above_ref, partial_ref, long_ref, move_ref, state_ref, turns, force
):
    add_halo_forces(lam_ref, data_ref, below_ref, above_ref, partial_ref, force, turns)
    total = force[0:3, :] + long_ref[0:3, :]
    velocity = move_ref[8:11, :] + 0.5 * STEP_DT * total * data_ref[5:6, :]
    for i in range(3):
        state_ref[i] = move_ref[i : i + 1, :]
        state_ref[3 + i] = velocity[i : i + 1]
        state_ref[6 + i] = move_ref[3 + i : 4 + i, :]
    state_ref[9] = move_ref[6:7, :]


def takes(round_index, here_ref, there_ref):
    window = lax.axis_index("lam")
    lower = window % 2 == round_index % 2
    inside = window + 1 < lax.axis_size("lam")
    return jnp.where(lower, jnp.where(inside, here_ref[9], 0.0), there_ref[9]) == 1.0


def first_trade_kernel(here_ref, there_ref, move_ref, out_ref):
    take = takes(0, here_ref, there_ref)
    for i in range(9):
        out_ref[i] = jnp.where(take, there_ref[i], here_ref[i])
    out_ref[9] = move_ref[7:8, :]


def last_trade_kernel(here_ref, there_ref, cells_ref, off_ref, vel_ref):
    take = takes(1, here_ref, there_ref)
    for i in range(3):
        off_ref[i] = jnp.where(take, there_ref[i], here_ref[i])
        vel_ref[i] = jnp.where(take, there_ref[3 + i], here_ref[3 + i])
        cells_ref[i] = jnp.where(take, there_ref[6 + i], here_ref[6 + i]).astype(jnp.int32)


PLACES = {
    "s": pl.BlockSpec(memory_space=pltpu.SMEM),
    "v": pl.BlockSpec(memory_space=pltpu.VMEM),
    "a": pl.BlockSpec(memory_space=pl.ANY),
}


def call(kernel, ins, outs, scratch=(), cost=0, limit=40):
    return pl.pallas_call(
        kernel,
        out_shape=[jax.ShapeDtypeStruct(shape, dtype) for shape, dtype in outs],
        in_specs=[PLACES[place] for place, _ in ins],
        out_specs=[PLACES["v"]] * len(outs),
        scratch_shapes=list(scratch),
        compiler_params=pltpu.CompilerParams(vmem_limit_bytes=limit * 2**20),
        cost_estimate=pl.CostEstimate(flops=cost, bytes_accessed=200000, transcendentals=0),
    )(*[value for _, value in ins])


def neighbours(low, high):
    size = lax.axis_size("dom")
    below = lax.ppermute(high, "dom", [(i, (i + 1) % size) for i in range(size)])
    above = lax.ppermute(low, "dom", [(i, (i - 1) % size) for i in range(size)])
    return below, above


def traded(state, round_index):
    pairs = []
    for w in range(round_index % 2, lax.axis_size("lam") - 1, 2):
        pairs += [(w, w + 1), (w + 1, w)]
    return lax.ppermute(state, "lam", pairs)


def exchanged(value):
    return lax.all_to_all(value, "dom", split_axis=0, concat_axis=0, tiled=True)


def body(
    cells, offsets, velocities, charges, coupling, inverse_mass, lambdas, tile_lists, halo_lists, accept_flags
):
    wide = ((8, A_DEV), F32)
    moving = ((16, A_DEV), F32)
    border = ((8, HALO), F32)
    turns = pltpu.VMEM((3, A_DEV), F32)
    pair_scratch = [
        turns, pltpu.VMEM((3, CLUSTERS * 8, CLUSTER), F32), pltpu.VMEM((3, A_DEV, CLUSTER), F32),
        pltpu.VMEM((A_DEV, 8), F32), pltpu.VMEM((3, CLUSTER, CLUSTER), jnp.int32), pltpu.VMEM((2, CLUSTER, CLUSTER), F32),
    ]
    spare = pltpu.VMEM((8, A_DEV), F32)
    tiles = jnp.transpose(tile_lists, (2, 0, 1))
    slab = jnp.asarray(slab_basis())
    square, factor = plane_gain()
    gain_rows = np.zeros((K, 8), np.float32)
    gain_rows[:, 0], gain_rows[:, 1] = square, factor
    gain_lanes = np.zeros((8, K), np.float32)
    gain_lanes[0], gain_lanes[1] = square, factor

    triple = (3, 1, A_DEV)

    def by_row(x):
        return jnp.transpose(x, (1, 0, 2))


    grid, data, move, low, high = call(
        spread_kernel,
        [
            ("s", lambdas), ("a", by_row(cells)), ("a", by_row(offsets)), ("a", by_row(velocities)),
            ("a", charges[None]), ("a", coupling[None]), ("a", inverse_mass[None]), ("a", halo_lists), ("a", slab),
            ("a", accept_flags.T),
        ],
        [((ROWS, K), F32), wide, moving, border, border],
        [
            pltpu.VMEM((ROWS, A_DEV), BF16), pltpu.VMEM((ROWS, A_DEV), BF16),
            pltpu.VMEM((3, 1, A_DEV), jnp.int32), pltpu.VMEM((3, 1, A_DEV), F32), pltpu.VMEM((3, 1, A_DEV), F32),
            pltpu.VMEM((1, A_DEV), F32), pltpu.VMEM((1, A_DEV), F32), pltpu.VMEM((1, A_DEV), F32),
            pltpu.VMEM((1, 2, HALO), jnp.int32), pltpu.VMEM((MODES, MODES), F32), pltpu.VMEM((1, 2), jnp.int32),
            pltpu.SemaphoreType.DMA((9,)),
        ],
        limit=60,
    )
    grid = exchanged(grid)
    below, above = neighbours(low, high)
    short, gain = call(
        gain_kernel,
        [
            ("s", lambdas), ("s", tiles), ("s", jnp.asarray(slab_weights())), ("v", data),
            ("v", jnp.asarray(gain_rows)), ("v", jnp.asarray(gain_lanes)),
        ],
        [wide, ((2, K, K), F32)],
        pair_scratch,
        cost=2 * 10**9,
    )
    (potential,) = call(
        mesh_kernel,
        [("v", grid), ("v", gain), ("v", jnp.asarray(basis_table())), ("a", below), ("a", above)],
        [((ROWS, K), F32)],
        [pltpu.VMEM((2 * K, K), F32)],
    )
    potential = exchanged(potential)
    (short,) = call(
        rest_kernel,
        [("s", lambdas), ("s", tiles), ("v", data), ("v", below), ("v", above), ("v", short)],
        [wide],
        [spare, *pair_scratch],
        cost=2 * 10**9,
    )
    far, data, move, low, high = call(
        gather_kernel,
        [("v", potential), ("v", data), ("v", move), ("v", short), ("v", halo_lists), ("v", slab)],
        [wide, wide, moving, border, border],
        [spare],
    )

    def own_call(data):
        (partial,) = call(
            own_kernel, [("s", lambdas), ("s", tiles), ("v", data)], [wide], pair_scratch, cost=2 * 10**9
        )
        return partial

    below, above = neighbours(low, high)
    short = own_call(data)
    data, move, low, high = call(
        halo_step_kernel,
        [
            ("s", lambdas), ("v", data), ("v", below), ("v", above), ("v", short), ("v", far), ("v", move),
            ("v", halo_lists),
        ],
        [wide, moving, border, border],
        [turns, spare],
    )
    below, above = neighbours(low, high)
    short = own_call(data)
    (state,) = call(
        halo_last_kernel,
        [
            ("s", lambdas), ("v", data), ("v", below), ("v", above), ("v", short), ("v", far), ("v", move),
        ],
        [((10, 1, A_DEV), F32)],
        [turns, spare],
    )
    (state,) = call(
        first_trade_kernel, [("v", state), ("v", traded(state, 0)), ("v", move)], [((10, 1, A_DEV), F32)]
    )
    out = call(
        last_trade_kernel,
        [("v", state), ("v", traded(state, 1))],
        [(triple, jnp.int32), (triple, F32), (triple, F32)],
    )
    return tuple(by_row(x) for x in out)


def solution(mesh):
    in_specs = (
        P("lam", None, "dom"),
        P("lam", None, "dom"),
        P("lam", None, "dom"),
        P("dom"),
        P("dom"),
        P("dom"),
        P("lam"),
        P("lam", "dom", None),
        P("lam", "dom", None),
        P(None, "lam"),
    )
    out_specs = (P("lam", None, "dom"), P("lam", None, "dom"), P("lam", None, "dom"))
    return jax.shard_map(body, mesh=mesh, in_specs=in_specs, out_specs=out_specs, check_vma=False)
```

```python
import functools
import math

import jax
import jax.numpy as jnp
import ml_dtypes
import numpy as np
from jax import lax
from jax.experimental import pallas as pl
from jax.experimental.pallas import tpu as pltpu
from jax.sharding import PartitionSpec as P

K = 128
CLUSTER = 128
N_DOM = 16
A_DEV = 1024
CLUSTERS = 8
HALO = 512
MODES = 32
SLAB = 24
ROWS = N_DOM * SLAB

EWALD_BETA = 0.5
COULOMB = 20.0
LJ_DEPTH = 1.0
LJ_SIGMA_SQ = 0.49
SOFT_SCALE = 0.5
SOFT_FLOOR = 0.5
STEP_DT = 0.25

F32 = jnp.float32
BF16 = jnp.bfloat16
HIGHEST = lax.Precision.HIGHEST

TURN = 2.0**32
SPAN_SQ = 2.0**-50
SPAN = 2.0**-25

SCREEN = (
    -0.0818439527,
    0.648023047,
    -2.23331568,
    4.38709699,
    -5.37737017,
    4.16223694,
    -1.81397109,
    0.0540053844,
    0.5630337,
    -5.2346482e-05,
    0.282096019,
)


def real_basis(count):
    half = count // 2
    place = np.arange(count)
    rows = []
    for k in range(half + 1):
        scale = math.sqrt((1.0 if k in (0, half) else 2.0) / count)
        rows.append(scale * np.cos(2.0 * np.pi * (k * place % count) / count))
    for k in range(1, half):
        rows.append(math.sqrt(2.0 / count) * np.sin(2.0 * np.pi * (k * place % count) / count))
    return np.stack(rows)


def halves(table):
    high = table.astype(np.float32).astype(ml_dtypes.bfloat16)
    low = (table - high.astype(np.float64)).astype(np.float32).astype(ml_dtypes.bfloat16)
    return high, low


def basis_table():
    basis = real_basis(K)
    high, low = halves(basis)
    return np.concatenate([high, low, high.T, low.T], axis=0)


def slab_basis():
    basis = real_basis(MODES)
    order = [0, MODES // 2]
    for k in range(1, MODES // 2):
        order += [k, MODES // 2 + k]
    return basis[np.array(order)].astype(np.float32)


def spline_modulus(k):
    return (3.0 / (2.0 + np.cos(2.0 * np.pi * k / K))) ** 2


def slab_weights():
    k = np.arange(K // 2 + 1)
    delta = np.arange(-MODES // 2 + 1, MODES // 2 + 1)
    folded = np.where((k == 0) | (k == K // 2), 1.0, 2.0)
    own = folded * np.exp(-np.pi**2 * (k / K) ** 2 / EWALD_BETA**2) * spline_modulus(k)
    rows = []
    for j in range(MODES // 2 + 1):
        window = np.cos(2 * np.pi * k[:, None] * delta / K) * np.cos(2 * np.pi * j * delta / MODES)
        rows.append(own * window.sum(axis=1))
    return np.stack(rows).astype(np.float32)


def plane_gain():
    k = np.concatenate([np.arange(K // 2 + 1), np.arange(1, K // 2)])
    square = (k / K) ** 2
    factor = np.exp(-np.pi**2 * square / EWALD_BETA**2) * spline_modulus(k)
    return square.astype(np.float32), factor.astype(np.float32)


def split(x):
    high = x.astype(BF16)
    return high, (x - high.astype(F32)).astype(BF16)


def dot3(left, right, dims=(((1,), (0,)), ((), ()))):
    lh, ll = left
    rh, rl = right
    dot = functools.partial(lax.dot_general, dimension_numbers=dims, preferred_element_type=F32)
    return dot(lh, rh) + (dot(lh, rl) + dot(ll, rh))


def spline_set(u):
    v = 1.0 - u
    u2 = u * u
    u3 = u2 * u
    weights = (
        v * v * v / 6.0,
        (3.0 * u3 - 6.0 * u2 + 4.0) / 6.0,
        (-3.0 * u3 + 3.0 * u2 + 3.0 * u + 1.0) / 6.0,
        u3 / 6.0,
    )
    slopes = (-0.5 * v * v, 1.5 * u2 - 2.0 * u, -1.5 * u2 + u + 0.5, 0.5 * u2)
    return weights, slopes


def chosen(distance, rows):
    out = jnp.where(distance == 3, rows[3], 0.0)
    for k in (2, 1, 0):
        out = jnp.where(distance == k, rows[k], out)
    return out


def iota_rows(rows, columns):
    return lax.broadcasted_iota(jnp.int32, (rows, columns), 0)


def fixed_turns(x):
    t = x * (1.0 / K)
    f = t - jnp.floor(t + 0.5)
    return jnp.maximum(f, -0.5) * TURN


def pair_terms(own, other, floor_value):
    ax, ay, az, qa, wa = own
    bx, by, bz, qb, wb = other
    dx = (ax - bx).astype(F32)
    dy = (ay - by).astype(F32)
    dz = (az - bz).astype(F32)
    s = (dx * dx + dy * dy + dz * dz) * SPAN_SQ + floor_value
    w = lax.rsqrt(s)
    u = w * w
    screen = jnp.full_like(w, SCREEN[0])
    for c in SCREEN[1:]:
        screen = screen * w + c
    gauss = jnp.exp2(s * (-(EWALD_BETA**2) * math.log2(math.e)))
    t = u * u * u
    g = u * ((qa * qb) * (gauss * screen) + (wa * wb) * (t * (t - 0.5 / LJ_SIGMA_SQ**3)))
    return g * dx, g * dy, g * dz


def own_rows(data_ref, turns, start, rows=8):
    def spread(row):
        return jnp.broadcast_to(row, (rows, CLUSTER))

    columns = pl.ds(start, CLUSTER)
    xyz = [spread(turns[i : i + 1, columns].astype(jnp.int32)) for i in range(3)]
    q = spread(data_ref[3:4, columns] * (2.0 * COULOMB))
    w = spread(data_ref[4:5, columns] * (48.0 * LJ_DEPTH * LJ_SIGMA_SQ**6))
    return (*xyz, q, w)


def write_halo(data, lists_ref, low_ref, high_ref):
    lane = lax.broadcasted_iota(jnp.int32, (8, CLUSTER), 1)
    for row, out_ref in ((0, low_ref), (1, high_ref)):
        for k in range(HALO // CLUSTER):
            columns = slice(k * CLUSTER, (k + 1) * CLUSTER)
            index = jnp.broadcast_to(lists_ref[0, row : row + 1, columns] & (CLUSTER - 1), (8, CLUSTER))
            first = data[:, 2 * k * CLUSTER : (2 * k + 1) * CLUSTER]
            second = data[:, (2 * k + 1) * CLUSTER : (2 * k + 2) * CLUSTER]
            out_ref[:, columns] = jnp.where(
                lane < CLUSTER // 2,
                jnp.take_along_axis(first, index, axis=1, mode="promise_in_bounds"),
                jnp.take_along_axis(second, index, axis=1, mode="promise_in_bounds"),
            )


def spread_kernel(
    lam_ref, cells_hbm, off_hbm, vel_hbm, charge_hbm, coup_hbm, mass_hbm, lists_hbm, slab_hbm, flag_hbm,
    out_ref, data_ref, move_ref, low_ref, high_ref, mixed_high, mixed_low,
    cells_ref, off_ref, vel_ref, charge_ref, coup_ref, mass_ref, lists_ref, slab_ref, flag_ref, arrived,
):
    copies = [
        pltpu.make_async_copy(source, target, arrived.at[i])
        for i, (source, target) in enumerate(
            (
                (cells_hbm, cells_ref), (off_hbm, off_ref), (vel_hbm, vel_ref), (charge_hbm, charge_ref),
                (coup_hbm, coup_ref), (mass_hbm, mass_ref), (lists_hbm, lists_ref), (slab_hbm, slab_ref),
                (flag_hbm, flag_ref),
            )
        )
    ]
    for copy in copies:
        copy.start()
    for copy in copies:
        copy.wait()
    weight = 1.0 - lam_ref[0] * coup_ref[...]
    charge = charge_ref[...] * weight

    for i in range(3):
        cell = cells_ref[i].astype(F32)
        move_ref[i : i + 1, :] = off_ref[i]
        move_ref[3 + i : 4 + i, :] = cell
        move_ref[8 + i : 9 + i, :] = vel_ref[i]
        data_ref[i : i + 1, :] = cell + off_ref[i]
    move_ref[6:7, :] = jnp.broadcast_to(flag_ref[0:1, 0:1].astype(F32), (1, A_DEV))
    move_ref[7:8, :] = jnp.broadcast_to(flag_ref[0:1, 1:2].astype(F32), (1, A_DEV))
    move_ref[11:16, :] = jnp.zeros((5, A_DEV), F32)
    data_ref[3:4, :] = charge
    data_ref[4:5, :] = weight
    data_ref[5:6, :] = mass_ref[...]
    data_ref[6:8, :] = jnp.zeros((2, A_DEV), F32)
    write_halo(data_ref[...], lists_ref, low_ref, high_ref)

    off = move_ref[0:3, :]
    cells = [cells_ref[i] for i in range(3)]
    weights, _ = spline_set(off)
    row = iota_rows(16, A_DEV)
    plane = jnp.where(row < 8, row, 8 + (row & 3))
    x_table = chosen(plane - (cells[0] & 7), [m[0:1] for m in weights]) * charge
    z_table = chosen((iota_rows(MODES, A_DEV) - cells[2]) & (MODES - 1), [m[2:3] for m in weights])
    z_modes = jnp.dot(slab_ref[...], z_table, precision=HIGHEST, preferred_element_type=F32)
    y_table = chosen((iota_rows(K, A_DEV) - cells[1]) & (K - 1), [m[1:2] for m in weights])

    near, far = x_table[0:8], x_table[8:16]
    upper = iota_rows(8, A_DEV) < 4
    for i in range(0, N_DOM, 2):
        pieces = []
        for k in (i, i + 1):
            first = jnp.broadcast_to(z_modes[2 * k : 2 * k + 1], (8, A_DEV))
            second = jnp.broadcast_to(z_modes[2 * k + 1 : 2 * k + 2], (8, A_DEV))
            pieces += [near * first, near * second, far * jnp.where(upper, first, second)]
        high, low = split(jnp.concatenate(pieces, axis=0))
        mixed_high[i * SLAB : (i + 2) * SLAB, :] = high
        mixed_low[i * SLAB : (i + 2) * SLAB, :] = low
    out_ref[...] = dot3((mixed_high[...], mixed_low[...]), split(y_table), (((1,), (1,)), ((), ())))


def mesh_kernel(grid_ref, gain_ref, basis_ref, below_ref, above_ref, out_ref, block):
    del below_ref, above_ref
    top = iota_rows(8, K) < 4
    for e in range(N_DOM):
        spill = grid_ref[((e - 1) % N_DOM) * SLAB + 16 : ((e - 1) % N_DOM) * SLAB + 24, :]
        turned = pltpu.roll(spill, 4, 0)
        block[8 * e : 8 * e + 8, :] = grid_ref[e * SLAB : e * SLAB + 8, :] + jnp.where(top, spill, 0.0)
        block[K + 8 * e : K + 8 * e + 8, :] = grid_ref[e * SLAB + 8 : e * SLAB + 16, :] + jnp.where(top, turned, 0.0)
    basis = (basis_ref[0:K, :], basis_ref[K : 2 * K, :])
    turned_basis = (basis_ref[2 * K : 3 * K, :], basis_ref[3 * K : 4 * K, :])
    along_y = dot3(split(block[...]), turned_basis)
    for mode in range(2):
        part = split(along_y[mode * K : (mode + 1) * K])
        scaled = dot3(basis, part) * gain_ref[mode]
        block[mode * K : (mode + 1) * K, :] = dot3(turned_basis, split(scaled))
    block[...] = dot3(split(block[...]), basis)
    for e in range(N_DOM):
        following = 8 * ((e + 1) % N_DOM)
        out_ref[e * SLAB : e * SLAB + 8, :] = block[8 * e : 8 * e + 8, :]
        out_ref[e * SLAB + 8 : e * SLAB + 16, :] = block[K + 8 * e : K + 8 * e + 8, :]
        out_ref[e * SLAB + 16 : e * SLAB + 24, :] = jnp.where(
            top,
            block[following : following + 8, :],
            pltpu.roll(block[K + following : K + following + 8, :], 4, 0),
        )


def write_gain(mode_weights_ref, rows_ref, lanes_ref, gain_ref):
    dom = lax.axis_index("dom")
    square_y, factor_y = lanes_ref[0:1, :], lanes_ref[1:2, :]
    scale = COULOMB / (math.pi * K)
    first = dom
    second = jnp.where(dom == 0, MODES // 2, dom)

    def totals(square):
        one = jnp.zeros_like(square)
        two = jnp.zeros_like(square)
        for k in range(K // 2 + 1):
            whole = square + (k / K) ** 2
            inverse = 1.0 / whole if k else jnp.where(whole > 0.0, 1.0 / jnp.where(whole > 0.0, whole, 1.0), 0.0)
            one = one + inverse * mode_weights_ref[first, k]
            two = two + inverse * mode_weights_ref[second, k]
        return one, two

    def block(start):
        rows = pl.ds(start, 8)
        square = jnp.broadcast_to(rows_ref[rows, 0:1], (8, K)) + square_y
        factor = jnp.broadcast_to(rows_ref[rows, 1:2], (8, K)) * factor_y * scale
        one, two = totals(square)
        return one * factor, two * factor

    def step(b, carry):
        start = pl.multiple_of(b * 8, 8)
        one, two = block(start)
        gain_ref[0, pl.ds(start, 8), :] = one
        gain_ref[1, pl.ds(start, 8), :] = two
        gain_ref[0, pl.ds(start + K // 2, 8), :] = one
        gain_ref[1, pl.ds(start + K // 2, 8), :] = two
        return carry

    lax.fori_loop(0, 8, step, 0)
    one, two = block(K // 2)
    gain_ref[0, K // 2 : K // 2 + 1, :] = one[0:1]
    gain_ref[1, K // 2 : K // 2 + 1, :] = two[0:1]


def listed(tiles_ref, row, cluster):
    count = jnp.int32(0)
    for slot in range(1, 4):
        count = count + jnp.where(tiles_ref[slot, 0, row] == cluster, 1, 0)
    return count.astype(F32)


def own_forces(lam_ref, tiles_ref, data_ref, force_ref, turns, near, sides, columns, places, factors, first, last):
    turns[...] = fixed_turns(data_ref[0:3, :])
    near[...] = jnp.zeros_like(near)
    floor_value = SOFT_FLOOR + SOFT_SCALE * lam_ref[0]
    for b in range(first, last):
        lanes = slice(b * CLUSTER, (b + 1) * CLUSTER)
        columns[lanes, :] = jnp.concatenate([turns[:, lanes], data_ref[3:8, lanes]], axis=0).T

    def one_cluster(b, carry):
        start = pl.multiple_of(b * CLUSTER, CLUSTER)
        for j in range(3):
            a = b if j == 0 else (b + j) % CLUSTERS
            own = own_rows(data_ref, turns, pl.multiple_of(a * CLUSTER, CLUSTER))
            total = [jnp.zeros((8, CLUSTER), F32) for _ in range(3)]
            back = listed(tiles_ref, b, a) if j else None
            for chunk in range(CLUSTER // 8):
                here = slice(chunk * 8, chunk * 8 + 8)
                rows = pl.ds(pl.multiple_of(start + chunk * 8, 8), 8)
                if j == 0:
                    part = columns[rows, :]
                    other = [jnp.broadcast_to(part[:, i : i + 1], (8, CLUSTER)) for i in range(5)]
                    other[:3] = [x.astype(jnp.int32) for x in other[:3]]
                    for i in range(3):
                        places[i, here, :] = other[i]
                    for i in range(2):
                        factors[i, here, :] = other[3 + i]
                else:
                    other = [places[i, here, :] for i in range(3)] + [factors[i, here, :] for i in range(2)]
                terms = pair_terms(own, other, floor_value)
                total = [p + q for p, q in zip(total, terms)]
                if j:
                    for i in range(3):
                        sides[3 * j - 3 + i, rows, :] = back * terms[i]
            rows = pl.ds(pl.multiple_of(a * 8, 8), 8)
            for i in range(3):
                near[i, rows, :] = near[i, rows, :] + (listed(tiles_ref, a, b) * total[i] if j else total[i])
        return carry

    lax.fori_loop(first, last, one_cluster, 0)
    force_ref[...] = jnp.zeros_like(force_ref)
    ones = jnp.ones((8, CLUSTER), BF16)
    for c in range(CLUSTERS):
        lanes = slice(c * CLUSTER, (c + 1) * CLUSTER)
        for i in range(3):
            force_ref[i : i + 1, lanes] = SPAN * jnp.sum(near[i, c * 8 : (c + 1) * 8, :], axis=0, keepdims=True)
    rows = slice(first * CLUSTER, last * CLUSTER)
    for i in range(3):
        total = jnp.zeros((8, (last - first) * CLUSTER), F32)
        for part in split(sides[i, rows, :] + sides[3 + i, rows, :]):
            total = total + lax.dot_general(ones, part, (((1,), (1,)), ((), ())), preferred_element_type=F32)
        force_ref[i : i + 1, rows] = force_ref[i : i + 1, rows] - SPAN * total[0:1]


def own_kernel(lam_ref, tiles_ref, data_ref, force_ref, turns, near, sides, *kept):
    own_forces(lam_ref, tiles_ref, data_ref, force_ref, turns, near, sides, *kept, 0, CLUSTERS)


def gain_kernel(
    lam_ref, tiles_ref, weights_ref, data_ref, rows_ref, lanes_ref, force_ref, gain_ref, turns, near, sides, *kept
):
    write_gain(weights_ref, rows_ref, lanes_ref, gain_ref)
    own_forces(lam_ref, tiles_ref, data_ref, force_ref, turns, near, sides, *kept, 0, CLUSTERS // 2)


def add_halo_forces(lam_ref, data_ref, below_ref, above_ref, partial_ref, force_ref, turns):
    turns[...] = fixed_turns(data_ref[0:3, :])
    floor_value = SOFT_FLOOR + SOFT_SCALE * lam_ref[0]

    def one_pair(k, carry):
        start = pl.multiple_of(k * CLUSTER, CLUSTER)
        starts = [pl.multiple_of(k * (2 * CLUSTER), CLUSTER), pl.multiple_of(k * (2 * CLUSTER) + CLUSTER, CLUSTER)]
        owns = [own_rows(data_ref, turns, s) for s in starts]
        totals = [[jnp.zeros((8, CLUSTER), F32) for _ in range(3)] for _ in range(2)]
        for source in (below_ref, above_ref):
            block = source[:, pl.ds(start, CLUSTER)]
            stack = jnp.where(iota_rows(8, CLUSTER) < 3, fixed_turns(block), block)
            turned = stack.T
            for chunk in range(CLUSTER // 8):
                part = turned[chunk * 8 : chunk * 8 + 8]
                other = [jnp.broadcast_to(part[:, i : i + 1], (8, CLUSTER)) for i in range(5)]
                other[:3] = [x.astype(jnp.int32) for x in other[:3]]
                for j in range(2):
                    terms = pair_terms(owns[j], other, floor_value)
                    totals[j] = [a + b for a, b in zip(totals[j], terms)]
        for j in range(2):
            lanes = pl.ds(starts[j], CLUSTER)
            for i in range(3):
                force_ref[i : i + 1, lanes] = partial_ref[i : i + 1, lanes] + SPAN * jnp.sum(
                    totals[j][i], axis=0, keepdims=True
                )
        return carry

    lax.fori_loop(0, HALO // CLUSTER, one_pair, 0)


def rest_kernel(
    lam_ref, tiles_ref, data_ref, below_ref, above_ref, partial_ref, move_ref, slab_ref,
    force_ref, y_high, y_low, z_ref, x_ref, second, turns, near, sides, *kept
):
    write_tables(move_ref, slab_ref, y_high, y_low, z_ref, x_ref)
    own_forces(lam_ref, tiles_ref, data_ref, second, turns, near, sides, *kept, CLUSTERS // 2, CLUSTERS)
    second[...] = second[...] + partial_ref[...]
    force_ref[...] = jnp.zeros_like(force_ref)
    add_halo_forces(lam_ref, data_ref, below_ref, above_ref, second, force_ref, turns)


def advance(force, kicks, data_ref, move_ref, lists_ref, data_out, move_out, low_ref, high_ref):
    mass = data_ref[5:6, :]
    velocity = move_ref[8:11, :]
    for _ in range(kicks):
        velocity = velocity + 0.5 * STEP_DT * force * mass
    off = move_ref[0:3, :] + STEP_DT * velocity
    move_out[...] = move_ref[...]
    move_out[0:3, :] = off
    move_out[8:11, :] = velocity
    data_out[...] = data_ref[...]
    data_out[0:3, :] = move_ref[3:6, :] + off
    write_halo(data_out[...], lists_ref, low_ref, high_ref)


def write_tables(move_ref, slab_ref, y_high, y_low, z_ref, x_ref):
    off = move_ref[0:3, :]
    cells = move_ref[3:6, :].astype(jnp.int32)
    weights, slopes = spline_set(off)
    row = iota_rows(16, A_DEV)
    reach = jnp.where(row < 8, row, 8 + (row & 3)) - (cells[0:1] & 7)
    x_ref[0:16, :] = chosen(reach, [m[0:1] for m in weights])
    x_ref[16:32, :] = chosen(reach, [m[0:1] for m in slopes])
    reach = (iota_rows(MODES, A_DEV) - cells[2:3]) & (MODES - 1)
    for i, rows in enumerate((weights, slopes)):
        table = chosen(reach, [m[2:3] for m in rows])
        z_ref[i * MODES : (i + 1) * MODES, :] = jnp.dot(
            slab_ref[...], table, precision=HIGHEST, preferred_element_type=F32
        )
    for c in range(CLUSTERS):
        lanes = slice(c * CLUSTER, (c + 1) * CLUSTER)
        reach = (iota_rows(K, CLUSTER) - cells[1:2, lanes]) & (K - 1)
        for i, rows in enumerate((weights, slopes)):
            target = slice((2 * c + i) * CLUSTER, (2 * c + i + 1) * CLUSTER)
            y_high[:, target], y_low[:, target] = split(chosen(reach, [m[1:2, lanes] for m in rows]))


def gather_kernel(
    pot_ref, data_ref, move_ref, short_ref, lists_ref, y_high, y_low, z_ref, x_ref,
    long_ref, data_out, move_out, low_ref, high_ref, force,
):
    charge = data_ref[3:4, :]
    potential = split(pot_ref[...])
    upper = iota_rows(8, CLUSTER) < 4
    for c in range(CLUSTERS):
        lanes = slice(c * CLUSTER, (c + 1) * CLUSTER)
        both = slice(2 * c * CLUSTER, (2 * c + 2) * CLUSTER)
        along = dot3(potential, (y_high[:, both], y_low[:, both]))
        value, tilt = along[:, :CLUSTER], along[:, CLUSTER:]
        sums = [[jnp.zeros((8, CLUSTER), F32) for _ in range(2)] for _ in range(3)]
        for i in range(N_DOM):
            pairs = []
            for k in (2 * i, MODES + 2 * i):
                first = jnp.broadcast_to(z_ref[k : k + 1, lanes], (8, CLUSTER))
                second = jnp.broadcast_to(z_ref[k + 1 : k + 2, lanes], (8, CLUSTER))
                pairs.append((first, second, jnp.where(upper, first, second)))
            for which, (source, table) in enumerate(((value, 0), (tilt, 0), (value, 1))):
                block = source[i * SLAB : (i + 1) * SLAB]
                first, second, mixed = pairs[table]
                sums[which][0] = sums[which][0] + (first * block[0:8] + second * block[8:16])
                sums[which][1] = sums[which][1] + mixed * block[16:24]
        for i in range(3):
            k = 16 if i == 0 else 0
            near = x_ref[k : k + 8, lanes] * sums[i][0] + x_ref[k + 8 : k + 16, lanes] * sums[i][1]
            force[i : i + 1, lanes] = -charge[:, lanes] * jnp.sum(near, axis=0, keepdims=True)
    long_ref[...] = jnp.zeros_like(long_ref)
    long_ref[0:3, :] = force[0:3, :]
    advance(
        short_ref[0:3, :] + force[0:3, :], 1, data_ref, move_ref, lists_ref, data_out, move_out, low_ref, high_ref
    )


def halo_step_kernel(
    lam_ref, data_ref, below_ref, above_ref, partial_ref, long_ref, move_ref, lists_ref,
    data_out, move_out, low_ref, high_ref, turns, force,
):
    add_halo_forces(lam_ref, data_ref, below_ref, above_ref, partial_ref, force, turns)
    total = force[0:3, :] + long_ref[0:3, :]
    advance(total, 2, data_ref, move_ref, lists_ref, data_out, move_out, low_ref, high_ref)


def halo_last_kernel(
    lam_ref, data_ref, below_ref, above_ref, partial_ref, long_ref, move_ref, state_ref, turns, force
):
    add_halo_forces(lam_ref, data_ref, below_ref, above_ref, partial_ref, force, turns)
    total = force[0:3, :] + long_ref[0:3, :]
    velocity = move_ref[8:11, :] + 0.5 * STEP_DT * total * data_ref[5:6, :]
    for i in range(3):
        state_ref[i] = move_ref[i : i + 1, :]
        state_ref[3 + i] = velocity[i : i + 1]
        state_ref[6 + i] = move_ref[3 + i : 4 + i, :]
    state_ref[9] = move_ref[6:7, :]


def takes(round_index, here_ref, there_ref):
    window = lax.axis_index("lam")
    lower = window % 2 == round_index % 2
    inside = window + 1 < lax.axis_size("lam")
    return jnp.where(lower, jnp.where(inside, here_ref[9], 0.0), there_ref[9]) == 1.0


def first_trade_kernel(here_ref, there_ref, move_ref, out_ref):
    take = takes(0, here_ref, there_ref)
    for i in range(9):
        out_ref[i] = jnp.where(take, there_ref[i], here_ref[i])
    out_ref[9] = move_ref[7:8, :]


def last_trade_kernel(here_ref, there_ref, cells_ref, off_ref, vel_ref):
    take = takes(1, here_ref, there_ref)
    for i in range(3):
        off_ref[i] = jnp.where(take, there_ref[i], here_ref[i])
        vel_ref[i] = jnp.where(take, there_ref[3 + i], here_ref[3 + i])
        cells_ref[i] = jnp.where(take, there_ref[6 + i], here_ref[6 + i]).astype(jnp.int32)


PLACES = {
    "s": pl.BlockSpec(memory_space=pltpu.SMEM),
    "v": pl.BlockSpec(memory_space=pltpu.VMEM),
    "a": pl.BlockSpec(memory_space=pl.ANY),
}


def call(kernel, ins, outs, scratch=(), cost=0, limit=40):
    return pl.pallas_call(
        kernel,
        out_shape=[jax.ShapeDtypeStruct(shape, dtype) for shape, dtype in outs],
        in_specs=[PLACES[place] for place, _ in ins],
        out_specs=[PLACES["v"]] * len(outs),
        scratch_shapes=list(scratch),
        compiler_params=pltpu.CompilerParams(vmem_limit_bytes=limit * 2**20),
        cost_estimate=pl.CostEstimate(flops=cost, bytes_accessed=200000, transcendentals=0),
    )(*[value for _, value in ins])


def neighbours(low, high):
    size = lax.axis_size("dom")
    below = lax.ppermute(high, "dom", [(i, (i + 1) % size) for i in range(size)])
    above = lax.ppermute(low, "dom", [(i, (i - 1) % size) for i in range(size)])
    return below, above


def traded(state, round_index):
    pairs = []
    for w in range(round_index % 2, lax.axis_size("lam") - 1, 2):
        pairs += [(w, w + 1), (w + 1, w)]
    return lax.ppermute(state, "lam", pairs)


def exchanged(value):
    return lax.all_to_all(value, "dom", split_axis=0, concat_axis=0, tiled=True)


def body(
    cells, offsets, velocities, charges, coupling, inverse_mass, lambdas, tile_lists, halo_lists, accept_flags
):
    wide = ((8, A_DEV), F32)
    moving = ((16, A_DEV), F32)
    border = ((8, HALO), F32)
    turns = pltpu.VMEM((3, A_DEV), F32)
    pair_scratch = [
        turns, pltpu.VMEM((3, CLUSTERS * 8, CLUSTER), F32), pltpu.VMEM((6, A_DEV, CLUSTER), F32),
        pltpu.VMEM((A_DEV, 8), F32), pltpu.VMEM((3, CLUSTER, CLUSTER), jnp.int32), pltpu.VMEM((2, CLUSTER, CLUSTER), F32),
    ]
    spare = pltpu.VMEM((8, A_DEV), F32)
    tiles = jnp.transpose(tile_lists, (2, 0, 1))
    slab = jnp.asarray(slab_basis())
    square, factor = plane_gain()
    gain_rows = np.zeros((K, 8), np.float32)
    gain_rows[:, 0], gain_rows[:, 1] = square, factor
    gain_lanes = np.zeros((8, K), np.float32)
    gain_lanes[0], gain_lanes[1] = square, factor

    triple = (3, 1, A_DEV)

    def by_row(x):
        return jnp.transpose(x, (1, 0, 2))


    grid, data, move, low, high = call(
        spread_kernel,
        [
            ("s", lambdas), ("a", by_row(cells)), ("a", by_row(offsets)), ("a", by_row(velocities)),
            ("a", charges[None]), ("a", coupling[None]), ("a", inverse_mass[None]), ("a", halo_lists), ("a", slab),
            ("a", accept_flags.T),
        ],
        [((ROWS, K), F32), wide, moving, border, border],
        [
            pltpu.VMEM((ROWS, A_DEV), BF16), pltpu.VMEM((ROWS, A_DEV), BF16),
            pltpu.VMEM((3, 1, A_DEV), jnp.int32), pltpu.VMEM((3, 1, A_DEV), F32), pltpu.VMEM((3, 1, A_DEV), F32),
            pltpu.VMEM((1, A_DEV), F32), pltpu.VMEM((1, A_DEV), F32), pltpu.VMEM((1, A_DEV), F32),
            pltpu.VMEM((1, 2, HALO), jnp.int32), pltpu.VMEM((MODES, MODES), F32), pltpu.VMEM((1, 2), jnp.int32),
            pltpu.SemaphoreType.DMA((9,)),
        ],
        limit=60,
    )
    grid = exchanged(grid)
    below, above = neighbours(low, high)
    short, gain = call(
        gain_kernel,
        [
            ("s", lambdas), ("s", tiles), ("s", jnp.asarray(slab_weights())), ("v", data),
            ("v", jnp.asarray(gain_rows)), ("v", jnp.asarray(gain_lanes)),
        ],
        [wide, ((2, K, K), F32)],
        pair_scratch,
        cost=2 * 10**9,
    )
    (potential,) = call(
        mesh_kernel,
        [("v", grid), ("v", gain), ("v", jnp.asarray(basis_table())), ("a", below), ("a", above)],
        [((ROWS, K), F32)],
        [pltpu.VMEM((2 * K, K), F32)],
    )
    potential = exchanged(potential)
    short, *tables = call(
        rest_kernel,
        [
            ("s", lambdas), ("s", tiles), ("v", data), ("v", below), ("v", above), ("v", short), ("v", move), ("v", slab),
        ],
        [wide, *[((K, 2 * A_DEV), BF16)] * 2, ((2 * MODES, A_DEV), F32), ((32, A_DEV), F32)],
        [spare, *pair_scratch],
        cost=2 * 10**9,
    )
    far, data, move, low, high = call(
        gather_kernel,
        [("v", potential), ("v", data), ("v", move), ("v", short), ("v", halo_lists), *(("v", x) for x in tables)],
        [wide, wide, moving, border, border],
        [spare],
    )

    def own_call(data):
        (partial,) = call(
            own_kernel, [("s", lambdas), ("s", tiles), ("v", data)], [wide], pair_scratch, cost=2 * 10**9
        )
        return partial

    below, above = neighbours(low, high)
    short = own_call(data)
    data, move, low, high = call(
        halo_step_kernel,
        [
            ("s", lambdas), ("v", data), ("v", below), ("v", above), ("v", short), ("v", far), ("v", move),
            ("v", halo_lists),
        ],
        [wide, moving, border, border],
        [turns, spare],
    )
    below, above = neighbours(low, high)
    short = own_call(data)
    (state,) = call(
        halo_last_kernel,
        [
            ("s", lambdas), ("v", data), ("v", below), ("v", above), ("v", short), ("v", far), ("v", move),
        ],
        [((10, 1, A_DEV), F32)],
        [turns, spare],
    )
    (state,) = call(
        first_trade_kernel, [("v", state), ("v", traded(state, 0)), ("v", move)], [((10, 1, A_DEV), F32)]
    )
    out = call(
        last_trade_kernel,
        [("v", state), ("v", traded(state, 1))],
        [(triple, jnp.int32), (triple, F32), (triple, F32)],
    )
    return tuple(by_row(x) for x in out)


def solution(mesh):
    in_specs = (
        P("lam", None, "dom"),
        P("lam", None, "dom"),
        P("lam", None, "dom"),
        P("dom"),
        P("dom"),
        P("dom"),
        P("lam"),
        P("lam", "dom", None),
        P("lam", "dom", None),
        P(None, "lam"),
    )
    out_specs = (P("lam", None, "dom"), P("lam", None, "dom"), P("lam", None, "dom"))
    return jax.shard_map(body, mesh=mesh, in_specs=in_specs, out_specs=out_specs, check_vma=False)
```

```python
import functools
import math

import jax
import jax.numpy as jnp
import ml_dtypes
import numpy as np
from jax import lax
from jax.experimental import pallas as pl
from jax.experimental.pallas import tpu as pltpu
from jax.sharding import PartitionSpec as P

K = 128
CLUSTER = 128
N_DOM = 16
A_DEV = 1024
CLUSTERS = 8
HALO = 512
MODES = 32
SLAB = 24
ROWS = N_DOM * SLAB

EWALD_BETA = 0.5
COULOMB = 20.0
LJ_DEPTH = 1.0
LJ_SIGMA_SQ = 0.49
SOFT_SCALE = 0.5
SOFT_FLOOR = 0.5
STEP_DT = 0.25

F32 = jnp.float32
BF16 = jnp.bfloat16
HIGHEST = lax.Precision.HIGHEST

TURN = 2.0**32
SPAN_SQ = 2.0**-50
SPAN = 2.0**-25

SCREEN = (
    -0.0818439527,
    0.648023047,
    -2.23331568,
    4.38709699,
    -5.37737017,
    4.16223694,
    -1.81397109,
    0.0540053844,
    0.5630337,
    -5.2346482e-05,
    0.282096019,
)


def real_basis(count):
    half = count // 2
    place = np.arange(count)
    rows = []
    for k in range(half + 1):
        scale = math.sqrt((1.0 if k in (0, half) else 2.0) / count)
        rows.append(scale * np.cos(2.0 * np.pi * (k * place % count) / count))
    for k in range(1, half):
        rows.append(math.sqrt(2.0 / count) * np.sin(2.0 * np.pi * (k * place % count) / count))
    return np.stack(rows)


def halves(table):
    high = table.astype(np.float32).astype(ml_dtypes.bfloat16)
    low = (table - high.astype(np.float64)).astype(np.float32).astype(ml_dtypes.bfloat16)
    return high, low


def basis_table():
    basis = real_basis(K)
    high, low = halves(basis)
    return np.concatenate([high, low, high.T, low.T], axis=0)


def slab_basis():
    basis = real_basis(MODES)
    order = [0, MODES // 2]
    for k in range(1, MODES // 2):
        order += [k, MODES // 2 + k]
    return basis[np.array(order)].astype(np.float32)


def spline_modulus(k):
    return (3.0 / (2.0 + np.cos(2.0 * np.pi * k / K))) ** 2


def slab_weights():
    k = np.arange(K // 2 + 1)
    delta = np.arange(-MODES // 2 + 1, MODES // 2 + 1)
    folded = np.where((k == 0) | (k == K // 2), 1.0, 2.0)
    own = folded * np.exp(-np.pi**2 * (k / K) ** 2 / EWALD_BETA**2) * spline_modulus(k)
    rows = []
    for j in range(MODES // 2 + 1):
        window = np.cos(2 * np.pi * k[:, None] * delta / K) * np.cos(2 * np.pi * j * delta / MODES)
        rows.append(own * window.sum(axis=1))
    return np.stack(rows).astype(np.float32)


def plane_gain():
    k = np.concatenate([np.arange(K // 2 + 1), np.arange(1, K // 2)])
    square = (k / K) ** 2
    factor = np.exp(-np.pi**2 * square / EWALD_BETA**2) * spline_modulus(k)
    return square.astype(np.float32), factor.astype(np.float32)


def split(x):
    high = x.astype(BF16)
    return high, (x - high.astype(F32)).astype(BF16)


def dot3(left, right, dims=(((1,), (0,)), ((), ()))):
    lh, ll = left
    rh, rl = right
    dot = functools.partial(lax.dot_general, dimension_numbers=dims, preferred_element_type=F32)
    return dot(lh, rh) + (dot(lh, rl) + dot(ll, rh))


def spline_set(u):
    v = 1.0 - u
    u2 = u * u
    u3 = u2 * u
    weights = (
        v * v * v / 6.0,
        (3.0 * u3 - 6.0 * u2 + 4.0) / 6.0,
        (-3.0 * u3 + 3.0 * u2 + 3.0 * u + 1.0) / 6.0,
        u3 / 6.0,
    )
    slopes = (-0.5 * v * v, 1.5 * u2 - 2.0 * u, -1.5 * u2 + u + 0.5, 0.5 * u2)
    return weights, slopes


def chosen(distance, rows):
    out = jnp.where(distance == 3, rows[3], 0.0)
    for k in (2, 1, 0):
        out = jnp.where(distance == k, rows[k], out)
    return out


def iota_rows(rows, columns):
    return lax.broadcasted_iota(jnp.int32, (rows, columns), 0)


def fixed_turns(x):
    t = x * (1.0 / K)
    f = t - jnp.floor(t + 0.5)
    return jnp.maximum(f, -0.5) * TURN


def pair_terms(own, other, floor_value):
    ax, ay, az, qa, wa = own
    bx, by, bz, qb, wb = other
    dx = (ax - bx).astype(F32)
    dy = (ay - by).astype(F32)
    dz = (az - bz).astype(F32)
    s = (dx * dx + dy * dy + dz * dz) * SPAN_SQ + floor_value
    w = lax.rsqrt(s)
    u = w * w
    screen = jnp.full_like(w, SCREEN[0])
    for c in SCREEN[1:]:
        screen = screen * w + c
    gauss = jnp.exp2(s * (-(EWALD_BETA**2) * math.log2(math.e)))
    t = u * u * u
    g = u * ((qa * qb) * (gauss * screen) + (wa * wb) * (t * (t - 0.5 / LJ_SIGMA_SQ**3)))
    return g * dx, g * dy, g * dz


def own_rows(data_ref, turns, start, rows=8):
    def spread(row):
        return jnp.broadcast_to(row, (rows, CLUSTER))

    columns = pl.ds(start, CLUSTER)
    xyz = [spread(turns[i : i + 1, columns].astype(jnp.int32)) for i in range(3)]
    q = spread(data_ref[3:4, columns] * (2.0 * COULOMB))
    w = spread(data_ref[4:5, columns] * (48.0 * LJ_DEPTH * LJ_SIGMA_SQ**6))
    return (*xyz, q, w)


def write_halo(data, lists, low_ref, high_ref):
    lane = lax.broadcasted_iota(jnp.int32, (8, CLUSTER), 1)
    for row, out_ref in ((0, low_ref), (1, high_ref)):
        for k in range(HALO // CLUSTER):
            columns = slice(k * CLUSTER, (k + 1) * CLUSTER)
            start = row * HALO + k * CLUSTER
            index = jnp.broadcast_to(lists[:, start : start + CLUSTER].astype(jnp.int32), (8, CLUSTER))
            first = data[:, 2 * k * CLUSTER : (2 * k + 1) * CLUSTER]
            second = data[:, (2 * k + 1) * CLUSTER : (2 * k + 2) * CLUSTER]
            out_ref[:, columns] = jnp.where(
                lane < CLUSTER // 2,
                jnp.take_along_axis(first, index, axis=1, mode="promise_in_bounds"),
                jnp.take_along_axis(second, index, axis=1, mode="promise_in_bounds"),
            )


def spread_kernel(
    lam_ref, cells_hbm, off_hbm, vel_hbm, charge_hbm, coup_hbm, mass_hbm, lists_hbm, slab_hbm, flag_hbm,
    out_ref, data_ref, move_ref, low_ref, high_ref, mixed_high, mixed_low,
    cells_ref, off_ref, vel_ref, charge_ref, coup_ref, mass_ref, lists_ref, slab_ref, flag_ref, arrived,
):
    copies = [
        pltpu.make_async_copy(source, target, arrived.at[i])
        for i, (source, target) in enumerate(
            (
                (cells_hbm, cells_ref), (off_hbm, off_ref), (vel_hbm, vel_ref), (charge_hbm, charge_ref),
                (coup_hbm, coup_ref), (mass_hbm, mass_ref), (lists_hbm, lists_ref), (slab_hbm, slab_ref),
                (flag_hbm, flag_ref),
            )
        )
    ]
    for copy in copies:
        copy.start()
    for copy in copies:
        copy.wait()
    weight = 1.0 - lam_ref[0] * coup_ref[...]
    charge = charge_ref[...] * weight

    for i in range(3):
        cell = cells_ref[i].astype(F32)
        move_ref[i : i + 1, :] = off_ref[i]
        move_ref[3 + i : 4 + i, :] = cell
        move_ref[8 + i : 9 + i, :] = vel_ref[i]
        data_ref[i : i + 1, :] = cell + off_ref[i]
    move_ref[6:7, :] = jnp.broadcast_to(flag_ref[0:1, 0:1].astype(F32), (1, A_DEV))
    move_ref[7:8, :] = jnp.broadcast_to(flag_ref[0:1, 1:2].astype(F32), (1, A_DEV))
    move_ref[11:12, 0:HALO] = (lists_ref[0, 0:1, :] & (CLUSTER - 1)).astype(F32)
    move_ref[11:12, HALO : 2 * HALO] = (lists_ref[0, 1:2, :] & (CLUSTER - 1)).astype(F32)
    move_ref[12:16, :] = jnp.zeros((4, A_DEV), F32)
    data_ref[3:4, :] = charge
    data_ref[4:5, :] = weight
    data_ref[5:6, :] = mass_ref[...]
    data_ref[6:8, :] = jnp.zeros((2, A_DEV), F32)
    write_halo(data_ref[...], move_ref[11:12, :], low_ref, high_ref)

    off = move_ref[0:3, :]
    cells = [cells_ref[i] for i in range(3)]
    weights, _ = spline_set(off)
    row = iota_rows(16, A_DEV)
    plane = jnp.where(row < 8, row, 8 + (row & 3))
    x_table = chosen(plane - (cells[0] & 7), [m[0:1] for m in weights]) * charge
    z_table = chosen((iota_rows(MODES, A_DEV) - cells[2]) & (MODES - 1), [m[2:3] for m in weights])
    z_modes = jnp.dot(slab_ref[...], z_table, precision=HIGHEST, preferred_element_type=F32)
    y_table = chosen((iota_rows(K, A_DEV) - cells[1]) & (K - 1), [m[1:2] for m in weights])

    near, far = x_table[0:8], x_table[8:16]
    upper = iota_rows(8, A_DEV) < 4
    for i in range(0, N_DOM, 2):
        pieces = []
        for k in (i, i + 1):
            first = jnp.broadcast_to(z_modes[2 * k : 2 * k + 1], (8, A_DEV))
            second = jnp.broadcast_to(z_modes[2 * k + 1 : 2 * k + 2], (8, A_DEV))
            pieces += [near * first, near * second, far * jnp.where(upper, first, second)]
        high, low = split(jnp.concatenate(pieces, axis=0))
        mixed_high[i * SLAB : (i + 2) * SLAB, :] = high
        mixed_low[i * SLAB : (i + 2) * SLAB, :] = low
    out_ref[...] = dot3((mixed_high[...], mixed_low[...]), split(y_table), (((1,), (1,)), ((), ())))


def mesh_kernel(grid_ref, gain_ref, basis_ref, below_ref, above_ref, out_ref, block):
    del below_ref, above_ref
    top = iota_rows(8, K) < 4
    for e in range(N_DOM):
        spill = grid_ref[((e - 1) % N_DOM) * SLAB + 16 : ((e - 1) % N_DOM) * SLAB + 24, :]
        turned = pltpu.roll(spill, 4, 0)
        block[8 * e : 8 * e + 8, :] = grid_ref[e * SLAB : e * SLAB + 8, :] + jnp.where(top, spill, 0.0)
        block[K + 8 * e : K + 8 * e + 8, :] = grid_ref[e * SLAB + 8 : e * SLAB + 16, :] + jnp.where(top, turned, 0.0)
    basis = (basis_ref[0:K, :], basis_ref[K : 2 * K, :])
    turned_basis = (basis_ref[2 * K : 3 * K, :], basis_ref[3 * K : 4 * K, :])
    along_y = dot3(split(block[...]), turned_basis)
    for mode in range(2):
        part = split(along_y[mode * K : (mode + 1) * K])
        scaled = dot3(basis, part) * gain_ref[mode]
        block[mode * K : (mode + 1) * K, :] = dot3(turned_basis, split(scaled))
    block[...] = dot3(split(block[...]), basis)
    for e in range(N_DOM):
        following = 8 * ((e + 1) % N_DOM)
        out_ref[e * SLAB : e * SLAB + 8, :] = block[8 * e : 8 * e + 8, :]
        out_ref[e * SLAB + 8 : e * SLAB + 16, :] = block[K + 8 * e : K + 8 * e + 8, :]
        out_ref[e * SLAB + 16 : e * SLAB + 24, :] = jnp.where(
            top,
            block[following : following + 8, :],
            pltpu.roll(block[K + following : K + following + 8, :], 4, 0),
        )


def write_gain(mode_weights_ref, rows_ref, lanes_ref, gain_ref):
    dom = lax.axis_index("dom")
    square_y, factor_y = lanes_ref[0:1, :], lanes_ref[1:2, :]
    scale = COULOMB / (math.pi * K)
    first = dom
    second = jnp.where(dom == 0, MODES // 2, dom)

    def totals(square):
        one = jnp.zeros_like(square)
        two = jnp.zeros_like(square)
        for k in range(K // 2 + 1):
            whole = square + (k / K) ** 2
            inverse = 1.0 / whole if k else jnp.where(whole > 0.0, 1.0 / jnp.where(whole > 0.0, whole, 1.0), 0.0)
            one = one + inverse * mode_weights_ref[first, k]
            two = two + inverse * mode_weights_ref[second, k]
        return one, two

    def block(start):
        rows = pl.ds(start, 8)
        square = jnp.broadcast_to(rows_ref[rows, 0:1], (8, K)) + square_y
        factor = jnp.broadcast_to(rows_ref[rows, 1:2], (8, K)) * factor_y * scale
        one, two = totals(square)
        return one * factor, two * factor

    def step(b, carry):
        start = pl.multiple_of(b * 8, 8)
        one, two = block(start)
        gain_ref[0, pl.ds(start, 8), :] = one
        gain_ref[1, pl.ds(start, 8), :] = two
        gain_ref[0, pl.ds(start + K // 2, 8), :] = one
        gain_ref[1, pl.ds(start + K // 2, 8), :] = two
        return carry

    lax.fori_loop(0, 8, step, 0)
    one, two = block(K // 2)
    gain_ref[0, K // 2 : K // 2 + 1, :] = one[0:1]
    gain_ref[1, K // 2 : K // 2 + 1, :] = two[0:1]


def listed(tiles_ref, row, cluster):
    count = jnp.int32(0)
    for slot in range(1, 4):
        count = count + jnp.where(tiles_ref[slot, 0, row] == cluster, 1, 0)
    return count.astype(F32)


def own_forces(lam_ref, tiles_ref, data_ref, force_ref, turns, near, sides, columns, places, factors, first, last):
    turns[...] = fixed_turns(data_ref[0:3, :])
    near[...] = jnp.zeros_like(near)
    floor_value = SOFT_FLOOR + SOFT_SCALE * lam_ref[0]
    for b in range(first, last):
        lanes = slice(b * CLUSTER, (b + 1) * CLUSTER)
        columns[lanes, :] = jnp.concatenate([turns[:, lanes], data_ref[3:8, lanes]], axis=0).T

    def one_cluster(b, side):
        start = pl.multiple_of(b * CLUSTER, CLUSTER)
        for j in range(3):
            a = b if j == 0 else (b + j) % CLUSTERS
            own = own_rows(data_ref, turns, pl.multiple_of(a * CLUSTER, CLUSTER))
            total = [jnp.zeros((8, CLUSTER), F32) for _ in range(3)]
            back = listed(tiles_ref, b, a) if j else None
            for chunk in range(CLUSTER // 8):
                here = slice(chunk * 8, chunk * 8 + 8)
                rows = pl.ds(pl.multiple_of(start + chunk * 8, 8), 8)
                if j == 0:
                    part = columns[rows, :]
                    other = [jnp.broadcast_to(part[:, i : i + 1], (8, CLUSTER)) for i in range(5)]
                    other[:3] = [x.astype(jnp.int32) for x in other[:3]]
                    for i in range(3):
                        places[3 * side + i, here, :] = other[i]
                    for i in range(2):
                        factors[2 * side + i, here, :] = other[3 + i]
                else:
                    other = [places[3 * side + i, here, :] for i in range(3)]
                    other += [factors[2 * side + i, here, :] for i in range(2)]
                terms = pair_terms(own, other, floor_value)
                total = [p + q for p, q in zip(total, terms)]
                if j:
                    for i in range(3):
                        sides[3 * j - 3 + i, rows, :] = back * terms[i]
            rows = pl.ds(pl.multiple_of(a * 8, 8), 8)
            for i in range(3):
                near[i, rows, :] = near[i, rows, :] + (listed(tiles_ref, a, b) * total[i] if j else total[i])

    def two_clusters(k, carry):
        for side in range(2):
            one_cluster(2 * k + side, side)
        return carry

    lax.fori_loop(first // 2, last // 2, two_clusters, 0)
    force_ref[...] = jnp.zeros_like(force_ref)
    ones = jnp.ones((8, CLUSTER), BF16)
    for c in range(CLUSTERS):
        lanes = slice(c * CLUSTER, (c + 1) * CLUSTER)
        for i in range(3):
            force_ref[i : i + 1, lanes] = SPAN * jnp.sum(near[i, c * 8 : (c + 1) * 8, :], axis=0, keepdims=True)
    rows = slice(first * CLUSTER, last * CLUSTER)
    for i in range(3):
        total = jnp.zeros((8, (last - first) * CLUSTER), F32)
        for part in split(sides[i, rows, :] + sides[3 + i, rows, :]):
            total = total + lax.dot_general(ones, part, (((1,), (1,)), ((), ())), preferred_element_type=F32)
        force_ref[i : i + 1, rows] = force_ref[i : i + 1, rows] - SPAN * total[0:1]


def own_kernel(lam_ref, tiles_ref, data_ref, force_ref, turns, near, sides, *kept):
    own_forces(lam_ref, tiles_ref, data_ref, force_ref, turns, near, sides, *kept, 0, CLUSTERS)


def gain_kernel(
    lam_ref, tiles_ref, weights_ref, data_ref, rows_ref, lanes_ref, force_ref, gain_ref, turns, near, sides, *kept
):
    write_gain(weights_ref, rows_ref, lanes_ref, gain_ref)
    own_forces(lam_ref, tiles_ref, data_ref, force_ref, turns, near, sides, *kept, 0, CLUSTERS // 2)


def add_halo_forces(lam_ref, data_ref, below_ref, above_ref, partial_ref, force_ref, turns):
    turns[...] = fixed_turns(data_ref[0:3, :])
    floor_value = SOFT_FLOOR + SOFT_SCALE * lam_ref[0]

    def one_pair(k, carry):
        start = pl.multiple_of(k * CLUSTER, CLUSTER)
        starts = [pl.multiple_of(k * (2 * CLUSTER), CLUSTER), pl.multiple_of(k * (2 * CLUSTER) + CLUSTER, CLUSTER)]
        owns = [own_rows(data_ref, turns, s) for s in starts]
        totals = [[jnp.zeros((8, CLUSTER), F32) for _ in range(3)] for _ in range(2)]
        for source in (below_ref, above_ref):
            block = source[:, pl.ds(start, CLUSTER)]
            stack = jnp.where(iota_rows(8, CLUSTER) < 3, fixed_turns(block), block)
            turned = stack.T
            for chunk in range(CLUSTER // 8):
                part = turned[chunk * 8 : chunk * 8 + 8]
                other = [jnp.broadcast_to(part[:, i : i + 1], (8, CLUSTER)) for i in range(5)]
                other[:3] = [x.astype(jnp.int32) for x in other[:3]]
                for j in range(2):
                    terms = pair_terms(owns[j], other, floor_value)
                    totals[j] = [a + b for a, b in zip(totals[j], terms)]
        for j in range(2):
            lanes = pl.ds(starts[j], CLUSTER)
            for i in range(3):
                force_ref[i : i + 1, lanes] = partial_ref[i : i + 1, lanes] + SPAN * jnp.sum(
                    totals[j][i], axis=0, keepdims=True
                )
        return carry

    lax.fori_loop(0, HALO // CLUSTER, one_pair, 0)


def rest_kernel(
    lam_ref, tiles_ref, data_ref, below_ref, above_ref, partial_ref, move_ref, slab_ref,
    force_ref, y_high, y_low, z_ref, x_ref, second, turns, near, sides, *kept
):
    write_tables(move_ref, slab_ref, y_high, y_low, z_ref, x_ref)
    own_forces(lam_ref, tiles_ref, data_ref, second, turns, near, sides, *kept, CLUSTERS // 2, CLUSTERS)
    second[...] = second[...] + partial_ref[...]
    force_ref[...] = jnp.zeros_like(force_ref)
    add_halo_forces(lam_ref, data_ref, below_ref, above_ref, second, force_ref, turns)


def advance(force, kicks, data_ref, move_ref, data_out, move_out, low_ref, high_ref):
    mass = data_ref[5:6, :]
    velocity = move_ref[8:11, :]
    for _ in range(kicks):
        velocity = velocity + 0.5 * STEP_DT * force * mass
    off = move_ref[0:3, :] + STEP_DT * velocity
    move_out[...] = move_ref[...]
    move_out[0:3, :] = off
    move_out[8:11, :] = velocity
    data_out[...] = data_ref[...]
    data_out[0:3, :] = move_ref[3:6, :] + off
    write_halo(data_out[...], move_ref[11:12, :], low_ref, high_ref)


def write_tables(move_ref, slab_ref, y_high, y_low, z_ref, x_ref):
    off = move_ref[0:3, :]
    cells = move_ref[3:6, :].astype(jnp.int32)
    weights, slopes = spline_set(off)
    row = iota_rows(16, A_DEV)
    reach = jnp.where(row < 8, row, 8 + (row & 3)) - (cells[0:1] & 7)
    x_ref[0:16, :] = chosen(reach, [m[0:1] for m in weights])
    x_ref[16:32, :] = chosen(reach, [m[0:1] for m in slopes])
    reach = (iota_rows(MODES, A_DEV) - cells[2:3]) & (MODES - 1)
    for i, rows in enumerate((weights, slopes)):
        table = chosen(reach, [m[2:3] for m in rows])
        z_ref[i * MODES : (i + 1) * MODES, :] = jnp.dot(
            slab_ref[...], table, precision=HIGHEST, preferred_element_type=F32
        )
    for c in range(CLUSTERS):
        lanes = slice(c * CLUSTER, (c + 1) * CLUSTER)
        reach = (iota_rows(K, CLUSTER) - cells[1:2, lanes]) & (K - 1)
        for i, rows in enumerate((weights, slopes)):
            target = slice((2 * c + i) * CLUSTER, (2 * c + i + 1) * CLUSTER)
            y_high[:, target], y_low[:, target] = split(chosen(reach, [m[1:2, lanes] for m in rows]))


def gather_kernel(
    pot_ref, data_ref, move_ref, short_ref, y_high, y_low, z_ref, x_ref,
    long_ref, data_out, move_out, low_ref, high_ref, force,
):
    charge = data_ref[3:4, :]
    potential = split(pot_ref[...])
    upper = iota_rows(8, CLUSTER) < 4
    for c in range(CLUSTERS):
        lanes = slice(c * CLUSTER, (c + 1) * CLUSTER)
        both = slice(2 * c * CLUSTER, (2 * c + 2) * CLUSTER)
        along = dot3(potential, (y_high[:, both], y_low[:, both]))
        value, tilt = along[:, :CLUSTER], along[:, CLUSTER:]
        sums = [[jnp.zeros((8, CLUSTER), F32) for _ in range(2)] for _ in range(3)]
        for i in range(N_DOM):
            pairs = []
            for k in (2 * i, MODES + 2 * i):
                first = jnp.broadcast_to(z_ref[k : k + 1, lanes], (8, CLUSTER))
                second = jnp.broadcast_to(z_ref[k + 1 : k + 2, lanes], (8, CLUSTER))
                pairs.append((first, second, jnp.where(upper, first, second)))
            for which, (source, table) in enumerate(((value, 0), (tilt, 0), (value, 1))):
                block = source[i * SLAB : (i + 1) * SLAB]
                first, second, mixed = pairs[table]
                sums[which][0] = sums[which][0] + (first * block[0:8] + second * block[8:16])
                sums[which][1] = sums[which][1] + mixed * block[16:24]
        for i in range(3):
            k = 16 if i == 0 else 0
            near = x_ref[k : k + 8, lanes] * sums[i][0] + x_ref[k + 8 : k + 16, lanes] * sums[i][1]
            force[i : i + 1, lanes] = -charge[:, lanes] * jnp.sum(near, axis=0, keepdims=True)
    long_ref[...] = jnp.zeros_like(long_ref)
    long_ref[0:3, :] = force[0:3, :]
    advance(
        short_ref[0:3, :] + force[0:3, :], 1, data_ref, move_ref, data_out, move_out, low_ref, high_ref
    )


def halo_step_kernel(
    lam_ref, data_ref, below_ref, above_ref, partial_ref, long_ref, move_ref,
    data_out, move_out, low_ref, high_ref, turns, force,
):
    add_halo_forces(lam_ref, data_ref, below_ref, above_ref, partial_ref, force, turns)
    total = force[0:3, :] + long_ref[0:3, :]
    advance(total, 2, data_ref, move_ref, data_out, move_out, low_ref, high_ref)


def halo_last_kernel(
    lam_ref, data_ref, below_ref, above_ref, partial_ref, long_ref, move_ref, state_ref, turns, force
):
    add_halo_forces(lam_ref, data_ref, below_ref, above_ref, partial_ref, force, turns)
    total = force[0:3, :] + long_ref[0:3, :]
    velocity = move_ref[8:11, :] + 0.5 * STEP_DT * total * data_ref[5:6, :]
    for i in range(3):
        state_ref[i] = move_ref[i : i + 1, :]
        state_ref[3 + i] = velocity[i : i + 1]
        state_ref[6 + i] = move_ref[3 + i : 4 + i, :]
    state_ref[9] = move_ref[6:7, :]


def takes(round_index, here_ref, there_ref):
    window = lax.axis_index("lam")
    lower = window % 2 == round_index % 2
    inside = window + 1 < lax.axis_size("lam")
    return jnp.where(lower, jnp.where(inside, here_ref[9], 0.0), there_ref[9]) == 1.0


def first_trade_kernel(here_ref, there_ref, move_ref, out_ref):
    take = takes(0, here_ref, there_ref)
    for i in range(9):
        out_ref[i] = jnp.where(take, there_ref[i], here_ref[i])
    out_ref[9] = move_ref[7:8, :]


def last_trade_kernel(here_ref, there_ref, cells_ref, off_ref, vel_ref):
    take = takes(1, here_ref, there_ref)
    for i in range(3):
        off_ref[i] = jnp.where(take, there_ref[i], here_ref[i])
        vel_ref[i] = jnp.where(take, there_ref[3 + i], here_ref[3 + i])
        cells_ref[i] = jnp.where(take, there_ref[6 + i], here_ref[6 + i]).astype(jnp.int32)


PLACES = {
    "s": pl.BlockSpec(memory_space=pltpu.SMEM),
    "v": pl.BlockSpec(memory_space=pltpu.VMEM),
    "a": pl.BlockSpec(memory_space=pl.ANY),
}


def call(kernel, ins, outs, scratch=(), cost=0, limit=40):
    return pl.pallas_call(
        kernel,
        out_shape=[jax.ShapeDtypeStruct(shape, dtype) for shape, dtype in outs],
        in_specs=[PLACES[place] for place, _ in ins],
        out_specs=[PLACES["v"]] * len(outs),
        scratch_shapes=list(scratch),
        compiler_params=pltpu.CompilerParams(vmem_limit_bytes=limit * 2**20),
        cost_estimate=pl.CostEstimate(flops=cost, bytes_accessed=200000, transcendentals=0),
    )(*[value for _, value in ins])


def neighbours(low, high):
    size = lax.axis_size("dom")
    below = lax.ppermute(high, "dom", [(i, (i + 1) % size) for i in range(size)])
    above = lax.ppermute(low, "dom", [(i, (i - 1) % size) for i in range(size)])
    return below, above


def traded(state, round_index):
    pairs = []
    for w in range(round_index % 2, lax.axis_size("lam") - 1, 2):
        pairs += [(w, w + 1), (w + 1, w)]
    return lax.ppermute(state, "lam", pairs)


def exchanged(value):
    return lax.all_to_all(value, "dom", split_axis=0, concat_axis=0, tiled=True)


def body(
    cells, offsets, velocities, charges, coupling, inverse_mass, lambdas, tile_lists, halo_lists, accept_flags
):
    wide = ((8, A_DEV), F32)
    moving = ((16, A_DEV), F32)
    border = ((8, HALO), F32)
    turns = pltpu.VMEM((3, A_DEV), F32)
    pair_scratch = [
        turns, pltpu.VMEM((3, CLUSTERS * 8, CLUSTER), F32), pltpu.VMEM((6, A_DEV, CLUSTER), F32),
        pltpu.VMEM((A_DEV, 8), F32), pltpu.VMEM((6, CLUSTER, CLUSTER), jnp.int32), pltpu.VMEM((4, CLUSTER, CLUSTER), F32),
    ]
    spare = pltpu.VMEM((8, A_DEV), F32)
    tiles = jnp.transpose(tile_lists, (2, 0, 1))
    slab = jnp.asarray(slab_basis())
    square, factor = plane_gain()
    gain_rows = np.zeros((K, 8), np.float32)
    gain_rows[:, 0], gain_rows[:, 1] = square, factor
    gain_lanes = np.zeros((8, K), np.float32)
    gain_lanes[0], gain_lanes[1] = square, factor

    triple = (3, 1, A_DEV)

    def by_row(x):
        return jnp.transpose(x, (1, 0, 2))


    grid, data, move, low, high = call(
        spread_kernel,
        [
            ("s", lambdas), ("a", by_row(cells)), ("a", by_row(offsets)), ("a", by_row(velocities)),
            ("a", charges[None]), ("a", coupling[None]), ("a", inverse_mass[None]), ("a", halo_lists), ("a", slab),
            ("a", accept_flags.T),
        ],
        [((ROWS, K), F32), wide, moving, border, border],
        [
            pltpu.VMEM((ROWS, A_DEV), BF16), pltpu.VMEM((ROWS, A_DEV), BF16),
            pltpu.VMEM((3, 1, A_DEV), jnp.int32), pltpu.VMEM((3, 1, A_DEV), F32), pltpu.VMEM((3, 1, A_DEV), F32),
            pltpu.VMEM((1, A_DEV), F32), pltpu.VMEM((1, A_DEV), F32), pltpu.VMEM((1, A_DEV), F32),
            pltpu.VMEM((1, 2, HALO), jnp.int32), pltpu.VMEM((MODES, MODES), F32), pltpu.VMEM((1, 2), jnp.int32),
            pltpu.SemaphoreType.DMA((9,)),
        ],
        limit=60,
    )
    grid = exchanged(grid)
    below, above = neighbours(low, high)
    short, gain = call(
        gain_kernel,
        [
            ("s", lambdas), ("s", tiles), ("s", jnp.asarray(slab_weights())), ("v", data),
            ("v", jnp.asarray(gain_rows)), ("v", jnp.asarray(gain_lanes)),
        ],
        [wide, ((2, K, K), F32)],
        pair_scratch,
        cost=2 * 10**9,
    )
    (potential,) = call(
        mesh_kernel,
        [("v", grid), ("v", gain), ("v", jnp.asarray(basis_table())), ("a", below), ("a", above)],
        [((ROWS, K), F32)],
        [pltpu.VMEM((2 * K, K), F32)],
    )
    potential = exchanged(potential)
    short, *tables = call(
        rest_kernel,
        [
            ("s", lambdas), ("s", tiles), ("v", data), ("v", below), ("v", above), ("v", short), ("v", move), ("v", slab),
        ],
        [wide, *[((K, 2 * A_DEV), BF16)] * 2, ((2 * MODES, A_DEV), F32), ((32, A_DEV), F32)],
        [spare, *pair_scratch],
        cost=2 * 10**9,
    )
    far, data, move, low, high = call(
        gather_kernel,
        [("v", potential), ("v", data), ("v", move), ("v", short), *(("v", x) for x in tables)],
        [wide, wide, moving, border, border],
        [spare],
    )

    def own_call(data):
        (partial,) = call(
            own_kernel, [("s", lambdas), ("s", tiles), ("v", data)], [wide], pair_scratch, cost=2 * 10**9
        )
        return partial

    below, above = neighbours(low, high)
    short = own_call(data)
    data, move, low, high = call(
        halo_step_kernel,
        [
            ("s", lambdas), ("v", data), ("v", below), ("v", above), ("v", short), ("v", far), ("v", move),
        ],
        [wide, moving, border, border],
        [turns, spare],
    )
    below, above = neighbours(low, high)
    short = own_call(data)
    (state,) = call(
        halo_last_kernel,
        [
            ("s", lambdas), ("v", data), ("v", below), ("v", above), ("v", short), ("v", far), ("v", move),
        ],
        [((10, 1, A_DEV), F32)],
        [turns, spare],
    )
    (state,) = call(
        first_trade_kernel, [("v", state), ("v", traded(state, 0)), ("v", move)], [((10, 1, A_DEV), F32)]
    )
    out = call(
        last_trade_kernel,
        [("v", state), ("v", traded(state, 1))],
        [(triple, jnp.int32), (triple, F32), (triple, F32)],
    )
    return tuple(by_row(x) for x in out)


def solution(mesh):
    in_specs = (
        P("lam", None, "dom"),
        P("lam", None, "dom"),
        P("lam", None, "dom"),
        P("dom"),
        P("dom"),
        P("dom"),
        P("lam"),
        P("lam", "dom", None),
        P("lam", "dom", None),
        P(None, "lam"),
    )
    out_specs = (P("lam", None, "dom"), P("lam", None, "dom"), P("lam", None, "dom"))
    return jax.shard_map(body, mesh=mesh, in_specs=in_specs, out_specs=out_specs, check_vma=False)
```

```python
import functools
import math

import jax
import jax.numpy as jnp
import ml_dtypes
import numpy as np
from jax import lax
from jax.experimental import pallas as pl
from jax.experimental.pallas import tpu as pltpu
from jax.sharding import PartitionSpec as P

K = 128
CLUSTER = 128
N_DOM = 16
A_DEV = 1024
CLUSTERS = 8
HALO = 512
MODES = 32
SLAB = 24
ROWS = N_DOM * SLAB

EWALD_BETA = 0.5
COULOMB = 20.0
LJ_DEPTH = 1.0
LJ_SIGMA_SQ = 0.49
SOFT_SCALE = 0.5
SOFT_FLOOR = 0.5
STEP_DT = 0.25

F32 = jnp.float32
BF16 = jnp.bfloat16
HIGHEST = lax.Precision.HIGHEST

TURN = 2.0**32
SPAN_SQ = 2.0**-50
SPAN = 2.0**-25

SCREEN = (
    -0.0818439527,
    0.648023047,
    -2.23331568,
    4.38709699,
    -5.37737017,
    4.16223694,
    -1.81397109,
    0.0540053844,
    0.5630337,
    -5.2346482e-05,
    0.282096019,
)


def real_basis(count):
    half = count // 2
    place = np.arange(count)
    rows = []
    for k in range(half + 1):
        scale = math.sqrt((1.0 if k in (0, half) else 2.0) / count)
        rows.append(scale * np.cos(2.0 * np.pi * (k * place % count) / count))
    for k in range(1, half):
        rows.append(math.sqrt(2.0 / count) * np.sin(2.0 * np.pi * (k * place % count) / count))
    return np.stack(rows)


def halves(table):
    high = table.astype(np.float32).astype(ml_dtypes.bfloat16)
    low = (table - high.astype(np.float64)).astype(np.float32).astype(ml_dtypes.bfloat16)
    return high, low


def basis_table():
    basis = real_basis(K)
    high, low = halves(basis)
    return np.concatenate([high, low, high.T, low.T], axis=0)


def slab_basis():
    basis = real_basis(MODES)
    order = [0, MODES // 2]
    for k in range(1, MODES // 2):
        order += [k, MODES // 2 + k]
    return basis[np.array(order)].astype(np.float32)


def spline_modulus(k):
    return (3.0 / (2.0 + np.cos(2.0 * np.pi * k / K))) ** 2


def slab_weights():
    k = np.arange(K // 2 + 1)
    delta = np.arange(-MODES // 2 + 1, MODES // 2 + 1)
    folded = np.where((k == 0) | (k == K // 2), 1.0, 2.0)
    own = folded * np.exp(-np.pi**2 * (k / K) ** 2 / EWALD_BETA**2) * spline_modulus(k)
    rows = []
    for j in range(MODES // 2 + 1):
        window = np.cos(2 * np.pi * k[:, None] * delta / K) * np.cos(2 * np.pi * j * delta / MODES)
        rows.append(own * window.sum(axis=1))
    return np.stack(rows).astype(np.float32)


def plane_gain():
    k = np.concatenate([np.arange(K // 2 + 1), np.arange(1, K // 2)])
    square = (k / K) ** 2
    factor = np.exp(-np.pi**2 * square / EWALD_BETA**2) * spline_modulus(k)
    return square.astype(np.float32), factor.astype(np.float32)


def split(x):
    high = x.astype(BF16)
    return high, (x - high.astype(F32)).astype(BF16)


def dot3(left, right, dims=(((1,), (0,)), ((), ()))):
    lh, ll = left
    rh, rl = right
    dot = functools.partial(lax.dot_general, dimension_numbers=dims, preferred_element_type=F32)
    return dot(lh, rh) + (dot(lh, rl) + dot(ll, rh))


def spline_set(u):
    v = 1.0 - u
    u2 = u * u
    u3 = u2 * u
    weights = (
        v * v * v / 6.0,
        (3.0 * u3 - 6.0 * u2 + 4.0) / 6.0,
        (-3.0 * u3 + 3.0 * u2 + 3.0 * u + 1.0) / 6.0,
        u3 / 6.0,
    )
    slopes = (-0.5 * v * v, 1.5 * u2 - 2.0 * u, -1.5 * u2 + u + 0.5, 0.5 * u2)
    return weights, slopes


def chosen(distance, rows):
    out = jnp.where(distance == 3, rows[3], 0.0)
    for k in (2, 1, 0):
        out = jnp.where(distance == k, rows[k], out)
    return out


def iota_rows(rows, columns):
    return lax.broadcasted_iota(jnp.int32, (rows, columns), 0)


def fixed_turns(x):
    t = x * (1.0 / K)
    f = t - jnp.floor(t + 0.5)
    return jnp.maximum(f, -0.5) * TURN


def pair_terms(own, other, floor_value):
    ax, ay, az, qa, wa = own
    bx, by, bz, qb, wb = other
    dx = (ax - bx).astype(F32)
    dy = (ay - by).astype(F32)
    dz = (az - bz).astype(F32)
    s = (dx * dx + dy * dy + dz * dz) * SPAN_SQ + floor_value
    w = lax.rsqrt(s)
    u = w * w
    screen = jnp.full_like(w, SCREEN[0])
    for c in SCREEN[1:]:
        screen = screen * w + c
    gauss = jnp.exp2(s * (-(EWALD_BETA**2) * math.log2(math.e)))
    t = u * u * u
    g = u * ((qa * qb) * (gauss * screen) + (wa * wb) * (t * (t - 0.5 / LJ_SIGMA_SQ**3)))
    return g * dx, g * dy, g * dz


def own_rows(data_ref, turns, start, rows=8):
    def spread(row):
        return jnp.broadcast_to(row, (rows, CLUSTER))

    columns = pl.ds(start, CLUSTER)
    xyz = [spread(turns[i : i + 1, columns].astype(jnp.int32)) for i in range(3)]
    q = spread(data_ref[3:4, columns] * (2.0 * COULOMB))
    w = spread(data_ref[4:5, columns] * (48.0 * LJ_DEPTH * LJ_SIGMA_SQ**6))
    return (*xyz, q, w)


def write_halo(data, lists, low_ref, high_ref):
    lane = lax.broadcasted_iota(jnp.int32, (8, CLUSTER), 1)
    for row, out_ref in ((0, low_ref), (1, high_ref)):
        for k in range(HALO // CLUSTER):
            columns = slice(k * CLUSTER, (k + 1) * CLUSTER)
            start = row * HALO + k * CLUSTER
            index = jnp.broadcast_to(lists[:, start : start + CLUSTER].astype(jnp.int32), (8, CLUSTER))
            first = data[:, 2 * k * CLUSTER : (2 * k + 1) * CLUSTER]
            second = data[:, (2 * k + 1) * CLUSTER : (2 * k + 2) * CLUSTER]
            out_ref[:, columns] = jnp.where(
                lane < CLUSTER // 2,
                jnp.take_along_axis(first, index, axis=1, mode="promise_in_bounds"),
                jnp.take_along_axis(second, index, axis=1, mode="promise_in_bounds"),
            )


def state_kernel(
    lam_ref, cells_ref, off_ref, vel_ref, charge_ref, coup_ref, mass_ref, lists_ref, flag_ref, grid_ref,
    data_ref, move_ref, low_ref, high_ref,
):
    del grid_ref
    weight = 1.0 - lam_ref[0] * coup_ref[...]
    for i in range(3):
        cell = cells_ref[i].astype(F32)
        move_ref[i : i + 1, :] = off_ref[i]
        move_ref[3 + i : 4 + i, :] = cell
        move_ref[8 + i : 9 + i, :] = vel_ref[i]
        data_ref[i : i + 1, :] = cell + off_ref[i]
    move_ref[6:7, :] = jnp.broadcast_to(flag_ref[0:1, 0:1].astype(F32), (1, A_DEV))
    move_ref[7:8, :] = jnp.broadcast_to(flag_ref[0:1, 1:2].astype(F32), (1, A_DEV))
    move_ref[11:12, 0:HALO] = (lists_ref[0, 0:1, :] & (CLUSTER - 1)).astype(F32)
    move_ref[11:12, HALO : 2 * HALO] = (lists_ref[0, 1:2, :] & (CLUSTER - 1)).astype(F32)
    move_ref[12:16, :] = jnp.zeros((4, A_DEV), F32)
    data_ref[3:4, :] = charge_ref[...] * weight
    data_ref[4:5, :] = weight
    data_ref[5:6, :] = mass_ref[...]
    data_ref[6:8, :] = jnp.zeros((2, A_DEV), F32)
    write_halo(data_ref[...], move_ref[11:12, :], low_ref, high_ref)


def spread_kernel(
    lam_ref, cells_hbm, off_hbm, charge_hbm, coup_hbm, slab_hbm,
    out_ref, mixed_high, mixed_low, cells_ref, off_ref, charge_ref, coup_ref, slab_ref, rows_ref, arrived,
):
    copies = [
        pltpu.make_async_copy(source, target, arrived.at[i])
        for i, (source, target) in enumerate(
            (
                (cells_hbm, cells_ref), (off_hbm, off_ref), (charge_hbm, charge_ref), (coup_hbm, coup_ref),
                (slab_hbm, slab_ref),
            )
        )
    ]
    for copy in copies:
        copy.start()
    for copy in copies:
        copy.wait()
    charge = charge_ref[...] * (1.0 - lam_ref[0] * coup_ref[...])
    for i in range(3):
        rows_ref[i : i + 1, :] = off_ref[i]
    off = rows_ref[0:3, :]
    cells = [cells_ref[i] for i in range(3)]
    weights, _ = spline_set(off)
    row = iota_rows(16, A_DEV)
    plane = jnp.where(row < 8, row, 8 + (row & 3))
    x_table = chosen(plane - (cells[0] & 7), [m[0:1] for m in weights]) * charge
    z_table = chosen((iota_rows(MODES, A_DEV) - cells[2]) & (MODES - 1), [m[2:3] for m in weights])
    z_modes = jnp.dot(slab_ref[...], z_table, precision=HIGHEST, preferred_element_type=F32)
    y_table = chosen((iota_rows(K, A_DEV) - cells[1]) & (K - 1), [m[1:2] for m in weights])

    near, far = x_table[0:8], x_table[8:16]
    upper = iota_rows(8, A_DEV) < 4
    for i in range(0, N_DOM, 2):
        pieces = []
        for k in (i, i + 1):
            first = jnp.broadcast_to(z_modes[2 * k : 2 * k + 1], (8, A_DEV))
            second = jnp.broadcast_to(z_modes[2 * k + 1 : 2 * k + 2], (8, A_DEV))
            pieces += [near * first, near * second, far * jnp.where(upper, first, second)]
        high, low = split(jnp.concatenate(pieces, axis=0))
        mixed_high[i * SLAB : (i + 2) * SLAB, :] = high
        mixed_low[i * SLAB : (i + 2) * SLAB, :] = low
    out_ref[...] = dot3((mixed_high[...], mixed_low[...]), split(y_table), (((1,), (1,)), ((), ())))


def mesh_kernel(grid_ref, gain_ref, basis_ref, below_ref, above_ref, out_ref, block):
    del below_ref, above_ref
    top = iota_rows(8, K) < 4
    for e in range(N_DOM):
        spill = grid_ref[((e - 1) % N_DOM) * SLAB + 16 : ((e - 1) % N_DOM) * SLAB + 24, :]
        turned = pltpu.roll(spill, 4, 0)
        block[8 * e : 8 * e + 8, :] = grid_ref[e * SLAB : e * SLAB + 8, :] + jnp.where(top, spill, 0.0)
        block[K + 8 * e : K + 8 * e + 8, :] = grid_ref[e * SLAB + 8 : e * SLAB + 16, :] + jnp.where(top, turned, 0.0)
    basis = (basis_ref[0:K, :], basis_ref[K : 2 * K, :])
    turned_basis = (basis_ref[2 * K : 3 * K, :], basis_ref[3 * K : 4 * K, :])
    along_y = dot3(split(block[...]), turned_basis)
    for mode in range(2):
        part = split(along_y[mode * K : (mode + 1) * K])
        scaled = dot3(basis, part) * gain_ref[mode]
        block[mode * K : (mode + 1) * K, :] = dot3(turned_basis, split(scaled))
    block[...] = dot3(split(block[...]), basis)
    for e in range(N_DOM):
        following = 8 * ((e + 1) % N_DOM)
        out_ref[e * SLAB : e * SLAB + 8, :] = block[8 * e : 8 * e + 8, :]
        out_ref[e * SLAB + 8 : e * SLAB + 16, :] = block[K + 8 * e : K + 8 * e + 8, :]
        out_ref[e * SLAB + 16 : e * SLAB + 24, :] = jnp.where(
            top,
            block[following : following + 8, :],
            pltpu.roll(block[K + following : K + following + 8, :], 4, 0),
        )


def write_gain(mode_weights_ref, rows_ref, lanes_ref, gain_ref):
    dom = lax.axis_index("dom")
    square_y, factor_y = lanes_ref[0:1, :], lanes_ref[1:2, :]
    scale = COULOMB / (math.pi * K)
    first = dom
    second = jnp.where(dom == 0, MODES // 2, dom)

    def totals(square):
        one = jnp.zeros_like(square)
        two = jnp.zeros_like(square)
        for k in range(K // 2 + 1):
            whole = square + (k / K) ** 2
            inverse = 1.0 / whole if k else jnp.where(whole > 0.0, 1.0 / jnp.where(whole > 0.0, whole, 1.0), 0.0)
            one = one + inverse * mode_weights_ref[first, k]
            two = two + inverse * mode_weights_ref[second, k]
        return one, two

    def block(start):
        rows = pl.ds(start, 8)
        square = jnp.broadcast_to(rows_ref[rows, 0:1], (8, K)) + square_y
        factor = jnp.broadcast_to(rows_ref[rows, 1:2], (8, K)) * factor_y * scale
        one, two = totals(square)
        return one * factor, two * factor

    def step(b, carry):
        start = pl.multiple_of(b * 8, 8)
        one, two = block(start)
        gain_ref[0, pl.ds(start, 8), :] = one
        gain_ref[1, pl.ds(start, 8), :] = two
        gain_ref[0, pl.ds(start + K // 2, 8), :] = one
        gain_ref[1, pl.ds(start + K // 2, 8), :] = two
        return carry

    lax.fori_loop(0, 8, step, 0)
    one, two = block(K // 2)
    gain_ref[0, K // 2 : K // 2 + 1, :] = one[0:1]
    gain_ref[1, K // 2 : K // 2 + 1, :] = two[0:1]


def listed(tiles_ref, row, cluster):
    count = jnp.int32(0)
    for slot in range(1, 4):
        count = count + jnp.where(tiles_ref[slot, 0, row] == cluster, 1, 0)
    return count.astype(F32)


def own_forces(lam_ref, tiles_ref, data_ref, force_ref, turns, near, sides, columns, places, factors, first, last):
    turns[...] = fixed_turns(data_ref[0:3, :])
    near[...] = jnp.zeros_like(near)
    floor_value = SOFT_FLOOR + SOFT_SCALE * lam_ref[0]
    for b in range(first, last):
        lanes = slice(b * CLUSTER, (b + 1) * CLUSTER)
        columns[lanes, :] = jnp.concatenate([turns[:, lanes], data_ref[3:8, lanes]], axis=0).T

    def one_cluster(b, side):
        start = pl.multiple_of(b * CLUSTER, CLUSTER)
        for j in range(3):
            a = b if j == 0 else (b + j) % CLUSTERS
            own = own_rows(data_ref, turns, pl.multiple_of(a * CLUSTER, CLUSTER))
            total = [jnp.zeros((8, CLUSTER), F32) for _ in range(3)]
            back = listed(tiles_ref, b, a) if j else None
            for chunk in range(CLUSTER // 8):
                here = slice(chunk * 8, chunk * 8 + 8)
                rows = pl.ds(pl.multiple_of(start + chunk * 8, 8), 8)
                if j == 0:
                    part = columns[rows, :]
                    other = [jnp.broadcast_to(part[:, i : i + 1], (8, CLUSTER)) for i in range(5)]
                    other[:3] = [x.astype(jnp.int32) for x in other[:3]]
                    for i in range(3):
                        places[3 * side + i, here, :] = other[i]
                    for i in range(2):
                        factors[2 * side + i, here, :] = other[3 + i]
                else:
                    other = [places[3 * side + i, here, :] for i in range(3)]
                    other += [factors[2 * side + i, here, :] for i in range(2)]
                terms = pair_terms(own, other, floor_value)
                total = [p + q for p, q in zip(total, terms)]
                if j:
                    for i in range(3):
                        sides[3 * j - 3 + i, rows, :] = back * terms[i]
            rows = pl.ds(pl.multiple_of(a * 8, 8), 8)
            for i in range(3):
                near[i, rows, :] = near[i, rows, :] + (listed(tiles_ref, a, b) * total[i] if j else total[i])

    def four_clusters(k, carry):
        for side in range(4):
            one_cluster(4 * k + side, side)
        return carry

    lax.fori_loop(first // 4, last // 4, four_clusters, 0)
    force_ref[...] = jnp.zeros_like(force_ref)
    ones = jnp.ones((8, CLUSTER), BF16)
    for c in range(CLUSTERS):
        lanes = slice(c * CLUSTER, (c + 1) * CLUSTER)
        for i in range(3):
            force_ref[i : i + 1, lanes] = SPAN * jnp.sum(near[i, c * 8 : (c + 1) * 8, :], axis=0, keepdims=True)
    rows = slice(first * CLUSTER, last * CLUSTER)
    for i in range(3):
        total = jnp.zeros((8, (last - first) * CLUSTER), F32)
        for part in split(sides[i, rows, :] + sides[3 + i, rows, :]):
            total = total + lax.dot_general(ones, part, (((1,), (1,)), ((), ())), preferred_element_type=F32)
        force_ref[i : i + 1, rows] = force_ref[i : i + 1, rows] - SPAN * total[0:1]


def own_kernel(lam_ref, tiles_ref, data_ref, force_ref, turns, near, sides, *kept):
    own_forces(lam_ref, tiles_ref, data_ref, force_ref, turns, near, sides, *kept, 0, CLUSTERS)


def gain_kernel(
    lam_ref, tiles_ref, weights_ref, data_ref, rows_ref, lanes_ref, force_ref, gain_ref, turns, near, sides, *kept
):
    write_gain(weights_ref, rows_ref, lanes_ref, gain_ref)
    own_forces(lam_ref, tiles_ref, data_ref, force_ref, turns, near, sides, *kept, 0, CLUSTERS // 2)


def add_halo_forces(lam_ref, data_ref, below_ref, above_ref, partial_ref, force_ref, turns):
    turns[...] = fixed_turns(data_ref[0:3, :])
    floor_value = SOFT_FLOOR + SOFT_SCALE * lam_ref[0]

    def one_pair(k, carry):
        start = pl.multiple_of(k * CLUSTER, CLUSTER)
        starts = [pl.multiple_of(k * (2 * CLUSTER), CLUSTER), pl.multiple_of(k * (2 * CLUSTER) + CLUSTER, CLUSTER)]
        owns = [own_rows(data_ref, turns, s) for s in starts]
        totals = [[jnp.zeros((8, CLUSTER), F32) for _ in range(3)] for _ in range(2)]
        for source in (below_ref, above_ref):
            block = source[:, pl.ds(start, CLUSTER)]
            stack = jnp.where(iota_rows(8, CLUSTER) < 3, fixed_turns(block), block)
            turned = stack.T
            for chunk in range(CLUSTER // 8):
                part = turned[chunk * 8 : chunk * 8 + 8]
                other = [jnp.broadcast_to(part[:, i : i + 1], (8, CLUSTER)) for i in range(5)]
                other[:3] = [x.astype(jnp.int32) for x in other[:3]]
                for j in range(2):
                    terms = pair_terms(owns[j], other, floor_value)
                    totals[j] = [a + b for a, b in zip(totals[j], terms)]
        for j in range(2):
            lanes = pl.ds(starts[j], CLUSTER)
            for i in range(3):
                force_ref[i : i + 1, lanes] = partial_ref[i : i + 1, lanes] + SPAN * jnp.sum(
                    totals[j][i], axis=0, keepdims=True
                )
        return carry

    def two_pairs(k, carry):
        for side in range(2):
            one_pair(2 * k + side, carry)
        return carry

    lax.fori_loop(0, HALO // CLUSTER // 2, two_pairs, 0)


def rest_kernel(
    lam_ref, tiles_ref, data_ref, below_ref, above_ref, partial_ref, move_ref, slab_ref,
    force_ref, y_high, y_low, z_ref, x_ref, second, turns, near, sides, *kept
):
    write_tables(move_ref, slab_ref, y_high, y_low, z_ref, x_ref)
    own_forces(lam_ref, tiles_ref, data_ref, second, turns, near, sides, *kept, CLUSTERS // 2, CLUSTERS)
    second[...] = second[...] + partial_ref[...]
    force_ref[...] = jnp.zeros_like(force_ref)
    add_halo_forces(lam_ref, data_ref, below_ref, above_ref, second, force_ref, turns)


def advance(force, kicks, data_ref, move_ref, data_out, move_out, low_ref, high_ref):
    mass = data_ref[5:6, :]
    velocity = move_ref[8:11, :]
    for _ in range(kicks):
        velocity = velocity + 0.5 * STEP_DT * force * mass
    off = move_ref[0:3, :] + STEP_DT * velocity
    move_out[...] = move_ref[...]
    move_out[0:3, :] = off
    move_out[8:11, :] = velocity
    data_out[...] = data_ref[...]
    data_out[0:3, :] = move_ref[3:6, :] + off
    write_halo(data_out[...], move_ref[11:12, :], low_ref, high_ref)


def write_tables(move_ref, slab_ref, y_high, y_low, z_ref, x_ref):
    off = move_ref[0:3, :]
    cells = move_ref[3:6, :].astype(jnp.int32)
    weights, slopes = spline_set(off)
    row = iota_rows(16, A_DEV)
    reach = jnp.where(row < 8, row, 8 + (row & 3)) - (cells[0:1] & 7)
    x_ref[0:16, :] = chosen(reach, [m[0:1] for m in weights])
    x_ref[16:32, :] = chosen(reach, [m[0:1] for m in slopes])
    reach = (iota_rows(MODES, A_DEV) - cells[2:3]) & (MODES - 1)
    for i, rows in enumerate((weights, slopes)):
        table = chosen(reach, [m[2:3] for m in rows])
        z_ref[i * MODES : (i + 1) * MODES, :] = jnp.dot(
            slab_ref[...], table, precision=HIGHEST, preferred_element_type=F32
        )
    for c in range(CLUSTERS):
        lanes = slice(c * CLUSTER, (c + 1) * CLUSTER)
        reach = (iota_rows(K, CLUSTER) - cells[1:2, lanes]) & (K - 1)
        for i, rows in enumerate((weights, slopes)):
            target = slice((2 * c + i) * CLUSTER, (2 * c + i + 1) * CLUSTER)
            y_high[:, target], y_low[:, target] = split(chosen(reach, [m[1:2, lanes] for m in rows]))


def gather_kernel(
    pot_ref, data_ref, move_ref, short_ref, y_high, y_low, z_ref, x_ref,
    long_ref, data_out, move_out, low_ref, high_ref, force,
):
    charge = data_ref[3:4, :]
    potential = split(pot_ref[...])
    upper = iota_rows(8, CLUSTER) < 4
    for c in range(CLUSTERS):
        lanes = slice(c * CLUSTER, (c + 1) * CLUSTER)
        both = slice(2 * c * CLUSTER, (2 * c + 2) * CLUSTER)
        along = dot3(potential, (y_high[:, both], y_low[:, both]))
        value, tilt = along[:, :CLUSTER], along[:, CLUSTER:]
        sums = [[jnp.zeros((8, CLUSTER), F32) for _ in range(2)] for _ in range(3)]
        for i in range(N_DOM):
            pairs = []
            for k in (2 * i, MODES + 2 * i):
                first = jnp.broadcast_to(z_ref[k : k + 1, lanes], (8, CLUSTER))
                second = jnp.broadcast_to(z_ref[k + 1 : k + 2, lanes], (8, CLUSTER))
                pairs.append((first, second, jnp.where(upper, first, second)))
            for which, (source, table) in enumerate(((value, 0), (tilt, 0), (value, 1))):
                block = source[i * SLAB : (i + 1) * SLAB]
                first, second, mixed = pairs[table]
                sums[which][0] = sums[which][0] + (first * block[0:8] + second * block[8:16])
                sums[which][1] = sums[which][1] + mixed * block[16:24]
        for i in range(3):
            k = 16 if i == 0 else 0
            near = x_ref[k : k + 8, lanes] * sums[i][0] + x_ref[k + 8 : k + 16, lanes] * sums[i][1]
            force[i : i + 1, lanes] = -charge[:, lanes] * jnp.sum(near, axis=0, keepdims=True)
    long_ref[...] = jnp.zeros_like(long_ref)
    long_ref[0:3, :] = force[0:3, :]
    advance(
        short_ref[0:3, :] + force[0:3, :], 1, data_ref, move_ref, data_out, move_out, low_ref, high_ref
    )


def halo_step_kernel(
    lam_ref, data_ref, below_ref, above_ref, partial_ref, long_ref, move_ref,
    data_out, move_out, low_ref, high_ref, turns, force,
):
    add_halo_forces(lam_ref, data_ref, below_ref, above_ref, partial_ref, force, turns)
    total = force[0:3, :] + long_ref[0:3, :]
    advance(total, 2, data_ref, move_ref, data_out, move_out, low_ref, high_ref)


def halo_last_kernel(
    lam_ref, data_ref, below_ref, above_ref, partial_ref, long_ref, move_ref, state_ref, turns, force
):
    add_halo_forces(lam_ref, data_ref, below_ref, above_ref, partial_ref, force, turns)
    total = force[0:3, :] + long_ref[0:3, :]
    velocity = move_ref[8:11, :] + 0.5 * STEP_DT * total * data_ref[5:6, :]
    for i in range(3):
        state_ref[i] = move_ref[i : i + 1, :]
        state_ref[3 + i] = velocity[i : i + 1]
        state_ref[6 + i] = move_ref[3 + i : 4 + i, :]
    state_ref[9] = move_ref[6:7, :]


def takes(round_index, here_ref, there_ref):
    window = lax.axis_index("lam")
    lower = window % 2 == round_index % 2
    inside = window + 1 < lax.axis_size("lam")
    return jnp.where(lower, jnp.where(inside, here_ref[9], 0.0), there_ref[9]) == 1.0


def first_trade_kernel(here_ref, there_ref, move_ref, out_ref):
    take = takes(0, here_ref, there_ref)
    for i in range(9):
        out_ref[i] = jnp.where(take, there_ref[i], here_ref[i])
    out_ref[9] = move_ref[7:8, :]


def last_trade_kernel(here_ref, there_ref, cells_ref, off_ref, vel_ref):
    take = takes(1, here_ref, there_ref)
    for i in range(3):
        off_ref[i] = jnp.where(take, there_ref[i], here_ref[i])
        vel_ref[i] = jnp.where(take, there_ref[3 + i], here_ref[3 + i])
        cells_ref[i] = jnp.where(take, there_ref[6 + i], here_ref[6 + i]).astype(jnp.int32)


PLACES = {
    "s": pl.BlockSpec(memory_space=pltpu.SMEM),
    "v": pl.BlockSpec(memory_space=pltpu.VMEM),
    "a": pl.BlockSpec(memory_space=pl.ANY),
}


def call(kernel, ins, outs, scratch=(), cost=0, limit=40):
    return pl.pallas_call(
        kernel,
        out_shape=[jax.ShapeDtypeStruct(shape, dtype) for shape, dtype in outs],
        in_specs=[PLACES[place] for place, _ in ins],
        out_specs=[PLACES["v"]] * len(outs),
        scratch_shapes=list(scratch),
        compiler_params=pltpu.CompilerParams(vmem_limit_bytes=limit * 2**20),
        cost_estimate=pl.CostEstimate(flops=cost, bytes_accessed=200000, transcendentals=0),
    )(*[value for _, value in ins])


def neighbours(low, high):
    size = lax.axis_size("dom")
    below = lax.ppermute(high, "dom", [(i, (i + 1) % size) for i in range(size)])
    above = lax.ppermute(low, "dom", [(i, (i - 1) % size) for i in range(size)])
    return below, above


def traded(state, round_index):
    pairs = []
    for w in range(round_index % 2, lax.axis_size("lam") - 1, 2):
        pairs += [(w, w + 1), (w + 1, w)]
    return lax.ppermute(state, "lam", pairs)


def exchanged(value):
    return lax.all_to_all(value, "dom", split_axis=0, concat_axis=0, tiled=True)


def body(
    cells, offsets, velocities, charges, coupling, inverse_mass, lambdas, tile_lists, halo_lists, accept_flags
):
    wide = ((8, A_DEV), F32)
    moving = ((16, A_DEV), F32)
    border = ((8, HALO), F32)
    turns = pltpu.VMEM((3, A_DEV), F32)
    pair_scratch = [
        turns, pltpu.VMEM((3, CLUSTERS * 8, CLUSTER), F32), pltpu.VMEM((6, A_DEV, CLUSTER), F32),
        pltpu.VMEM((A_DEV, 8), F32), pltpu.VMEM((12, CLUSTER, CLUSTER), jnp.int32), pltpu.VMEM((8, CLUSTER, CLUSTER), F32),
    ]
    spare = pltpu.VMEM((8, A_DEV), F32)
    tiles = jnp.transpose(tile_lists, (2, 0, 1))
    slab = jnp.asarray(slab_basis())
    square, factor = plane_gain()
    gain_rows = np.zeros((K, 8), np.float32)
    gain_rows[:, 0], gain_rows[:, 1] = square, factor
    gain_lanes = np.zeros((8, K), np.float32)
    gain_lanes[0], gain_lanes[1] = square, factor

    triple = (3, 1, A_DEV)

    def by_row(x):
        return jnp.transpose(x, (1, 0, 2))


    rows = [by_row(x) for x in (cells, offsets, velocities)]
    whole, some = (3, 1, A_DEV), (1, A_DEV)
    (grid,) = call(
        spread_kernel,
        [
            ("s", lambdas), ("a", rows[0]), ("a", rows[1]), ("a", charges[None]), ("a", coupling[None]), ("a", slab),
        ],
        [((ROWS, K), F32)],
        [
            pltpu.VMEM((ROWS, A_DEV), BF16), pltpu.VMEM((ROWS, A_DEV), BF16), pltpu.VMEM(whole, jnp.int32),
            pltpu.VMEM(whole, F32), pltpu.VMEM(some, F32), pltpu.VMEM(some, F32), pltpu.VMEM((MODES, MODES), F32),
            pltpu.VMEM((8, A_DEV), F32), pltpu.SemaphoreType.DMA((5,)),
        ],
        limit=60,
    )
    data, move, low, high = call(
        state_kernel,
        [
            ("s", lambdas), *(("v", x) for x in rows), ("v", charges[None]), ("v", coupling[None]),
            ("v", inverse_mass[None]), ("v", halo_lists), ("v", accept_flags.T), ("a", grid),
        ],
        [wide, moving, border, border],
    )
    grid = exchanged(grid)
    below, above = neighbours(low, high)
    short, gain = call(
        gain_kernel,
        [
            ("s", lambdas), ("s", tiles), ("s", jnp.asarray(slab_weights())), ("v", data),
            ("v", jnp.asarray(gain_rows)), ("v", jnp.asarray(gain_lanes)),
        ],
        [wide, ((2, K, K), F32)],
        pair_scratch,
        cost=2 * 10**9,
    )
    (potential,) = call(
        mesh_kernel,
        [("v", grid), ("v", gain), ("v", jnp.asarray(basis_table())), ("a", below), ("a", above)],
        [((ROWS, K), F32)],
        [pltpu.VMEM((2 * K, K), F32)],
    )
    potential = exchanged(potential)
    short, *tables = call(
        rest_kernel,
        [
            ("s", lambdas), ("s", tiles), ("v", data), ("v", below), ("v", above), ("v", short), ("v", move), ("v", slab),
        ],
        [wide, *[((K, 2 * A_DEV), BF16)] * 2, ((2 * MODES, A_DEV), F32), ((32, A_DEV), F32)],
        [spare, *pair_scratch],
        cost=2 * 10**9,
    )
    far, data, move, low, high = call(
        gather_kernel,
        [("v", potential), ("v", data), ("v", move), ("v", short), *(("v", x) for x in tables)],
        [wide, wide, moving, border, border],
        [spare],
    )

    def own_call(data):
        (partial,) = call(
            own_kernel, [("s", lambdas), ("s", tiles), ("v", data)], [wide], pair_scratch, cost=2 * 10**9
        )
        return partial

    below, above = neighbours(low, high)
    short = own_call(data)
    data, move, low, high = call(
        halo_step_kernel,
        [
            ("s", lambdas), ("v", data), ("v", below), ("v", above), ("v", short), ("v", far), ("v", move),
        ],
        [wide, moving, border, border],
        [turns, spare],
    )
    below, above = neighbours(low, high)
    short = own_call(data)
    (state,) = call(
        halo_last_kernel,
        [
            ("s", lambdas), ("v", data), ("v", below), ("v", above), ("v", short), ("v", far), ("v", move),
        ],
        [((10, 1, A_DEV), F32)],
        [turns, spare],
    )
    (state,) = call(
        first_trade_kernel, [("v", state), ("v", traded(state, 0)), ("v", move)], [((10, 1, A_DEV), F32)]
    )
    out = call(
        last_trade_kernel,
        [("v", state), ("v", traded(state, 1))],
        [(triple, jnp.int32), (triple, F32), (triple, F32)],
    )
    return tuple(by_row(x) for x in out)


def solution(mesh):
    in_specs = (
        P("lam", None, "dom"),
        P("lam", None, "dom"),
        P("lam", None, "dom"),
        P("dom"),
        P("dom"),
        P("dom"),
        P("lam"),
        P("lam", "dom", None),
        P("lam", "dom", None),
        P(None, "lam"),
    )
    out_specs = (P("lam", None, "dom"), P("lam", None, "dom"), P("lam", None, "dom"))
    return jax.shard_map(body, mesh=mesh, in_specs=in_specs, out_specs=out_specs, check_vma=False)
```

```python
import functools
import math

import jax
import jax.numpy as jnp
import ml_dtypes
import numpy as np
from jax import lax
from jax.experimental import pallas as pl
from jax.experimental.pallas import tpu as pltpu
from jax.sharding import PartitionSpec as P

K = 128
CLUSTER = 128
N_DOM = 16
A_DEV = 1024
CLUSTERS = 8
HALO = 512
MODES = 32
SLAB = 24
ROWS = N_DOM * SLAB

EWALD_BETA = 0.5
COULOMB = 20.0
LJ_DEPTH = 1.0
LJ_SIGMA_SQ = 0.49
SOFT_SCALE = 0.5
SOFT_FLOOR = 0.5
STEP_DT = 0.25

F32 = jnp.float32
BF16 = jnp.bfloat16
HIGHEST = lax.Precision.HIGHEST

TURN = 2.0**32
SPAN_SQ = 2.0**-50
SPAN = 2.0**-25

SCREEN = (
    -0.0818439527,
    0.648023047,
    -2.23331568,
    4.38709699,
    -5.37737017,
    4.16223694,
    -1.81397109,
    0.0540053844,
    0.5630337,
    -5.2346482e-05,
    0.282096019,
)


def real_basis(count):
    half = count // 2
    place = np.arange(count)
    rows = []
    for k in range(half + 1):
        scale = math.sqrt((1.0 if k in (0, half) else 2.0) / count)
        rows.append(scale * np.cos(2.0 * np.pi * (k * place % count) / count))
    for k in range(1, half):
        rows.append(math.sqrt(2.0 / count) * np.sin(2.0 * np.pi * (k * place % count) / count))
    return np.stack(rows)


def halves(table):
    high = table.astype(np.float32).astype(ml_dtypes.bfloat16)
    low = (table - high.astype(np.float64)).astype(np.float32).astype(ml_dtypes.bfloat16)
    return high, low


def basis_table():
    basis = real_basis(K)
    high, low = halves(basis)
    return np.concatenate([high, low, high.T, low.T], axis=0)


def slab_basis():
    basis = real_basis(MODES)
    order = [0, MODES // 2]
    for k in range(1, MODES // 2):
        order += [k, MODES // 2 + k]
    return basis[np.array(order)].astype(np.float32)


def spline_modulus(k):
    return (3.0 / (2.0 + np.cos(2.0 * np.pi * k / K))) ** 2


def slab_weights():
    k = np.arange(K // 2 + 1)
    delta = np.arange(-MODES // 2 + 1, MODES // 2 + 1)
    folded = np.where((k == 0) | (k == K // 2), 1.0, 2.0)
    own = folded * np.exp(-np.pi**2 * (k / K) ** 2 / EWALD_BETA**2) * spline_modulus(k)
    rows = []
    for j in range(MODES // 2 + 1):
        window = np.cos(2 * np.pi * k[:, None] * delta / K) * np.cos(2 * np.pi * j * delta / MODES)
        rows.append(own * window.sum(axis=1))
    return np.stack(rows).astype(np.float32)


def plane_gain():
    k = np.concatenate([np.arange(K // 2 + 1), np.arange(1, K // 2)])
    square = (k / K) ** 2
    factor = np.exp(-np.pi**2 * square / EWALD_BETA**2) * spline_modulus(k)
    return square.astype(np.float32), factor.astype(np.float32)


def split(x):
    high = x.astype(BF16)
    return high, (x - high.astype(F32)).astype(BF16)


def dot3(left, right, dims=(((1,), (0,)), ((), ()))):
    lh, ll = left
    rh, rl = right
    dot = functools.partial(lax.dot_general, dimension_numbers=dims, preferred_element_type=F32)
    return dot(lh, rh) + (dot(lh, rl) + dot(ll, rh))


def spline_set(u):
    v = 1.0 - u
    u2 = u * u
    u3 = u2 * u
    weights = (
        v * v * v / 6.0,
        (3.0 * u3 - 6.0 * u2 + 4.0) / 6.0,
        (-3.0 * u3 + 3.0 * u2 + 3.0 * u + 1.0) / 6.0,
        u3 / 6.0,
    )
    slopes = (-0.5 * v * v, 1.5 * u2 - 2.0 * u, -1.5 * u2 + u + 0.5, 0.5 * u2)
    return weights, slopes


def chosen(distance, rows):
    out = jnp.where(distance == 3, rows[3], 0.0)
    for k in (2, 1, 0):
        out = jnp.where(distance == k, rows[k], out)
    return out


def iota_rows(rows, columns):
    return lax.broadcasted_iota(jnp.int32, (rows, columns), 0)


def fixed_turns(x):
    t = x * (1.0 / K)
    f = t - jnp.floor(t + 0.5)
    return jnp.maximum(f, -0.5) * TURN


def pair_terms(own, other, floor_value):
    ax, ay, az, qa, wa = own
    bx, by, bz, qb, wb = other
    dx = (ax - bx).astype(F32)
    dy = (ay - by).astype(F32)
    dz = (az - bz).astype(F32)
    s = (dx * dx + dy * dy + dz * dz) * SPAN_SQ + floor_value
    w = lax.rsqrt(s)
    u = w * w
    screen = jnp.full_like(w, SCREEN[0])
    for c in SCREEN[1:]:
        screen = screen * w + c
    gauss = jnp.exp2(s * (-(EWALD_BETA**2) * math.log2(math.e)))
    t = u * u * u
    g = u * ((qa * qb) * (gauss * screen) + (wa * wb) * (t * (t - 0.5 / LJ_SIGMA_SQ**3)))
    return g * dx, g * dy, g * dz


def own_rows(data_ref, turns, start, rows=8):
    def spread(row):
        return jnp.broadcast_to(row, (rows, CLUSTER))

    columns = pl.ds(start, CLUSTER)
    xyz = [spread(turns[i : i + 1, columns].astype(jnp.int32)) for i in range(3)]
    q = spread(data_ref[3:4, columns] * (2.0 * COULOMB))
    w = spread(data_ref[4:5, columns] * (48.0 * LJ_DEPTH * LJ_SIGMA_SQ**6))
    return (*xyz, q, w)


def write_halo(data, lists, low_ref, high_ref):
    lane = lax.broadcasted_iota(jnp.int32, (8, CLUSTER), 1)
    for row, out_ref in ((0, low_ref), (1, high_ref)):
        for k in range(HALO // CLUSTER):
            columns = slice(k * CLUSTER, (k + 1) * CLUSTER)
            start = row * HALO + k * CLUSTER
            index = jnp.broadcast_to(lists[:, start : start + CLUSTER].astype(jnp.int32), (8, CLUSTER))
            first = data[:, 2 * k * CLUSTER : (2 * k + 1) * CLUSTER]
            second = data[:, (2 * k + 1) * CLUSTER : (2 * k + 2) * CLUSTER]
            out_ref[:, columns] = jnp.where(
                lane < CLUSTER // 2,
                jnp.take_along_axis(first, index, axis=1, mode="promise_in_bounds"),
                jnp.take_along_axis(second, index, axis=1, mode="promise_in_bounds"),
            )


def state_kernel(
    lam_ref, cells_ref, off_ref, vel_ref, charge_ref, coup_ref, mass_ref, lists_ref, flag_ref, grid_ref,
    data_ref, move_ref, low_ref, high_ref,
):
    del grid_ref
    weight = 1.0 - lam_ref[0] * coup_ref[...]
    for i in range(3):
        cell = cells_ref[i].astype(F32)
        move_ref[i : i + 1, :] = off_ref[i]
        move_ref[3 + i : 4 + i, :] = cell
        move_ref[8 + i : 9 + i, :] = vel_ref[i]
        data_ref[i : i + 1, :] = cell + off_ref[i]
    move_ref[6:7, :] = jnp.broadcast_to(flag_ref[0:1, 0:1].astype(F32), (1, A_DEV))
    move_ref[7:8, :] = jnp.broadcast_to(flag_ref[0:1, 1:2].astype(F32), (1, A_DEV))
    move_ref[11:12, 0:HALO] = (lists_ref[0, 0:1, :] & (CLUSTER - 1)).astype(F32)
    move_ref[11:12, HALO : 2 * HALO] = (lists_ref[0, 1:2, :] & (CLUSTER - 1)).astype(F32)
    move_ref[12:16, :] = jnp.zeros((4, A_DEV), F32)
    data_ref[3:4, :] = charge_ref[...] * weight
    data_ref[4:5, :] = weight
    data_ref[5:6, :] = mass_ref[...]
    data_ref[6:8, :] = jnp.zeros((2, A_DEV), F32)
    write_halo(data_ref[...], move_ref[11:12, :], low_ref, high_ref)


def spread_kernel(
    lam_ref, cells_hbm, off_hbm, charge_hbm, coup_hbm, slab_hbm,
    out_ref, mixed_high, mixed_low, cells_ref, off_ref, charge_ref, coup_ref, slab_ref, rows_ref, arrived,
):
    copies = [
        pltpu.make_async_copy(source, target, arrived.at[i])
        for i, (source, target) in enumerate(
            (
                (cells_hbm, cells_ref), (off_hbm, off_ref), (charge_hbm, charge_ref), (coup_hbm, coup_ref),
                (slab_hbm, slab_ref),
            )
        )
    ]
    for copy in copies:
        copy.start()
    for copy in copies:
        copy.wait()
    charge = charge_ref[...] * (1.0 - lam_ref[0] * coup_ref[...])
    for i in range(3):
        rows_ref[i : i + 1, :] = off_ref[i]
    off = rows_ref[0:3, :]
    cells = [cells_ref[i] for i in range(3)]
    weights, _ = spline_set(off)
    row = iota_rows(16, A_DEV)
    plane = jnp.where(row < 8, row, 8 + (row & 3))
    x_table = chosen(plane - (cells[0] & 7), [m[0:1] for m in weights]) * charge
    z_table = chosen((iota_rows(MODES, A_DEV) - cells[2]) & (MODES - 1), [m[2:3] for m in weights])
    z_modes = jnp.dot(slab_ref[...], z_table, precision=HIGHEST, preferred_element_type=F32)
    y_table = chosen((iota_rows(K, A_DEV) - cells[1]) & (K - 1), [m[1:2] for m in weights])

    near, far = x_table[0:8], x_table[8:16]
    upper = iota_rows(8, A_DEV) < 4
    for i in range(0, N_DOM, 2):
        pieces = []
        for k in (i, i + 1):
            first = jnp.broadcast_to(z_modes[2 * k : 2 * k + 1], (8, A_DEV))
            second = jnp.broadcast_to(z_modes[2 * k + 1 : 2 * k + 2], (8, A_DEV))
            pieces += [near * first, near * second, far * jnp.where(upper, first, second)]
        high, low = split(jnp.concatenate(pieces, axis=0))
        mixed_high[i * SLAB : (i + 2) * SLAB, :] = high
        mixed_low[i * SLAB : (i + 2) * SLAB, :] = low
    out_ref[...] = dot3((mixed_high[...], mixed_low[...]), split(y_table), (((1,), (1,)), ((), ())))


def mesh_kernel(grid_ref, gain_ref, basis_ref, below_ref, above_ref, out_ref, block):
    del below_ref, above_ref
    top = iota_rows(8, K) < 4
    for e in range(N_DOM):
        spill = grid_ref[((e - 1) % N_DOM) * SLAB + 16 : ((e - 1) % N_DOM) * SLAB + 24, :]
        turned = pltpu.roll(spill, 4, 0)
        block[8 * e : 8 * e + 8, :] = grid_ref[e * SLAB : e * SLAB + 8, :] + jnp.where(top, spill, 0.0)
        block[K + 8 * e : K + 8 * e + 8, :] = grid_ref[e * SLAB + 8 : e * SLAB + 16, :] + jnp.where(top, turned, 0.0)
    basis = (basis_ref[0:K, :], basis_ref[K : 2 * K, :])
    turned_basis = (basis_ref[2 * K : 3 * K, :], basis_ref[3 * K : 4 * K, :])
    along_y = dot3(split(block[...]), turned_basis)
    for mode in range(2):
        part = split(along_y[mode * K : (mode + 1) * K])
        scaled = dot3(basis, part) * gain_ref[mode]
        block[mode * K : (mode + 1) * K, :] = dot3(turned_basis, split(scaled))
    block[...] = dot3(split(block[...]), basis)
    for e in range(N_DOM):
        following = 8 * ((e + 1) % N_DOM)
        out_ref[e * SLAB : e * SLAB + 8, :] = block[8 * e : 8 * e + 8, :]
        out_ref[e * SLAB + 8 : e * SLAB + 16, :] = block[K + 8 * e : K + 8 * e + 8, :]
        out_ref[e * SLAB + 16 : e * SLAB + 24, :] = jnp.where(
            top,
            block[following : following + 8, :],
            pltpu.roll(block[K + following : K + following + 8, :], 4, 0),
        )


def write_gain(mode_weights_ref, rows_ref, lanes_ref, gain_ref):
    dom = lax.axis_index("dom")
    square_y, factor_y = lanes_ref[0:1, :], lanes_ref[1:2, :]
    scale = COULOMB / (math.pi * K)
    first = dom
    second = jnp.where(dom == 0, MODES // 2, dom)

    def totals(square):
        one = jnp.zeros_like(square)
        two = jnp.zeros_like(square)
        for k in range(K // 2 + 1):
            whole = square + (k / K) ** 2
            inverse = 1.0 / whole if k else jnp.where(whole > 0.0, 1.0 / jnp.where(whole > 0.0, whole, 1.0), 0.0)
            one = one + inverse * mode_weights_ref[first, k]
            two = two + inverse * mode_weights_ref[second, k]
        return one, two

    def block(start):
        rows = pl.ds(start, 8)
        square = jnp.broadcast_to(rows_ref[rows, 0:1], (8, K)) + square_y
        factor = jnp.broadcast_to(rows_ref[rows, 1:2], (8, K)) * factor_y * scale
        one, two = totals(square)
        return one * factor, two * factor

    def step(b, carry):
        start = pl.multiple_of(b * 8, 8)
        one, two = block(start)
        gain_ref[0, pl.ds(start, 8), :] = one
        gain_ref[1, pl.ds(start, 8), :] = two
        gain_ref[0, pl.ds(start + K // 2, 8), :] = one
        gain_ref[1, pl.ds(start + K // 2, 8), :] = two
        return carry

    lax.fori_loop(0, 8, step, 0)
    one, two = block(K // 2)
    gain_ref[0, K // 2 : K // 2 + 1, :] = one[0:1]
    gain_ref[1, K // 2 : K // 2 + 1, :] = two[0:1]


def listed(tiles_ref, row, cluster):
    count = jnp.int32(0)
    for slot in range(1, 4):
        count = count + jnp.where(tiles_ref[slot, 0, row] == cluster, 1, 0)
    return count.astype(F32)


def own_forces(lam_ref, tiles_ref, data_ref, force_ref, turns, near, sides, columns, places, factors, first, last):
    turns[...] = fixed_turns(data_ref[0:3, :])
    near[...] = jnp.zeros_like(near)
    floor_value = SOFT_FLOOR + SOFT_SCALE * lam_ref[0]
    for b in range(first, last):
        lanes = slice(b * CLUSTER, (b + 1) * CLUSTER)
        columns[lanes, :] = jnp.concatenate([turns[:, lanes], data_ref[3:8, lanes]], axis=0).T

    def one_cluster(b, side):
        start = pl.multiple_of(b * CLUSTER, CLUSTER)
        for j in range(3):
            a = b if j == 0 else (b + j) % CLUSTERS
            own = own_rows(data_ref, turns, pl.multiple_of(a * CLUSTER, CLUSTER))
            total = [jnp.zeros((8, CLUSTER), F32) for _ in range(3)]
            back = listed(tiles_ref, b, a) if j else None
            for chunk in range(CLUSTER // 8):
                here = slice(chunk * 8, chunk * 8 + 8)
                rows = pl.ds(pl.multiple_of(start + chunk * 8, 8), 8)
                if j == 0:
                    part = columns[rows, :]
                    other = [jnp.broadcast_to(part[:, i : i + 1], (8, CLUSTER)) for i in range(5)]
                    other[:3] = [x.astype(jnp.int32) for x in other[:3]]
                    for i in range(3):
                        places[3 * side + i, here, :] = other[i]
                    for i in range(2):
                        factors[2 * side + i, here, :] = other[3 + i]
                else:
                    other = [places[3 * side + i, here, :] for i in range(3)]
                    other += [factors[2 * side + i, here, :] for i in range(2)]
                terms = pair_terms(own, other, floor_value)
                total = [p + q for p, q in zip(total, terms)]
                if j:
                    for i in range(3):
                        sides[3 * j - 3 + i, rows, :] = back * terms[i]
            rows = pl.ds(pl.multiple_of(a * 8, 8), 8)
            for i in range(3):
                near[i, rows, :] = near[i, rows, :] + (listed(tiles_ref, a, b) * total[i] if j else total[i])

    def four_clusters(k, carry):
        for side in range(4):
            one_cluster(4 * k + side, side)
        return carry

    lax.fori_loop(first // 4, last // 4, four_clusters, 0)
    force_ref[...] = jnp.zeros_like(force_ref)
    ones = jnp.ones((8, CLUSTER), BF16)
    for c in range(CLUSTERS):
        lanes = slice(c * CLUSTER, (c + 1) * CLUSTER)
        for i in range(3):
            force_ref[i : i + 1, lanes] = SPAN * jnp.sum(near[i, c * 8 : (c + 1) * 8, :], axis=0, keepdims=True)
    rows = slice(first * CLUSTER, last * CLUSTER)
    for i in range(3):
        total = jnp.zeros((8, (last - first) * CLUSTER), F32)
        for part in split(sides[i, rows, :] + sides[3 + i, rows, :]):
            total = total + lax.dot_general(ones, part, (((1,), (1,)), ((), ())), preferred_element_type=F32)
        force_ref[i : i + 1, rows] = force_ref[i : i + 1, rows] - SPAN * total[0:1]


def own_kernel(lam_ref, tiles_ref, data_ref, force_ref, turns, near, sides, *kept):
    own_forces(lam_ref, tiles_ref, data_ref, force_ref, turns, near, sides, *kept, 0, CLUSTERS)


def gain_kernel(
    lam_ref, tiles_ref, weights_ref, data_ref, rows_ref, lanes_ref, force_ref, gain_ref, turns, near, sides, *kept
):
    write_gain(weights_ref, rows_ref, lanes_ref, gain_ref)
    own_forces(lam_ref, tiles_ref, data_ref, force_ref, turns, near, sides, *kept, 0, CLUSTERS // 2)


def add_halo_forces(lam_ref, data_ref, below_ref, above_ref, partial_ref, force_ref, turns):
    turns[...] = fixed_turns(data_ref[0:3, :])
    floor_value = SOFT_FLOOR + SOFT_SCALE * lam_ref[0]

    def one_pair(k):
        start = pl.multiple_of(k * CLUSTER, CLUSTER)
        starts = [pl.multiple_of(k * (2 * CLUSTER), CLUSTER), pl.multiple_of(k * (2 * CLUSTER) + CLUSTER, CLUSTER)]
        owns = [own_rows(data_ref, turns, s) for s in starts]
        totals = [[jnp.zeros((8, CLUSTER), F32) for _ in range(3)] for _ in range(2)]
        for source in (below_ref, above_ref):
            block = source[:, pl.ds(start, CLUSTER)]
            stack = jnp.where(iota_rows(8, CLUSTER) < 3, fixed_turns(block), block)
            turned = stack.T
            for chunk in range(CLUSTER // 8):
                part = turned[chunk * 8 : chunk * 8 + 8]
                other = [jnp.broadcast_to(part[:, i : i + 1], (8, CLUSTER)) for i in range(5)]
                other[:3] = [x.astype(jnp.int32) for x in other[:3]]
                for j in range(2):
                    terms = pair_terms(owns[j], other, floor_value)
                    totals[j] = [a + b for a, b in zip(totals[j], terms)]
        for j in range(2):
            lanes = pl.ds(starts[j], CLUSTER)
            for i in range(3):
                force_ref[i : i + 1, lanes] = partial_ref[i : i + 1, lanes] + SPAN * jnp.sum(
                    totals[j][i], axis=0, keepdims=True
                )

    for k in range(HALO // CLUSTER):
        one_pair(k)


def rest_kernel(
    lam_ref, tiles_ref, data_ref, below_ref, above_ref, partial_ref, move_ref, slab_ref,
    force_ref, y_high, y_low, z_ref, x_ref, second, turns, near, sides, *kept
):
    write_tables(move_ref, slab_ref, y_high, y_low, z_ref, x_ref)
    own_forces(lam_ref, tiles_ref, data_ref, second, turns, near, sides, *kept, CLUSTERS // 2, CLUSTERS)
    second[...] = second[...] + partial_ref[...]
    force_ref[...] = jnp.zeros_like(force_ref)
    add_halo_forces(lam_ref, data_ref, below_ref, above_ref, second, force_ref, turns)


def advance(force, kicks, data_ref, move_ref, data_out, move_out, low_ref, high_ref):
    mass = data_ref[5:6, :]
    velocity = move_ref[8:11, :]
    for _ in range(kicks):
        velocity = velocity + 0.5 * STEP_DT * force * mass
    off = move_ref[0:3, :] + STEP_DT * velocity
    move_out[...] = move_ref[...]
    move_out[0:3, :] = off
    move_out[8:11, :] = velocity
    data_out[...] = data_ref[...]
    data_out[0:3, :] = move_ref[3:6, :] + off
    write_halo(data_out[...], move_ref[11:12, :], low_ref, high_ref)


def write_tables(move_ref, slab_ref, y_high, y_low, z_ref, x_ref):
    off = move_ref[0:3, :]
    cells = move_ref[3:6, :].astype(jnp.int32)
    weights, slopes = spline_set(off)
    row = iota_rows(16, A_DEV)
    reach = jnp.where(row < 8, row, 8 + (row & 3)) - (cells[0:1] & 7)
    x_ref[0:16, :] = chosen(reach, [m[0:1] for m in weights])
    x_ref[16:32, :] = chosen(reach, [m[0:1] for m in slopes])
    reach = (iota_rows(MODES, A_DEV) - cells[2:3]) & (MODES - 1)
    for i, rows in enumerate((weights, slopes)):
        table = chosen(reach, [m[2:3] for m in rows])
        z_ref[i * MODES : (i + 1) * MODES, :] = jnp.dot(
            slab_ref[...], table, precision=HIGHEST, preferred_element_type=F32
        )
    for c in range(CLUSTERS):
        lanes = slice(c * CLUSTER, (c + 1) * CLUSTER)
        reach = (iota_rows(K, CLUSTER) - cells[1:2, lanes]) & (K - 1)
        for i, rows in enumerate((weights, slopes)):
            target = slice((2 * c + i) * CLUSTER, (2 * c + i + 1) * CLUSTER)
            y_high[:, target], y_low[:, target] = split(chosen(reach, [m[1:2, lanes] for m in rows]))


def gather_kernel(
    pot_ref, data_ref, move_ref, short_ref, y_high, y_low, z_ref, x_ref,
    long_ref, data_out, move_out, low_ref, high_ref, force,
):
    charge = data_ref[3:4, :]
    potential = split(pot_ref[...])
    upper = iota_rows(8, CLUSTER) < 4
    for c in range(CLUSTERS):
        lanes = slice(c * CLUSTER, (c + 1) * CLUSTER)
        both = slice(2 * c * CLUSTER, (2 * c + 2) * CLUSTER)
        along = dot3(potential, (y_high[:, both], y_low[:, both]))
        value, tilt = along[:, :CLUSTER], along[:, CLUSTER:]
        sums = [[jnp.zeros((8, CLUSTER), F32) for _ in range(2)] for _ in range(3)]
        for i in range(N_DOM):
            pairs = []
            for k in (2 * i, MODES + 2 * i):
                first = jnp.broadcast_to(z_ref[k : k + 1, lanes], (8, CLUSTER))
                second = jnp.broadcast_to(z_ref[k + 1 : k + 2, lanes], (8, CLUSTER))
                pairs.append((first, second, jnp.where(upper, first, second)))
            for which, (source, table) in enumerate(((value, 0), (tilt, 0), (value, 1))):
                block = source[i * SLAB : (i + 1) * SLAB]
                first, second, mixed = pairs[table]
                sums[which][0] = sums[which][0] + (first * block[0:8] + second * block[8:16])
                sums[which][1] = sums[which][1] + mixed * block[16:24]
        for i in range(3):
            k = 16 if i == 0 else 0
            near = x_ref[k : k + 8, lanes] * sums[i][0] + x_ref[k + 8 : k + 16, lanes] * sums[i][1]
            force[i : i + 1, lanes] = -charge[:, lanes] * jnp.sum(near, axis=0, keepdims=True)
    long_ref[...] = jnp.zeros_like(long_ref)
    long_ref[0:3, :] = force[0:3, :]
    advance(
        short_ref[0:3, :] + force[0:3, :], 1, data_ref, move_ref, data_out, move_out, low_ref, high_ref
    )


def halo_step_kernel(
    lam_ref, data_ref, below_ref, above_ref, partial_ref, long_ref, move_ref,
    data_out, move_out, low_ref, high_ref, turns, force,
):
    add_halo_forces(lam_ref, data_ref, below_ref, above_ref, partial_ref, force, turns)
    total = force[0:3, :] + long_ref[0:3, :]
    advance(total, 2, data_ref, move_ref, data_out, move_out, low_ref, high_ref)


def halo_last_kernel(
    lam_ref, data_ref, below_ref, above_ref, partial_ref, long_ref, move_ref, state_ref, turns, force
):
    add_halo_forces(lam_ref, data_ref, below_ref, above_ref, partial_ref, force, turns)
    total = force[0:3, :] + long_ref[0:3, :]
    velocity = move_ref[8:11, :] + 0.5 * STEP_DT * total * data_ref[5:6, :]
    for i in range(3):
        state_ref[i] = move_ref[i : i + 1, :]
        state_ref[3 + i] = velocity[i : i + 1]
        state_ref[6 + i] = move_ref[3 + i : 4 + i, :]
    state_ref[9] = move_ref[6:7, :]


def takes(round_index, here_ref, there_ref):
    window = lax.axis_index("lam")
    lower = window % 2 == round_index % 2
    inside = window + 1 < lax.axis_size("lam")
    return jnp.where(lower, jnp.where(inside, here_ref[9], 0.0), there_ref[9]) == 1.0


def first_trade_kernel(here_ref, there_ref, move_ref, out_ref):
    take = takes(0, here_ref, there_ref)
    for i in range(9):
        out_ref[i] = jnp.where(take, there_ref[i], here_ref[i])
    out_ref[9] = move_ref[7:8, :]


def last_trade_kernel(here_ref, there_ref, cells_ref, off_ref, vel_ref):
    take = takes(1, here_ref, there_ref)
    for i in range(3):
        off_ref[i] = jnp.where(take, there_ref[i], here_ref[i])
        vel_ref[i] = jnp.where(take, there_ref[3 + i], here_ref[3 + i])
        cells_ref[i] = jnp.where(take, there_ref[6 + i], here_ref[6 + i]).astype(jnp.int32)


PLACES = {
    "s": pl.BlockSpec(memory_space=pltpu.SMEM),
    "v": pl.BlockSpec(memory_space=pltpu.VMEM),
    "a": pl.BlockSpec(memory_space=pl.ANY),
}


def call(kernel, ins, outs, scratch=(), cost=0, limit=40):
    return pl.pallas_call(
        kernel,
        out_shape=[jax.ShapeDtypeStruct(shape, dtype) for shape, dtype in outs],
        in_specs=[PLACES[place] for place, _ in ins],
        out_specs=[PLACES["v"]] * len(outs),
        scratch_shapes=list(scratch),
        compiler_params=pltpu.CompilerParams(vmem_limit_bytes=limit * 2**20),
        cost_estimate=pl.CostEstimate(flops=cost, bytes_accessed=200000, transcendentals=0),
    )(*[value for _, value in ins])


def neighbours(low, high):
    size = lax.axis_size("dom")
    below = lax.ppermute(high, "dom", [(i, (i + 1) % size) for i in range(size)])
    above = lax.ppermute(low, "dom", [(i, (i - 1) % size) for i in range(size)])
    return below, above


def traded(state, round_index):
    pairs = []
    for w in range(round_index % 2, lax.axis_size("lam") - 1, 2):
        pairs += [(w, w + 1), (w + 1, w)]
    return lax.ppermute(state, "lam", pairs)


def exchanged(value):
    return lax.all_to_all(value, "dom", split_axis=0, concat_axis=0, tiled=True)


def body(
    cells, offsets, velocities, charges, coupling, inverse_mass, lambdas, tile_lists, halo_lists, accept_flags
):
    wide = ((8, A_DEV), F32)
    moving = ((16, A_DEV), F32)
    border = ((8, HALO), F32)
    turns = pltpu.VMEM((3, A_DEV), F32)
    pair_scratch = [
        turns, pltpu.VMEM((3, CLUSTERS * 8, CLUSTER), F32), pltpu.VMEM((6, A_DEV, CLUSTER), F32),
        pltpu.VMEM((A_DEV, 8), F32), pltpu.VMEM((12, CLUSTER, CLUSTER), jnp.int32), pltpu.VMEM((8, CLUSTER, CLUSTER), F32),
    ]
    spare = pltpu.VMEM((8, A_DEV), F32)
    tiles = jnp.transpose(tile_lists, (2, 0, 1))
    slab = jnp.asarray(slab_basis())
    square, factor = plane_gain()
    gain_rows = np.zeros((K, 8), np.float32)
    gain_rows[:, 0], gain_rows[:, 1] = square, factor
    gain_lanes = np.zeros((8, K), np.float32)
    gain_lanes[0], gain_lanes[1] = square, factor

    triple = (3, 1, A_DEV)

    def by_row(x):
        return jnp.transpose(x, (1, 0, 2))


    rows = [by_row(x) for x in (cells, offsets, velocities)]
    whole, some = (3, 1, A_DEV), (1, A_DEV)
    (grid,) = call(
        spread_kernel,
        [
            ("s", lambdas), ("a", rows[0]), ("a", rows[1]), ("a", charges[None]), ("a", coupling[None]), ("a", slab),
        ],
        [((ROWS, K), F32)],
        [
            pltpu.VMEM((ROWS, A_DEV), BF16), pltpu.VMEM((ROWS, A_DEV), BF16), pltpu.VMEM(whole, jnp.int32),
            pltpu.VMEM(whole, F32), pltpu.VMEM(some, F32), pltpu.VMEM(some, F32), pltpu.VMEM((MODES, MODES), F32),
            pltpu.VMEM((8, A_DEV), F32), pltpu.SemaphoreType.DMA((5,)),
        ],
        limit=60,
    )
    data, move, low, high = call(
        state_kernel,
        [
            ("s", lambdas), *(("v", x) for x in rows), ("v", charges[None]), ("v", coupling[None]),
            ("v", inverse_mass[None]), ("v", halo_lists), ("v", accept_flags.T), ("a", grid),
        ],
        [wide, moving, border, border],
    )
    grid = exchanged(grid)
    below, above = neighbours(low, high)
    short, gain = call(
        gain_kernel,
        [
            ("s", lambdas), ("s", tiles), ("s", jnp.asarray(slab_weights())), ("v", data),
            ("v", jnp.asarray(gain_rows)), ("v", jnp.asarray(gain_lanes)),
        ],
        [wide, ((2, K, K), F32)],
        pair_scratch,
        cost=2 * 10**9,
    )
    (potential,) = call(
        mesh_kernel,
        [("v", grid), ("v", gain), ("v", jnp.asarray(basis_table())), ("a", below), ("a", above)],
        [((ROWS, K), F32)],
        [pltpu.VMEM((2 * K, K), F32)],
    )
    potential = exchanged(potential)
    short, *tables = call(
        rest_kernel,
        [
            ("s", lambdas), ("s", tiles), ("v", data), ("v", below), ("v", above), ("v", short), ("v", move), ("v", slab),
        ],
        [wide, *[((K, 2 * A_DEV), BF16)] * 2, ((2 * MODES, A_DEV), F32), ((32, A_DEV), F32)],
        [spare, *pair_scratch],
        cost=2 * 10**9,
    )
    far, data, move, low, high = call(
        gather_kernel,
        [("v", potential), ("v", data), ("v", move), ("v", short), *(("v", x) for x in tables)],
        [wide, wide, moving, border, border],
        [spare],
    )

    def own_call(data):
        (partial,) = call(
            own_kernel, [("s", lambdas), ("s", tiles), ("v", data)], [wide], pair_scratch, cost=2 * 10**9
        )
        return partial

    below, above = neighbours(low, high)
    short = own_call(data)
    data, move, low, high = call(
        halo_step_kernel,
        [
            ("s", lambdas), ("v", data), ("v", below), ("v", above), ("v", short), ("v", far), ("v", move),
        ],
        [wide, moving, border, border],
        [turns, spare],
    )
    below, above = neighbours(low, high)
    short = own_call(data)
    (state,) = call(
        halo_last_kernel,
        [
            ("s", lambdas), ("v", data), ("v", below), ("v", above), ("v", short), ("v", far), ("v", move),
        ],
        [((10, 1, A_DEV), F32)],
        [turns, spare],
    )
    (state,) = call(
        first_trade_kernel, [("v", state), ("v", traded(state, 0)), ("v", move)], [((10, 1, A_DEV), F32)]
    )
    out = call(
        last_trade_kernel,
        [("v", state), ("v", traded(state, 1))],
        [(triple, jnp.int32), (triple, F32), (triple, F32)],
    )
    return tuple(by_row(x) for x in out)


def solution(mesh):
    in_specs = (
        P("lam", None, "dom"),
        P("lam", None, "dom"),
        P("lam", None, "dom"),
        P("dom"),
        P("dom"),
        P("dom"),
        P("lam"),
        P("lam", "dom", None),
        P("lam", "dom", None),
        P(None, "lam"),
    )
    out_specs = (P("lam", None, "dom"), P("lam", None, "dom"), P("lam", None, "dom"))
    return jax.shard_map(body, mesh=mesh, in_specs=in_specs, out_specs=out_specs, check_vma=False)
```
